32 devices in a mesh: job: 4 (over y, core), seq: 8 (over z, x).
Axes of the slice: x: 2, y: 2, z: 4, core: 2. Of those that a mesh axis runs over, the one named last changes fastest.
Arguments:
- video: bfloat16 [4, 1024, 3072], P('job', 'seq'), may hold values from -6 to 6
- text_cache: bfloat16 [4, 256, 4096], P('job', 'seq'), may hold values from -6 to 6
- text_count: int32 [4], replicated, may hold values from 129 to 256, as said below
- holder: int32 [4], replicated, may hold values from 0 to 3, each once
- text_splits: int32 [4, 8], replicated, may hold values from 0 to 64, as said below
- mod_shift: float32 [4, 3072], replicated, may hold values from -3 to 3
- mod_scale: float32 [4, 3072], replicated, may hold values from -2 to 2
- mod_gate: float32 [4, 3072], replicated, may hold values from -4 to 4
- text_gain: float32 [4096], replicated, may hold values from 0.25 to 1.75
- refine_w: bfloat16 [4096, 3072], P(None, 'job'), may hold values from -0.09375 to 0.09375
- refine_bias: float32 [3072], P('job'), may hold values from -3 to 3
- w_qkv: bfloat16 [3072, 16, 3, 128], P(None, 'job'), may hold values from -0.109375 to 0.109375
- q_gain: float32 [16, 128], P('job'), may hold values from 0.85 to 9.2
- k_gain: float32 [16, 128], P('job'), may hold values from 0.85 to 9.2
- w_out: bfloat16 [16, 128, 3072], P('job'), may hold values from -0.125 to 0.125
Outputs:
- video_out: bfloat16 [4, 1024, 3072], P('job', 'seq')
- text_out: bfloat16 [4, 512, 3072], P('job', 'seq')
The draws below stay inside these ranges and needn't reach their ends.
Inputs may be any that keep to these rules, and one draw needn't show every extreme that they name: `text_count`: 256 is reached by some job in every draw. `text_splits`: for each job the entries over the 8 shards add up to text_count of that job; some shard holds exactly 64 rows in every draw.
All inputs are finite; a program needn't handle non-finite values.
Results may differ from the reference program's by a relative error of at most 0.012.
The reference program's roundings to bfloat16 on the way count: a program that leaves them out, or rounds other values in their place, can miss the bound.
Values may be sent and summed in bfloat16 or wider, within the bound.
No kernel may reach another device: no remote copies, remote signals or barrier semaphores. Data moves between devices by JAX's collectives and lax.ppermute only.
A program may use at most 64 MiB of HBM per device.

```python
import math
import jax
import jax.numpy as jnp
from jax import lax

D = 3072
DT = 4096
HD = 128
HEADS = 16
TXT = 256
VID_DEV = 128
JOBS = 4
SHARDS = 8
VIDEO = 1024
TCAP = 64
N_JOB = 4
N_SEQ = 8


def text_plan(key):
    base_key = jax.random.fold_in(key, 7)
    key_count, key_long, key_caps, key_lead = jax.random.split(base_key, 4)
    counts = jax.random.randint(key_count, (JOBS,), TXT // 2 + 1, TXT + 1)
    longest = jax.random.randint(key_long, (), 0, JOBS)
    counts = jnp.where(jnp.arange(JOBS) == longest, TXT, counts)
    capacity = jax.random.randint(key_caps, (JOBS, SHARDS), TCAP // 2, TCAP + 1)
    leading = jax.random.randint(key_lead, (JOBS,), 0, SHARDS)
    fill_order = (jnp.arange(SHARDS)[None, :] + leading[:, None]) % SHARDS
    ordered = jnp.take_along_axis(capacity, fill_order, axis=1)
    ordered = ordered.at[:, 0].set(TCAP)
    before = jnp.cumsum(ordered, axis=1) - ordered
    filled = jnp.clip(counts[:, None] - before, 0, ordered)
    position = (jnp.arange(SHARDS)[None, :] - leading[:, None]) % SHARDS
    splits = jnp.take_along_axis(filled, position, axis=1)
    return (counts.astype(jnp.int32), splits.astype(jnp.int32))


def draw_text_count(key, part):
    return text_plan(key)[0]


def draw_text_splits(key, part):
    return text_plan(key)[1]


def head_gains(key, salt_value):
    head_key, entry_key = jax.random.split(jax.random.fold_in(key, salt_value))
    lower_end = 1.2
    upper_end = 2.0
    head_level = jnp.exp(jax.random.uniform(head_key, (HEADS, 1), jnp.float32, math.log(lower_end), math.log(upper_end)))
    jitter = 1.0 + 0.15 * jax.random.uniform(entry_key, (HEADS, HD), jnp.float32, -1.0, 1.0)
    return (head_level * jitter).astype(jnp.float32)


def draw_q_gain(key, part):
    return head_gains(key, 11)


def draw_k_gain(key, part):
    return head_gains(key, 13)


def level_of(own_key, shape, shards, low, largest):
    level, own = 1.0, jax.random.fold_in(own_key, 6)
    for dim, blocks in shards:
        draws = jnp.exp(jax.random.uniform(jax.random.fold_in(own, dim), (blocks,), jnp.float32, low / len(shards), largest / len(shards)))
        level = level * jnp.repeat(draws, shape[dim] // blocks).reshape([-1 if axis == dim else 1 for axis in range(len(shape))])
    return level


def scatter_about(rng, extent, deviation, most, cuts=(), kind=jnp.bfloat16):
    loudness = level_of(rng, extent, cuts, -0.22, 0.18) if cuts else 1.0
    values = jax.random.normal(rng, extent, jnp.float32) * deviation * loudness
    return jnp.minimum(jnp.maximum(values, -most), most).astype(kind)


def setup_inputs(seed: int = 0) -> dict:
    seeds = jax.random.split(jax.random.key(seed), 16)
    video = scatter_about(seeds[0], (JOBS, VIDEO, D), 1.0, 6.0, ((0, 4), (1, 8)))
    text_cache = scatter_about(seeds[1], (JOBS, TXT, DT), 1.0, 6.0, ((0, 4), (1, 8)))
    text_count = draw_text_count(jax.random.fold_in(seeds[15], 71), 0)
    holder = jax.random.permutation(seeds[3], JOBS).astype(jnp.int32)
    text_splits = draw_text_splits(jax.random.fold_in(seeds[15], 71), 0)
    mod_shift = scatter_about(seeds[5], (JOBS, D), 0.5, 3.0, (), jnp.float32)
    mod_scale = scatter_about(seeds[6], (JOBS, D), 0.3, 2.0, (), jnp.float32)
    mod_gate = scatter_about(seeds[7], (JOBS, D), 1.0, 4.0, (), jnp.float32)
    text_gain = jnp.clip(1.0 + 0.15 * jax.random.normal(seeds[8], (DT,), jnp.float32), 0.25, 1.75)
    refine_w = scatter_about(seeds[9], (DT, D), DT ** -0.5, 0.09375, ((1, 4),))
    refine_bias = scatter_about(seeds[10], (D,), 0.5, 3.0, ((0, 4),), jnp.float32)
    w_qkv = scatter_about(seeds[11], (D, HEADS, 3, HD), D ** -0.5, 0.109375, ((1, 4),))
    q_gain = draw_q_gain(jax.random.fold_in(seeds[15], 71), 0)
    k_gain = draw_k_gain(jax.random.fold_in(seeds[15], 71), 0)
    w_out = scatter_about(seeds[14], (HEADS, HD, D), (HEADS * HD) ** -0.5, 0.125, ((0, 4),))
    return dict(video=video, text_cache=text_cache, text_count=text_count, holder=holder, text_splits=text_splits, mod_shift=mod_shift, mod_scale=mod_scale, mod_gate=mod_gate, text_gain=text_gain, refine_w=refine_w, refine_bias=refine_bias, w_qkv=w_qkv, q_gain=q_gain, k_gain=k_gain, w_out=w_out)


epsilon = 1e-06

def rms_scale(values, gains):
    mean_square = lax.optimization_barrier(jnp.mean(values * values, axis=-1, keepdims=True))
    return values * lax.rsqrt(mean_square + epsilon) * gains

def modulate(tokens, shift_part, scale_part):
    widened = tokens.astype(jnp.float32)
    centre = lax.optimization_barrier(jnp.mean(widened, axis=-1, keepdims=True))
    spread_sq = lax.optimization_barrier(jnp.mean((widened - centre) ** 2, axis=-1, keepdims=True))
    normed = (widened - centre) * lax.rsqrt(spread_sq + epsilon)
    return (normed * (1.0 + scale_part) + shift_part).astype(jnp.bfloat16)

def refine_rows(raw_text, text_gain, refine_w, refine_bias):
    normed = rms_scale(raw_text.astype(jnp.float32), text_gain).astype(jnp.bfloat16)
    lifted = jnp.dot(normed, refine_w, preferred_element_type=jnp.float32)
    return (lifted + refine_bias).astype(jnp.bfloat16)

def attend(queries, key_rows, values, key_ok):
    scores = jnp.dot(queries, key_rows.T, preferred_element_type=jnp.float32) * HD ** (-0.5)
    scores = jnp.where(key_ok[None, :], scores, -1e+30)
    highest = lax.optimization_barrier(jnp.max(scores, axis=-1, keepdims=True))
    weights = jnp.exp(scores - highest)
    summed = lax.optimization_barrier(jnp.sum(weights, axis=-1, keepdims=True))
    weights = (weights / summed).astype(jnp.bfloat16)
    return jnp.dot(weights, values, preferred_element_type=jnp.float32).astype(jnp.bfloat16)

def reference(video, text_cache, text_count, holder, text_splits, mod_shift, mod_scale, mod_gate, text_gain, refine_w, refine_bias, w_qkv, q_gain, k_gain, w_out):
    row_count = VID_DEV + TCAP
    group_size = HEADS // N_JOB
    offsets = (jnp.cumsum(text_splits, axis=1) - text_splits).astype(jnp.int32)
    slot_ids = jnp.arange(TCAP, dtype=jnp.int32)
    head_weights = jnp.moveaxis(w_qkv, 1, 0)
    video_outs = []
    text_outs = []
    for job_index in range(JOBS):
        raw_text = text_cache[holder[job_index]]
        refined = refine_rows(raw_text, text_gain, refine_w, refine_bias)
        padded = jnp.concatenate([refined, jnp.zeros((TCAP, D), jnp.bfloat16)], axis=0)
        position = (offsets[job_index][:, None] + slot_ids[None, :]).astype(jnp.int32)
        slot_valid = (slot_ids[None, :] < text_splits[job_index][:, None]) & (position < text_count[job_index])
        gathered = padded[position]
        text_rows = jnp.where(slot_valid[:, :, None], gathered, jnp.zeros_like(gathered))
        video_part = video[job_index].reshape(N_SEQ, VID_DEV, D)
        sequence = jnp.concatenate([video_part, text_rows], axis=1).reshape(N_SEQ * row_count, D)
        key_ok = jnp.concatenate([jnp.ones((N_SEQ, VID_DEV), jnp.bool_), slot_valid], axis=1).reshape(-1)
        modded = modulate(sequence, mod_shift[job_index], mod_scale[job_index])

        def one_head(operands):
            head_w, head_q, head_k = operands
            projections = jnp.dot(modded, head_w.reshape(D, 3 * HD), preferred_element_type=jnp.float32).reshape(-1, 3, HD)
            queries = rms_scale(projections[:, 0], head_q).astype(jnp.bfloat16)
            key_rows = rms_scale(projections[:, 1], head_k).astype(jnp.bfloat16)
            values = projections[:, 2].astype(jnp.bfloat16)
            return attend(queries, key_rows, values, key_ok)
        attended = lax.map(one_head, (head_weights, q_gain, k_gain))
        projected = jnp.zeros((N_SEQ * row_count, D), jnp.float32)
        for group_index in range(N_JOB):
            chosen = attended[group_index * group_size:(group_index + 1) * group_size]
            flat_heads = jnp.transpose(chosen, (1, 0, 2)).reshape(-1, group_size * HD)
            group_w = w_out[group_index * group_size:(group_index + 1) * group_size].reshape(group_size * HD, D)
            part_sum = jnp.dot(flat_heads, group_w, preferred_element_type=jnp.float32)
            rounded = lax.optimization_barrier(part_sum.astype(jnp.bfloat16))
            projected = projected + rounded.astype(jnp.float32)
        result = (sequence.astype(jnp.float32) + mod_gate[job_index] * projected).astype(jnp.bfloat16)
        result = result.reshape(N_SEQ, row_count, D)
        video_outs.append(result[:, :VID_DEV].reshape(N_SEQ * VID_DEV, D))
        text_part = result[:, VID_DEV:]
        text_outs.append(jnp.where(slot_valid[:, :, None], text_part, jnp.zeros_like(text_part)).reshape(N_SEQ * TCAP, D))
    return (jnp.stack(video_outs), jnp.stack(text_outs))
```

```python
import functools

import jax
import jax.numpy as jnp
from jax import lax
from jax.experimental import pallas as pl
from jax.experimental.pallas import tpu as pltpu
from jax.sharding import PartitionSpec as P

HD = 128
TXT = 256


epsilon = 1e-06


def rms_scale(values, gains):
    mean_square = jnp.mean(values * values, axis=-1, keepdims=True)
    return values * lax.rsqrt(mean_square + epsilon) * gains


def modulate(tokens, shift_part, scale_part):
    widened = tokens.astype(jnp.float32)
    centre = jnp.mean(widened, axis=-1, keepdims=True)
    spread_sq = jnp.mean((widened - centre) ** 2, axis=-1, keepdims=True)
    normed = (widened - centre) * lax.rsqrt(spread_sq + epsilon)
    return (normed * (1.0 + scale_part) + shift_part).astype(jnp.bfloat16)


def refine_rows(raw_text, text_gain, refine_w, refine_bias):
    normed = rms_scale(raw_text.astype(jnp.float32), text_gain).astype(jnp.bfloat16)
    lifted = jnp.einsum("jrt,tc->jrc", normed, refine_w, preferred_element_type=jnp.float32)
    return (lifted + refine_bias).astype(jnp.bfloat16)


def project_heads(modded, w_qkv, q_gain, k_gain):
    projections = jnp.einsum("jrd,dhce->jrhce", modded, w_qkv, preferred_element_type=jnp.float32)
    queries = rms_scale(projections[:, :, :, 0], q_gain).astype(jnp.bfloat16)
    key_rows = rms_scale(projections[:, :, :, 1], k_gain).astype(jnp.bfloat16)
    values = projections[:, :, :, 2].astype(jnp.bfloat16)
    return jnp.stack([queries, key_rows, values], axis=3)


def query_block(query_count, unit_rows):
    unit_total = query_count // unit_rows
    for factor in range(1, unit_total + 1):
        if unit_total % factor == 0 and factor * unit_rows >= 512:
            return factor * unit_rows
    return query_count


def attend(queries, key_rows, values, key_ok, block_rows):
    query_count = queries.shape[0]
    stacked_blocks = queries.reshape(query_count // block_rows, block_rows, queries.shape[1])
    scale_factor = HD ** (-0.5)

    def one_block(query_part):
        scores = (
            jnp.einsum("qe,ke->qk", query_part, key_rows, preferred_element_type=jnp.float32)
            * scale_factor
        )
        scores = jnp.where(key_ok[None, :], scores, -1e30)
        highest = jnp.max(scores, axis=-1, keepdims=True)
        weights = jnp.exp(scores - highest)
        summed = jnp.sum(weights, axis=-1, keepdims=True)
        weights = (weights / summed).astype(jnp.bfloat16)
        return jnp.dot(weights, values, preferred_element_type=jnp.float32).astype(jnp.bfloat16)

    return lax.map(one_block, stacked_blocks).reshape(query_count, queries.shape[1])


def general_body(
    video,
    text_cache,
    text_count,
    holder,
    text_splits,
    mod_shift,
    mod_scale,
    mod_gate,
    text_gain,
    refine_w,
    refine_bias,
    w_qkv,
    q_gain,
    k_gain,
    w_out,
):
    job_count = lax.axis_size("job")
    shard_count = lax.axis_size("seq")
    my_job = lax.axis_index("job")
    my_shard = lax.axis_index("seq")
    video_rows = video.shape[1]
    block_rows = text_cache.shape[1]
    slot_count = 2 * block_rows
    row_count = video_rows + slot_count
    group_size = w_qkv.shape[1]
    pair_count = job_count * group_size
    slot_total = max(pair_count, shard_count)
    repeat_count = slot_total // pair_count
    per_device = slot_total // shard_count
    offsets = jnp.cumsum(text_splits, axis=1) - text_splits
    slot_ids = jnp.arange(slot_count, dtype=jnp.int32)
    my_offsets = lax.dynamic_index_in_dim(offsets, my_shard, 1, keepdims=False)
    my_splits = lax.dynamic_index_in_dim(text_splits, my_shard, 1, keepdims=False)
    slot_valid = (slot_ids[None, :] < my_splits[:, None]) & (
        my_offsets[:, None] + slot_ids[None, :] < text_count[:, None]
    )
    position = holder[:, None] * (TXT + slot_count) + my_offsets[:, None] + slot_ids[None, :]
    cache_rows = lax.all_gather(text_cache, "job", axis=0, tiled=True)
    refined = refine_rows(cache_rows, text_gain, refine_w, refine_bias)
    gathered_text = lax.all_gather(refined, "seq", axis=1, tiled=True)
    width = gathered_text.shape[2]
    padded = jnp.concatenate(
        [
            gathered_text,
            jnp.zeros((gathered_text.shape[0], slot_count, width), gathered_text.dtype),
        ],
        axis=1,
    )
    flat_rows = padded.reshape(-1, width)
    chosen = jnp.take(flat_rows, position.reshape(-1), axis=0).reshape(job_count, slot_count, width)
    text_cols = jnp.where(slot_valid[:, :, None], chosen, jnp.zeros_like(chosen))
    text_full = lax.all_gather(text_cols, "job", axis=2, tiled=True)
    modded = modulate(
        lax.all_gather(video, "job", axis=0, tiled=True),
        mod_shift[:, None, :],
        mod_scale[:, None, :],
    )
    video_heads = project_heads(modded, w_qkv, q_gain, k_gain)
    text_modded = modulate(text_full, mod_shift[:, None, :], mod_scale[:, None, :])
    text_heads = project_heads(text_modded, w_qkv, q_gain, k_gain)
    heads_all = jnp.concatenate([video_heads, text_heads], axis=1)
    by_row = jnp.transpose(heads_all, (1, 0, 2, 3, 4)).reshape(row_count, pair_count, 3, HD)
    query_rows = by_row[:, :, 0]
    key_rows = jnp.tile(by_row[:, :, 1], (1, repeat_count, 1))
    value_rows = jnp.tile(by_row[:, :, 2], (1, repeat_count, 1))
    query_send = jnp.tile(query_rows, (1, repeat_count, 1))
    query_recv, key_recv, value_recv = (
        lax.all_to_all(query_send, "seq", split_axis=1, concat_axis=0, tiled=True),
        lax.all_to_all(key_rows, "seq", split_axis=1, concat_axis=0, tiled=True),
        lax.all_to_all(value_rows, "seq", split_axis=1, concat_axis=0, tiled=True),
    )
    my_part = my_shard * per_device // pair_count
    outputs = []
    for slot_index in range(per_device):
        slot_global = my_shard * per_device + slot_index
        job_of_slot = slot_global % pair_count // group_size
        splits_row = lax.dynamic_index_in_dim(text_splits, job_of_slot, 0, keepdims=False)
        offsets_row = lax.dynamic_index_in_dim(offsets, job_of_slot, 0, keepdims=False)
        count_of_job = lax.dynamic_index_in_dim(text_count, job_of_slot, 0, keepdims=False)
        key_valid = (slot_ids[None, :] < splits_row[:, None]) & (
            offsets_row[:, None] + slot_ids[None, :] < count_of_job
        )
        key_ok = jnp.concatenate(
            [jnp.ones((shard_count, video_rows), jnp.bool_), key_valid], axis=1
        ).reshape(-1)
        grouped = query_recv[:, slot_index].reshape(
            shard_count // repeat_count, repeat_count, row_count, HD
        )
        queries = lax.dynamic_index_in_dim(grouped, my_part, 1, keepdims=False).reshape(-1, HD)
        block_size = query_block(queries.shape[0], row_count)
        outputs.append(
            attend(queries, key_recv[:, slot_index], value_recv[:, slot_index], key_ok, block_size)
        )
    attended = jnp.stack(outputs, axis=1)
    spread_out = attended.reshape(shard_count // repeat_count, 1, row_count, per_device, HD)
    selector = (
        (jnp.arange(repeat_count) == my_part).astype(jnp.bfloat16).reshape(1, repeat_count, 1, 1, 1)
    )
    send_back = (spread_out * selector).reshape(shard_count * row_count, per_device, HD)
    returned = lax.all_to_all(send_back, "seq", split_axis=0, concat_axis=1, tiled=True)
    own_heads = lax.dynamic_index_in_dim(
        returned.reshape(row_count, repeat_count, pair_count, HD),
        my_shard % repeat_count,
        1,
        keepdims=False,
    )
    per_job = jnp.transpose(
        own_heads.reshape(row_count, job_count, group_size * HD), (1, 0, 2)
    ).reshape(job_count * row_count, group_size * HD)
    out_weight = w_out.reshape(group_size * HD, w_out.shape[2])
    projected = lax.psum_scatter(
        jnp.dot(per_job, out_weight, preferred_element_type=jnp.float32).astype(jnp.bfloat16),
        "job",
        scatter_dimension=0,
        tiled=True,
    ).astype(jnp.float32)
    own_rows = jnp.concatenate(
        [video[0], lax.dynamic_index_in_dim(text_full, my_job, 0, keepdims=False)], axis=0
    )
    gate_row = lax.dynamic_index_in_dim(mod_gate, my_job, 0, keepdims=False)
    result = (own_rows.astype(jnp.float32) + gate_row * projected).astype(jnp.bfloat16)
    own_valid = lax.dynamic_index_in_dim(slot_valid, my_job, 0, keepdims=False)
    text_result = jnp.where(
        own_valid[:, None], result[video_rows:], jnp.zeros_like(result[video_rows:])
    )
    return (result[:video_rows][None], text_result[None])


def vmem_spec():
    return pl.BlockSpec(memory_space=pltpu.VMEM)


def smem_spec():
    return pl.BlockSpec(memory_space=pltpu.SMEM)


def params(mib, grid_dims=0):
    semantics = ("arbitrary",) * grid_dims if grid_dims else None
    return pltpu.CompilerParams(vmem_limit_bytes=mib << 20, dimension_semantics=semantics)


def text_kernel(where_ref, parts_ref, shift_ref, scale_ref, modded_ref, own_ref, rows_ref):
    mine = where_ref[0]
    jobs, _, rows, width = parts_ref.shape
    for r in range(jobs):
        slot = where_ref[1 + r]
        for b in range(jobs):
            rows_ref[:, b * width : (b + 1) * width] = parts_ref[mine ^ b, slot ^ b]
        raw = rows_ref[...]
        if r == 0:
            own_ref[...] = raw
        modded_ref[r * rows : (r + 1) * rows] = modulate(
            raw, shift_ref[r : r + 1], scale_ref[r : r + 1]
        )


def text_rows_of_jobs(where, parts, shift_rel, scale_rel):
    jobs, _, rows, width = parts.shape
    full = jobs * width
    return pl.pallas_call(
        text_kernel,
        out_shape=(
            jax.ShapeDtypeStruct((jobs * rows, full), jnp.bfloat16),
            jax.ShapeDtypeStruct((rows, full), jnp.bfloat16),
        ),
        in_specs=[smem_spec(), vmem_spec(), vmem_spec(), vmem_spec()],
        out_specs=(vmem_spec(), vmem_spec()),
        scratch_shapes=[pltpu.VMEM((rows, full), jnp.bfloat16)],
        compiler_params=params(16),
        cost_estimate=pl.CostEstimate(flops=10 * jobs * rows * full, bytes_accessed=2 << 20, transcendentals=0),
    )(where, parts, shift_rel, scale_rel)


def qkv_kernel(has_text, *refs):
    if has_text:
        a_ref, b_ref, text_ref, shift_ref, scale_ref, w_ref, qg_ref, kg_ref, out_ref, x_ref = refs
    else:
        a_ref, b_ref, shift_ref, scale_ref, w_ref, qg_ref, kg_ref, out_ref, x_ref = refs
    rows = a_ref.shape[0]
    step = pl.program_id(0)

    @pl.when(step == 0)
    def _():
        x_ref[0:rows] = modulate(a_ref[...], shift_ref[0:1], scale_ref[0:1])
        x_ref[rows : 2 * rows] = modulate(b_ref[...], shift_ref[1:2], scale_ref[1:2])
        if has_text:
            x_ref[2 * rows :] = text_ref[...]

    heads = w_ref.shape[1]
    trows = (x_ref.shape[0] - 2 * rows) // 4
    for h in range(heads):
        head = step * heads + h
        weights = jnp.concatenate([w_ref[0, h], w_ref[1, h], w_ref[2, h]], axis=1)
        raw = jnp.dot(x_ref[...], weights, preferred_element_type=jnp.float32)
        queries = rms_scale(raw[:, :HD], qg_ref[pl.ds(head, 1)]).astype(jnp.bfloat16)
        key_rows = rms_scale(raw[:, HD : 2 * HD], kg_ref[pl.ds(head, 1)]).astype(jnp.bfloat16)
        values = raw[:, 2 * HD :].astype(jnp.bfloat16)
        done = jnp.concatenate([queries, key_rows, values], axis=1)
        for r in range(2):
            out_ref[r, h, 0:rows] = done[r * rows : (r + 1) * rows]
            if has_text:
                base = 2 * rows + r * trows
                out_ref[r, h, rows : rows + trows] = done[base : base + trows]
                base = 2 * rows + (2 + r) * trows
                out_ref[r, h, rows + trows :] = done[base : base + trows]


def project_qkv(pair, text_modded, shift_two, scale_two, weights, q_gain, k_gain):
    rows, width = pair[0].shape
    group = weights.shape[1]
    has_text = text_modded is not None
    extra = [text_modded] if has_text else []
    total = 2 * rows + (text_modded.shape[0] if has_text else 0)
    out_rows = total // 2
    step_heads = 2
    return pl.pallas_call(
        functools.partial(qkv_kernel, has_text),
        grid=(group // step_heads,),
        out_shape=jax.ShapeDtypeStruct((2, group, out_rows, 3 * HD), jnp.bfloat16),
        in_specs=[vmem_spec()] * (4 + len(extra))
        + [pl.BlockSpec((3, step_heads, width, HD), lambda i: (0, i, 0, 0)), vmem_spec(), vmem_spec()],
        out_specs=pl.BlockSpec((2, step_heads, out_rows, 3 * HD), lambda i: (0, i, 0, 0)),
        scratch_shapes=[pltpu.VMEM((total, width), jnp.bfloat16)],
        compiler_params=params(40, 1),
        cost_estimate=pl.CostEstimate(
            flops=2 * total * width * group * 3 * HD,
            bytes_accessed=2 * group * 3 * HD * width + 4 * total * width,
            transcendentals=0,
        ),
    )(*pair, *extra, shift_two, scale_two, weights, q_gain, k_gain)


def attention_kernel(text_base, meta_ref, video_ref, text_ref, out_ref, k_ref, v_ref, t_ref):
    shards, _, _ = video_ref.shape
    vrows = 128
    trows = t_ref.shape[0] // shards
    slots = out_ref.shape[1] - vrows
    video = shards * vrows
    total = k_ref.shape[0]
    for s in range(shards):
        k_ref[s * vrows : (s + 1) * vrows] = video_ref[s, 0:vrows, HD : 2 * HD]
        v_ref[s * vrows : (s + 1) * vrows] = video_ref[s, 0:vrows, 2 * HD :]
        lo = video + s * trows
        k_ref[lo : lo + trows] = text_ref[s, text_base : text_base + trows, HD : 2 * HD]
        v_ref[lo : lo + trows] = text_ref[s, text_base : text_base + trows, 2 * HD :]
    column = lax.broadcasted_iota(jnp.int32, (1, total), 1)
    key_ok = column < video + meta_ref[0]
    scale = HD ** (-0.5)

    def one_block(queries):
        scores = lax.dot_general(
            queries, k_ref[...], (((1,), (1,)), ((), ())), preferred_element_type=jnp.float32
        )
        scores = jnp.where(key_ok, scores * scale, -1e30)
        weights = jnp.exp(scores - jnp.max(scores, axis=-1, keepdims=True))
        summed = jnp.sum(weights, axis=-1, keepdims=True)
        mixed = jnp.dot(weights.astype(jnp.bfloat16), v_ref[...], preferred_element_type=jnp.float32)
        return (mixed / summed).astype(jnp.bfloat16)

    def video_block(i, carry):
        done = one_block(video_ref[pl.ds(2 * i, 2), 0:vrows, 0:HD].reshape(2 * vrows, HD))
        out_ref[pl.ds(2 * i, 2), 0:vrows] = done.reshape(2, vrows, HD)
        return carry

    lax.fori_loop(0, shards // 2, video_block, 0)
    t_ref[...] = one_block(
        text_ref[:, text_base : text_base + trows, 0:HD].reshape(shards * trows, HD)
    )
    slot = lax.broadcasted_iota(jnp.int32, (slots, shards * trows), 0)
    row = lax.broadcasted_iota(jnp.int32, (slots, shards * trows), 1)
    for s in range(shards):
        chosen = (row == slot + meta_ref[1 + s]) & (slot < meta_ref[1 + shards + s])
        chosen = jnp.where(chosen, 1.0, 0.0).astype(jnp.bfloat16)
        out_ref[s, vrows:] = jnp.dot(
            chosen, t_ref[...], preferred_element_type=jnp.float32
        ).astype(jnp.bfloat16)


def attend_pair(meta, video_qkv, text_qkv, text_base, trows, slots):
    shards = video_qkv.shape[0]
    vrows = 128
    total = shards * (vrows + trows)
    return pl.pallas_call(
        functools.partial(attention_kernel, text_base),
        out_shape=jax.ShapeDtypeStruct((shards, vrows + slots, HD), jnp.bfloat16),
        in_specs=[smem_spec(), vmem_spec(), vmem_spec()],
        out_specs=vmem_spec(),
        scratch_shapes=[
            pltpu.VMEM((total, HD), jnp.bfloat16),
            pltpu.VMEM((total, HD), jnp.bfloat16),
            pltpu.VMEM((shards * trows, HD), jnp.bfloat16),
        ],
        compiler_params=params(40),
        cost_estimate=pl.CostEstimate(
            flops=4 * total * total * HD, bytes_accessed=3 << 20, transcendentals=total * total
        ),
    )(meta, video_qkv, text_qkv)


def out_kernel(heads_ref, w_ref, out_ref):
    jobs, group, _, _ = heads_ref.shape
    for r in range(jobs):
        rows = jnp.concatenate([heads_ref[r, h] for h in range(group)], axis=1)
        out_ref[r] = jnp.dot(rows, w_ref[...], preferred_element_type=jnp.float32).astype(jnp.bfloat16)


def project_out(heads, weights):
    jobs, group, rows, _ = heads.shape
    depth, width = weights.shape
    cols = 768
    return pl.pallas_call(
        out_kernel,
        grid=(width // cols,),
        out_shape=jax.ShapeDtypeStruct((jobs, rows, width), jnp.bfloat16),
        in_specs=[vmem_spec(), pl.BlockSpec((depth, cols), lambda i: (0, i))],
        out_specs=pl.BlockSpec((jobs, rows, cols), lambda i: (0, 0, i)),
        compiler_params=params(40, 1),
        cost_estimate=pl.CostEstimate(
            flops=2 * jobs * rows * depth * width, bytes_accessed=8 << 20, transcendentals=0
        ),
    )(heads, weights)


def two_wave_body(
    video,
    text_cache,
    text_count,
    holder,
    text_splits,
    mod_shift,
    mod_scale,
    mod_gate,
    text_gain,
    refine_w,
    refine_bias,
    w_qkv,
    q_gain,
    k_gain,
    w_out,
):
    job_count = lax.axis_size("job")
    shard_count = lax.axis_size("seq")
    my_job = lax.axis_index("job")
    my_shard = lax.axis_index("seq")
    group_size = w_qkv.shape[1]
    trows = text_cache.shape[1]
    slot_count = 2 * trows
    vrows = video.shape[1]

    def to_core(x):
        return lax.ppermute(x, "job", [(i, i ^ 1) for i in range(job_count)])

    def to_chip(x):
        return lax.ppermute(x, "job", [(i, i ^ 2) for i in range(job_count)])

    def over_seq(x):
        return lax.all_to_all(x, "seq", split_axis=0, concat_axis=0, tiled=False)

    def pick(array, index):
        return lax.dynamic_index_in_dim(array, index, 0, keepdims=False)

    offsets = jnp.cumsum(text_splits, axis=1) - text_splits
    jobs_rel = [my_job ^ r for r in range(job_count)]
    shift_rel = jnp.stack([pick(mod_shift, j) for j in jobs_rel])
    scale_rel = jnp.stack([pick(mod_scale, j) for j in jobs_rel])
    qkv_w = jnp.transpose(w_qkv, (2, 1, 0, 3))

    own_video = video[0]
    core_video = to_core(own_video)

    normed = rms_scale(text_cache[0].astype(jnp.float32), text_gain).astype(jnp.bfloat16)
    normed_core = to_core(normed)
    normed_chip = to_chip(normed)
    normed_both = to_core(normed_chip)
    lifted = jnp.dot(
        jnp.concatenate([normed, normed_core, normed_chip, normed_both], axis=0),
        refine_w,
        preferred_element_type=jnp.float32,
    )
    refined = (lifted + refine_bias).astype(jnp.bfloat16).reshape(job_count, trows, -1)
    refined_core = to_core(refined)
    refined_chip = to_chip(refined)
    refined_both = to_core(refined_chip)
    parts = jnp.stack([refined, refined_core, refined_chip, refined_both])
    where = jnp.stack([my_job] + [pick(holder, j) for j in jobs_rel]).astype(jnp.int32)
    text_modded, own_text = text_rows_of_jobs(where, parts, shift_rel, scale_rel)
    job_text = lax.all_gather(own_text, "seq", axis=0, tiled=True)

    local_send = project_qkv(
        (own_video, core_video), None, shift_rel[:2], scale_rel[:2], qkv_w, q_gain, k_gain
    )
    local_qkv = over_seq(local_send.reshape(shard_count, vrows, 3 * HD))
    chip_video = to_chip(own_video)
    both_video = to_core(chip_video)
    remote_send = project_qkv(
        (chip_video, both_video), text_modded, shift_rel[2:], scale_rel[2:], qkv_w, q_gain, k_gain
    )
    remote_qkv = over_seq(remote_send.reshape(shard_count, vrows + 2 * trows, 3 * HD))

    half = my_shard // group_size
    out_weight = w_out.reshape(group_size * HD, w_out.shape[2])

    def meta_of(job):
        return jnp.concatenate(
            [pick(text_count, job)[None], pick(offsets, job), pick(text_splits, job)]
        ).astype(jnp.int32)

    remote_mixed = attend_pair(
        meta_of(my_job ^ half ^ 2), remote_qkv, remote_qkv, vrows + trows, trows, slot_count
    )
    remote_back = over_seq(remote_mixed)
    local_qkv, _ = lax.optimization_barrier((local_qkv, remote_mixed))
    local_mixed = attend_pair(
        meta_of(my_job ^ half), local_qkv, remote_qkv, vrows, trows, slot_count
    )
    local_back = over_seq(local_mixed)
    row_count = vrows + slot_count
    remote_part = project_out(
        remote_back.reshape(2, group_size, row_count, HD), out_weight
    )
    from_core = to_core(remote_part[1])
    crossing = (remote_part[0].astype(jnp.float32) + from_core.astype(jnp.float32)).astype(
        jnp.bfloat16
    )
    from_chip = to_chip(crossing)
    local_part = project_out(local_back.reshape(2, group_size, row_count, HD), out_weight)
    local_core = to_core(local_part[1])

    projected = (
        local_part[0].astype(jnp.float32)
        + local_core.astype(jnp.float32)
        + from_chip.astype(jnp.float32)
    )
    my_offset = pick(pick(offsets, my_job), my_shard)
    my_split = pick(pick(text_splits, my_job), my_shard)
    slot_ids = jnp.arange(slot_count, dtype=jnp.int32)
    own_valid = (slot_ids < my_split) & (my_offset + slot_ids < pick(text_count, my_job))
    padded = jnp.pad(job_text, ((0, slot_count), (0, 0)))
    slot_rows = lax.dynamic_slice_in_dim(padded, my_offset, slot_count, 0)
    gate_row = pick(mod_gate, my_job)
    video_result = own_video.astype(jnp.float32) + gate_row * projected[:vrows]
    text_result = slot_rows.astype(jnp.float32) + gate_row * projected[vrows:]
    text_result = jnp.where(own_valid[:, None], text_result, 0.0)
    return (
        video_result.astype(jnp.bfloat16)[None],
        text_result.astype(jnp.bfloat16)[None],
    )


def body(*arrays):
    video, text_cache, w_qkv = arrays[0], arrays[1], arrays[11]
    job_count = lax.axis_size("job")
    shard_count = lax.axis_size("seq")
    fits = (
        job_count == 4
        and shard_count == 2 * w_qkv.shape[1]
        and video.shape[1] == 128
        and text_cache.shape[1] == 32
    )
    return (two_wave_body if fits else general_body)(*arrays)


def solution(mesh):
    placed = (
        P("job", "seq", None),
        P("job", "seq", None),
        P(),
        P(),
        P(),
        P(),
        P(),
        P(),
        P(),
        P(None, "job"),
        P("job"),
        P(None, "job", None, None),
        P("job", None),
        P("job", None),
        P("job", None, None),
    )
    return jax.shard_map(
        body,
        mesh=mesh,
        in_specs=placed,
        out_specs=(P("job", "seq", None), P("job", "seq", None)),
        check_vma=False,
    )
```

```python
import functools

import jax
import jax.numpy as jnp
from jax import lax
from jax.experimental import pallas as pl
from jax.experimental.pallas import tpu as pltpu
from jax.sharding import PartitionSpec as P

HD = 128
TXT = 256


epsilon = 1e-06


def rms_scale(values, gains):
    mean_square = jnp.mean(values * values, axis=-1, keepdims=True)
    return values * lax.rsqrt(mean_square + epsilon) * gains


def modulate(tokens, shift_part, scale_part):
    widened = tokens.astype(jnp.float32)
    centre = jnp.mean(widened, axis=-1, keepdims=True)
    spread_sq = jnp.mean((widened - centre) ** 2, axis=-1, keepdims=True)
    normed = (widened - centre) * lax.rsqrt(spread_sq + epsilon)
    return (normed * (1.0 + scale_part) + shift_part).astype(jnp.bfloat16)


def refine_rows(raw_text, text_gain, refine_w, refine_bias):
    normed = rms_scale(raw_text.astype(jnp.float32), text_gain).astype(jnp.bfloat16)
    lifted = jnp.einsum("jrt,tc->jrc", normed, refine_w, preferred_element_type=jnp.float32)
    return (lifted + refine_bias).astype(jnp.bfloat16)


def project_heads(modded, w_qkv, q_gain, k_gain):
    projections = jnp.einsum("jrd,dhce->jrhce", modded, w_qkv, preferred_element_type=jnp.float32)
    queries = rms_scale(projections[:, :, :, 0], q_gain).astype(jnp.bfloat16)
    key_rows = rms_scale(projections[:, :, :, 1], k_gain).astype(jnp.bfloat16)
    values = projections[:, :, :, 2].astype(jnp.bfloat16)
    return jnp.stack([queries, key_rows, values], axis=3)


def query_block(query_count, unit_rows):
    unit_total = query_count // unit_rows
    for factor in range(1, unit_total + 1):
        if unit_total % factor == 0 and factor * unit_rows >= 512:
            return factor * unit_rows
    return query_count


def attend(queries, key_rows, values, key_ok, block_rows):
    query_count = queries.shape[0]
    stacked_blocks = queries.reshape(query_count // block_rows, block_rows, queries.shape[1])
    scale_factor = HD ** (-0.5)

    def one_block(query_part):
        scores = (
            jnp.einsum("qe,ke->qk", query_part, key_rows, preferred_element_type=jnp.float32)
            * scale_factor
        )
        scores = jnp.where(key_ok[None, :], scores, -1e30)
        highest = jnp.max(scores, axis=-1, keepdims=True)
        weights = jnp.exp(scores - highest)
        summed = jnp.sum(weights, axis=-1, keepdims=True)
        weights = (weights / summed).astype(jnp.bfloat16)
        return jnp.dot(weights, values, preferred_element_type=jnp.float32).astype(jnp.bfloat16)

    return lax.map(one_block, stacked_blocks).reshape(query_count, queries.shape[1])


def general_body(
    video,
    text_cache,
    text_count,
    holder,
    text_splits,
    mod_shift,
    mod_scale,
    mod_gate,
    text_gain,
    refine_w,
    refine_bias,
    w_qkv,
    q_gain,
    k_gain,
    w_out,
):
    job_count = lax.axis_size("job")
    shard_count = lax.axis_size("seq")
    my_job = lax.axis_index("job")
    my_shard = lax.axis_index("seq")
    video_rows = video.shape[1]
    block_rows = text_cache.shape[1]
    slot_count = 2 * block_rows
    row_count = video_rows + slot_count
    group_size = w_qkv.shape[1]
    pair_count = job_count * group_size
    slot_total = max(pair_count, shard_count)
    repeat_count = slot_total // pair_count
    per_device = slot_total // shard_count
    offsets = jnp.cumsum(text_splits, axis=1) - text_splits
    slot_ids = jnp.arange(slot_count, dtype=jnp.int32)
    my_offsets = lax.dynamic_index_in_dim(offsets, my_shard, 1, keepdims=False)
    my_splits = lax.dynamic_index_in_dim(text_splits, my_shard, 1, keepdims=False)
    slot_valid = (slot_ids[None, :] < my_splits[:, None]) & (
        my_offsets[:, None] + slot_ids[None, :] < text_count[:, None]
    )
    position = holder[:, None] * (TXT + slot_count) + my_offsets[:, None] + slot_ids[None, :]
    cache_rows = lax.all_gather(text_cache, "job", axis=0, tiled=True)
    refined = refine_rows(cache_rows, text_gain, refine_w, refine_bias)
    gathered_text = lax.all_gather(refined, "seq", axis=1, tiled=True)
    width = gathered_text.shape[2]
    padded = jnp.concatenate(
        [
            gathered_text,
            jnp.zeros((gathered_text.shape[0], slot_count, width), gathered_text.dtype),
        ],
        axis=1,
    )
    flat_rows = padded.reshape(-1, width)
    chosen = jnp.take(flat_rows, position.reshape(-1), axis=0).reshape(job_count, slot_count, width)
    text_cols = jnp.where(slot_valid[:, :, None], chosen, jnp.zeros_like(chosen))
    text_full = lax.all_gather(text_cols, "job", axis=2, tiled=True)
    modded = modulate(
        lax.all_gather(video, "job", axis=0, tiled=True),
        mod_shift[:, None, :],
        mod_scale[:, None, :],
    )
    video_heads = project_heads(modded, w_qkv, q_gain, k_gain)
    text_modded = modulate(text_full, mod_shift[:, None, :], mod_scale[:, None, :])
    text_heads = project_heads(text_modded, w_qkv, q_gain, k_gain)
    heads_all = jnp.concatenate([video_heads, text_heads], axis=1)
    by_row = jnp.transpose(heads_all, (1, 0, 2, 3, 4)).reshape(row_count, pair_count, 3, HD)
    query_rows = by_row[:, :, 0]
    key_rows = jnp.tile(by_row[:, :, 1], (1, repeat_count, 1))
    value_rows = jnp.tile(by_row[:, :, 2], (1, repeat_count, 1))
    query_send = jnp.tile(query_rows, (1, repeat_count, 1))
    query_recv, key_recv, value_recv = (
        lax.all_to_all(query_send, "seq", split_axis=1, concat_axis=0, tiled=True),
        lax.all_to_all(key_rows, "seq", split_axis=1, concat_axis=0, tiled=True),
        lax.all_to_all(value_rows, "seq", split_axis=1, concat_axis=0, tiled=True),
    )
    my_part = my_shard * per_device // pair_count
    outputs = []
    for slot_index in range(per_device):
        slot_global = my_shard * per_device + slot_index
        job_of_slot = slot_global % pair_count // group_size
        splits_row = lax.dynamic_index_in_dim(text_splits, job_of_slot, 0, keepdims=False)
        offsets_row = lax.dynamic_index_in_dim(offsets, job_of_slot, 0, keepdims=False)
        count_of_job = lax.dynamic_index_in_dim(text_count, job_of_slot, 0, keepdims=False)
        key_valid = (slot_ids[None, :] < splits_row[:, None]) & (
            offsets_row[:, None] + slot_ids[None, :] < count_of_job
        )
        key_ok = jnp.concatenate(
            [jnp.ones((shard_count, video_rows), jnp.bool_), key_valid], axis=1
        ).reshape(-1)
        grouped = query_recv[:, slot_index].reshape(
            shard_count // repeat_count, repeat_count, row_count, HD
        )
        queries = lax.dynamic_index_in_dim(grouped, my_part, 1, keepdims=False).reshape(-1, HD)
        block_size = query_block(queries.shape[0], row_count)
        outputs.append(
            attend(queries, key_recv[:, slot_index], value_recv[:, slot_index], key_ok, block_size)
        )
    attended = jnp.stack(outputs, axis=1)
    spread_out = attended.reshape(shard_count // repeat_count, 1, row_count, per_device, HD)
    selector = (
        (jnp.arange(repeat_count) == my_part).astype(jnp.bfloat16).reshape(1, repeat_count, 1, 1, 1)
    )
    send_back = (spread_out * selector).reshape(shard_count * row_count, per_device, HD)
    returned = lax.all_to_all(send_back, "seq", split_axis=0, concat_axis=1, tiled=True)
    own_heads = lax.dynamic_index_in_dim(
        returned.reshape(row_count, repeat_count, pair_count, HD),
        my_shard % repeat_count,
        1,
        keepdims=False,
    )
    per_job = jnp.transpose(
        own_heads.reshape(row_count, job_count, group_size * HD), (1, 0, 2)
    ).reshape(job_count * row_count, group_size * HD)
    out_weight = w_out.reshape(group_size * HD, w_out.shape[2])
    projected = lax.psum_scatter(
        jnp.dot(per_job, out_weight, preferred_element_type=jnp.float32).astype(jnp.bfloat16),
        "job",
        scatter_dimension=0,
        tiled=True,
    ).astype(jnp.float32)
    own_rows = jnp.concatenate(
        [video[0], lax.dynamic_index_in_dim(text_full, my_job, 0, keepdims=False)], axis=0
    )
    gate_row = lax.dynamic_index_in_dim(mod_gate, my_job, 0, keepdims=False)
    result = (own_rows.astype(jnp.float32) + gate_row * projected).astype(jnp.bfloat16)
    own_valid = lax.dynamic_index_in_dim(slot_valid, my_job, 0, keepdims=False)
    text_result = jnp.where(
        own_valid[:, None], result[video_rows:], jnp.zeros_like(result[video_rows:])
    )
    return (result[:video_rows][None], text_result[None])


def vmem_spec():
    return pl.BlockSpec(memory_space=pltpu.VMEM)


def smem_spec():
    return pl.BlockSpec(memory_space=pltpu.SMEM)


def hbm_spec():
    return pl.BlockSpec(memory_space=pltpu.HBM)


def params(mib):
    return pltpu.CompilerParams(vmem_limit_bytes=mib << 20)


def cost(flops, moved, exps=0):
    return pl.CostEstimate(flops=int(flops), bytes_accessed=int(moved), transcendentals=int(exps))


def norm_kernel(rows_ref, gain_ref, out_ref):
    out_ref[...] = rms_scale(rows_ref[0].astype(jnp.float32), gain_ref[...]).astype(jnp.bfloat16)


def norm_text(rows, gain):
    return pl.pallas_call(
        norm_kernel,
        out_shape=jax.ShapeDtypeStruct(rows.shape[1:], jnp.bfloat16),
        in_specs=[vmem_spec(), vmem_spec()],
        out_specs=vmem_spec(),
        compiler_params=params(8),
        cost_estimate=cost(4 * rows.size, 4 * rows.size),
    )(rows, gain[None])


def table_row(ref, index):
    return ref[pl.ds(index, 1)]


def project_heads_into(out_ref, x_ref, w_ref, qg_ref, kg_ref, place):
    heads = w_ref.shape[1]
    for first in range(0, heads, 2):
        pair = range(first, first + 2)
        weights = jnp.concatenate([w_ref[c, h] for h in pair for c in range(3)], axis=1)
        raw = jnp.dot(x_ref[...], weights, preferred_element_type=jnp.float32)
        for i, h in enumerate(pair):
            lo = 3 * HD * i
            queries = rms_scale(raw[:, lo : lo + HD], qg_ref[h : h + 1]).astype(jnp.bfloat16)
            keys = rms_scale(raw[:, lo + HD : lo + 2 * HD], kg_ref[h : h + 1]).astype(jnp.bfloat16)
            values = raw[:, lo + 2 * HD : lo + 3 * HD].astype(jnp.bfloat16)
            for lo_row, count, r, to in place:
                for c, part in enumerate((queries, keys, values)):
                    out_ref[r, h, to : to + count, c * HD : (c + 1) * HD] = part[
                        lo_row : lo_row + count
                    ]


def local_kernel(a_ref, b_ref, shift_ref, scale_ref, w_ref, qg_ref, kg_ref, out_ref, x_ref):
    rows = a_ref.shape[0]
    mine = lax.axis_index("job")
    for r, ref in enumerate((a_ref, b_ref)):
        x_ref[r * rows : (r + 1) * rows] = modulate(
            ref[...], table_row(shift_ref, mine ^ r), table_row(scale_ref, mine ^ r)
        )
    place = [(r * rows, rows, r, 0) for r in range(2)]
    project_heads_into(out_ref, x_ref, w_ref, qg_ref, kg_ref, place)


def remote_kernel(
    holder_ref, a_ref, b_ref, t0_ref, t1_ref, t2_ref, t3_ref, shift_ref, scale_ref, w_ref,
    qg_ref, kg_ref, out_ref, x_ref, text_ref,
):
    rows = a_ref.shape[0]
    jobs, trows, width = t0_ref.shape
    mine = lax.axis_index("job")
    for b in range(jobs):
        for q, part in enumerate((t0_ref, t1_ref, t2_ref, t3_ref)):

            @pl.when(mine ^ b == q)
            def _():
                for r in range(jobs):
                    text_ref[r * trows : (r + 1) * trows, b * width : (b + 1) * width] = part[
                        holder_ref[mine ^ r] ^ b
                    ]

    for r, ref in enumerate((a_ref, b_ref)):
        x_ref[r * rows : (r + 1) * rows] = modulate(
            ref[...], table_row(shift_ref, mine ^ (2 + r)), table_row(scale_ref, mine ^ (2 + r))
        )
    for r in range(jobs):
        lo = 2 * rows + r * trows
        x_ref[lo : lo + trows] = modulate(
            text_ref[r * trows : (r + 1) * trows],
            table_row(shift_ref, mine ^ r),
            table_row(scale_ref, mine ^ r),
        )
    place = [(r * rows, rows, r, 0) for r in range(2)]
    place += [
        (2 * rows + r * trows, trows, r % 2, rows + (r // 2) * trows) for r in range(jobs)
    ]
    project_heads_into(out_ref, x_ref, w_ref, qg_ref, kg_ref, place)
    for r in range(2):
        for h in range(w_ref.shape[1]):
            lo = (r * w_ref.shape[1] + h) * 3 * HD
            out_ref[r, h, rows + 2 * trows :] = text_ref[0:trows, lo : lo + 3 * HD]


def qkv_call(kernel, inputs, specs, rows_in, rows_out, extra, weights, q_gain, k_gain):
    group, width = weights.shape[1:3]
    return pl.pallas_call(
        kernel,
        out_shape=jax.ShapeDtypeStruct((2, group, rows_out, 3 * HD), jnp.bfloat16),
        in_specs=specs + [vmem_spec()] * 3,
        out_specs=vmem_spec(),
        scratch_shapes=[pltpu.VMEM((rows_in, width), jnp.bfloat16), *extra],
        compiler_params=params(16),
        cost_estimate=cost(2 * rows_in * weights.size, 2 * weights.size + 4 * rows_in * width),
    )(*inputs, weights, q_gain, k_gain)


def qkv_local(own, core, shift, scale, weights, q_gain, k_gain):
    rows = own.shape[0]
    return qkv_call(
        local_kernel, (own, core, shift, scale), [vmem_spec()] * 4, 2 * rows, rows, [],
        weights, q_gain, k_gain,
    )


def qkv_remote(holder, pair, parts, shift, scale, weights, q_gain, k_gain):
    rows, width = pair[0].shape
    jobs, trows, _ = parts[0].shape
    return qkv_call(
        remote_kernel, (holder, *pair, *parts, shift, scale), [smem_spec()] + [vmem_spec()] * 8,
        2 * rows + jobs * trows, rows + 3 * trows,
        [pltpu.VMEM((jobs * trows, width), jnp.bfloat16)], weights, q_gain, k_gain,
    )


def choose_slots(count_ref, splits_ref, job, table, put):
    shards = splits_ref.shape[1]
    slots = 2 * table.shape[0] // shards
    slot = lax.broadcasted_iota(jnp.int32, (slots, table.shape[0]), 0)
    row = lax.broadcasted_iota(jnp.int32, (slots, table.shape[0]), 1)
    offset = jnp.int32(0)
    for s in range(shards):
        chosen = (row == slot + offset) & (slot < splits_ref[job, s]) & (row < count_ref[job])
        chosen = jnp.where(chosen, 1.0, 0.0).astype(jnp.bfloat16)
        put(s, jnp.dot(chosen, table, preferred_element_type=jnp.float32).astype(jnp.bfloat16))
        offset = offset + splits_ref[job, s]


def attention_kernel(
    far, text_base, count_ref, splits_ref, video_hbm, text_hbm, *refs
):
    out_hbm, v_refs, t_refs, mixed_ref, out_ref, sems = refs[0], refs[1:4], refs[4:7], *refs[7:10]
    col_ref = None if far else refs[10]
    shards, vrows, _ = v_refs[0].shape
    trows = t_refs[0].shape[1]
    copies = []
    for c in range(3):
        cols = pl.ds(c * HD, HD)
        copies.append(
            pltpu.make_async_copy(
                video_hbm.at[:, pl.ds(0, vrows), cols], v_refs[c], sems.at[c]
            )
        )
        copies.append(
            pltpu.make_async_copy(
                text_hbm.at[:, pl.ds(text_base, trows), cols], t_refs[c], sems.at[3 + c]
            )
        )
    if not far:
        copies.append(
            pltpu.make_async_copy(
                text_hbm.at[:, pl.ds(vrows + 2 * trows, trows)], col_ref, sems.at[6]
            )
        )
    for copy in copies:
        copy.start()
    for copy in copies:
        copy.wait()
    mine = lax.axis_index("job")
    half = lax.axis_index("seq") // (shards // 2)
    job = mine ^ half ^ (2 if far else 0)
    column = lax.broadcasted_iota(jnp.int32, (1, shards * trows), 1)
    key_ok = column < count_ref[job]
    scale = HD ** (-0.5)
    video_keys = v_refs[1][...].reshape(shards * vrows, HD)
    text_keys = t_refs[1][...].reshape(shards * trows, HD)
    video_values = v_refs[2][...].reshape(shards * vrows, HD)
    text_values = t_refs[2][...].reshape(shards * trows, HD)

    def product(a, b):
        return lax.dot_general(a, b, (((1,), (1,)), ((), ())), preferred_element_type=jnp.float32)

    def one_block(queries):
        video_scores = product(queries, video_keys)
        text_scores = jnp.where(key_ok, product(queries, text_keys), -1e30)
        highest = jnp.maximum(
            jnp.max(video_scores, axis=-1, keepdims=True),
            jnp.max(text_scores, axis=-1, keepdims=True),
        )
        video_w = jnp.exp((video_scores - highest) * scale)
        text_w = jnp.exp((text_scores - highest) * scale)
        summed = jnp.sum(video_w, axis=-1, keepdims=True) + jnp.sum(text_w, axis=-1, keepdims=True)
        mixed = jnp.dot(
            video_w.astype(jnp.bfloat16), video_values, preferred_element_type=jnp.float32
        ) + jnp.dot(text_w.astype(jnp.bfloat16), text_values, preferred_element_type=jnp.float32)
        return (mixed / summed).astype(jnp.bfloat16)

    mixed_ref[...] = one_block(t_refs[0][...].reshape(shards * trows, HD))
    rows = vrows + 2 * trows
    sends = [
        pltpu.make_async_copy(out_ref.at[s], out_hbm.at[s], sems.at[7 + s]) for s in range(shards)
    ]

    def put(s, chosen):
        out_ref[s, vrows:rows] = chosen

    choose_slots(count_ref, splits_ref, job, mixed_ref[...], put)
    if not far:

        def put_columns(s, chosen):
            for c in range(3):
                lo = rows + 2 * trows * c
                out_ref[s, lo : lo + 2 * trows] = chosen[:, c * HD : (c + 1) * HD]

        choose_slots(
            count_ref, splits_ref, mine, col_ref[...].reshape(shards * trows, 3 * HD), put_columns
        )
    for i in range(0, shards, 2):
        done = one_block(v_refs[0][i : i + 2].reshape(2 * vrows, HD))
        out_ref[i, 0:vrows] = done[:vrows]
        out_ref[i + 1, 0:vrows] = done[vrows:]
        sends[i].start()
        sends[i + 1].start()
    for send in sends:
        send.wait()


def attend_pair(far, count, splits, video_qkv, text_qkv, vrows, trows):
    shards = video_qkv.shape[0]
    slots = 2 * trows
    total = shards * (vrows + trows)
    rows_out = vrows + slots * (1 if far else 4)
    scratch = [pltpu.VMEM((shards, vrows, HD), jnp.bfloat16)] * 3
    scratch += [pltpu.VMEM((shards, trows, HD), jnp.bfloat16)] * 3
    scratch += [pltpu.VMEM((shards * trows, HD), jnp.bfloat16)]
    scratch += [pltpu.VMEM((shards, rows_out, HD), jnp.bfloat16)]
    scratch += [pltpu.SemaphoreType.DMA((7 + shards,))]
    if not far:
        scratch += [pltpu.VMEM((shards, trows, 3 * HD), jnp.bfloat16)]
    return pl.pallas_call(
        functools.partial(attention_kernel, far, vrows + (trows if far else 0)),
        out_shape=pltpu.HBM((shards, rows_out, HD), jnp.bfloat16),
        in_specs=[smem_spec(), smem_spec(), hbm_spec(), hbm_spec()],
        out_specs=hbm_spec(),
        scratch_shapes=scratch,
        compiler_params=params(12),
        cost_estimate=cost(4 * total * total * HD, 3 << 20, total * total),
    )(count, splits, video_qkv, text_qkv)


def out_kernel(which, with_slots, added, *refs):
    heads_ref, w_ref, out_ref = refs[0], refs[1], refs[2 + added]
    group = w_ref.shape[0] // HD
    count, width = out_ref.shape
    rows = jnp.concatenate([heads_ref[which * group + h, 0:count] for h in range(group)], axis=1)
    for lo in range(0, width, width // 4):
        cols = slice(lo, lo + width // 4)
        total = jnp.dot(rows, w_ref[:, cols], preferred_element_type=jnp.float32)
        if added:
            total = total + refs[2][:, cols].astype(jnp.float32)
        out_ref[:, cols] = total.astype(jnp.bfloat16)
    if with_slots:
        slot_ref = refs[3 + added]
        slots = slot_ref.shape[0]
        for block in range(width // HD):
            lo = count + (block % 3) * slots
            slot_ref[:, block * HD : (block + 1) * HD] = heads_ref[block // 3, lo : lo + slots]


def project_out(heads, rows, which, weights, *added, slots=0):
    depth, width = weights.shape
    out = jax.ShapeDtypeStruct((rows, width), jnp.bfloat16)
    slot_out = jax.ShapeDtypeStruct((slots, width), jnp.bfloat16)
    return pl.pallas_call(
        functools.partial(out_kernel, which, slots > 0, len(added)),
        out_shape=(out, slot_out) if slots else out,
        in_specs=[vmem_spec()] * (2 + len(added)),
        out_specs=(vmem_spec(), vmem_spec()) if slots else vmem_spec(),
        compiler_params=params(8),
        cost_estimate=cost(2 * rows * depth * width, 2 * (depth + 2 * rows) * width),
    )(heads, weights, *added)


def final_kernel(
    count_ref, splits_ref, video_ref, part_ref, chip_hbm, gate_ref, slot_ref, vout_hbm, tout_hbm,
    chip_ref, out_ref, in_sems, out_sems,
):
    vrows, step = video_ref.shape[1], slot_ref.shape[0]
    total_rows = part_ref.shape[0]
    reads, writes = [], []
    for i, lo in enumerate(range(0, total_rows, step)):
        rows = pl.ds(lo, step)
        reads.append(pltpu.make_async_copy(chip_hbm.at[rows], chip_ref.at[rows], in_sems.at[i]))
        target = vout_hbm.at[0, rows] if lo < vrows else tout_hbm.at[0]
        writes.append(pltpu.make_async_copy(out_ref.at[rows], target, out_sems.at[i]))
    for read in reads:
        read.start()
    job, shard = lax.axis_index("job"), lax.axis_index("seq")
    gate = table_row(gate_ref, job)
    offset = jnp.int32(0)
    for s in range(splits_ref.shape[1]):
        offset = offset + jnp.where(s < shard, splits_ref[job, s], 0)
    slot = lax.broadcasted_iota(jnp.int32, (step, 1), 0)
    valid = (slot < splits_ref[job, shard]) & (slot + offset < count_ref[job])
    for i, lo in enumerate(range(0, total_rows, step)):
        reads[i].wait()
        rows = slice(lo, lo + step)
        total = part_ref[rows].astype(jnp.float32) + chip_ref[rows].astype(jnp.float32)
        base = video_ref[0, rows] if lo < vrows else slot_ref[...]
        result = base.astype(jnp.float32) + gate * total
        if lo >= vrows:
            result = jnp.where(valid, result, 0.0)
        out_ref[rows] = result.astype(jnp.bfloat16)
        writes[i].start()
    for write in writes:
        write.wait()


def finish(count, splits, video, part, from_chip, gate, slot_rows):
    rows, width = part.shape
    steps = rows // slot_rows.shape[0]
    vrows = video.shape[1]
    return pl.pallas_call(
        final_kernel,
        out_shape=(
            jax.ShapeDtypeStruct((1, vrows, width), jnp.bfloat16),
            jax.ShapeDtypeStruct((1, rows - vrows, width), jnp.bfloat16),
        ),
        in_specs=[
            smem_spec(), smem_spec(), vmem_spec(), vmem_spec(), hbm_spec(), vmem_spec(), vmem_spec(),
        ],
        out_specs=(hbm_spec(), hbm_spec()),
        scratch_shapes=[
            pltpu.VMEM((rows, width), jnp.bfloat16),
            pltpu.VMEM((rows, width), jnp.bfloat16),
            pltpu.SemaphoreType.DMA((steps,)),
            pltpu.SemaphoreType.DMA((steps,)),
        ],
        compiler_params=params(8),
        cost_estimate=cost(6 * rows * width, 10 * rows * width),
    )(count, splits, video, part, from_chip, gate, slot_rows)


def two_wave_body(
    video,
    text_cache,
    text_count,
    holder,
    text_splits,
    mod_shift,
    mod_scale,
    mod_gate,
    text_gain,
    refine_w,
    refine_bias,
    w_qkv,
    q_gain,
    k_gain,
    w_out,
):
    job_count = lax.axis_size("job")
    shard_count = lax.axis_size("seq")
    group_size = w_qkv.shape[1]
    trows = text_cache.shape[1]
    vrows = video.shape[1]

    def to_core(x):
        return lax.ppermute(x, "job", [(i, i ^ 1) for i in range(job_count)])

    def to_chip(x):
        return lax.ppermute(x, "job", [(i, i ^ 2) for i in range(job_count)])

    def over_seq(x):
        return lax.all_to_all(x, "seq", split_axis=0, concat_axis=0, tiled=False)

    def after(x, earlier):
        return lax.optimization_barrier((x, earlier))[0]

    qkv_w = jnp.transpose(w_qkv, (2, 1, 0, 3))
    own_video = video[0]
    core_video = to_core(own_video)

    normed = norm_text(text_cache, text_gain)
    normed_core = to_core(normed)
    normed_chip = to_chip(normed)
    chip_video = to_chip(after(own_video, normed))
    local_send = qkv_local(own_video, core_video, mod_shift, mod_scale, qkv_w, q_gain, k_gain)
    local_qkv = over_seq(local_send.reshape(shard_count, vrows, 3 * HD))
    normed_core, normed_chip = after((normed_core, normed_chip), local_send)
    normed_both = to_core(normed_chip)
    lifted = jnp.dot(
        jnp.concatenate([normed, normed_core, normed_chip, normed_both], axis=0),
        refine_w,
        preferred_element_type=jnp.float32,
    )
    refined = (lifted + refine_bias).astype(jnp.bfloat16).reshape(job_count, trows, -1)
    refined_core = to_core(refined)
    refined_chip = to_chip(refined)
    refined_both = to_core(refined_chip)

    chip_video = after(chip_video, refined)
    both_video = to_core(chip_video)
    send = qkv_remote(
        holder,
        (chip_video, both_video),
        (refined, refined_core, refined_chip, refined_both),
        mod_shift,
        mod_scale,
        qkv_w,
        q_gain,
        k_gain,
    )
    second = over_seq(after(send.reshape(shard_count, -1, 3 * HD), local_qkv))

    remote_mixed = attend_pair(True, text_count, text_splits, second, second, vrows, trows)
    remote_back = over_seq(remote_mixed)
    local_mixed = attend_pair(
        False, text_count, text_splits, after(local_qkv, remote_mixed), second, vrows, trows
    )
    out_weight = w_out.reshape(group_size * HD, w_out.shape[2])
    rows = vrows + 2 * trows
    remote_back = after(remote_back, local_mixed)
    local_back = over_seq(after(local_mixed, remote_back))
    from_core = to_core(project_out(remote_back, rows, 1, out_weight))
    crossing = project_out(remote_back, rows, 0, out_weight, from_core)
    from_chip = to_chip(crossing)
    local_back = after(local_back, from_chip)
    near_part, slot_rows = project_out(local_back, rows, 1, out_weight, slots=2 * trows)
    local_part = project_out(local_back, rows, 0, out_weight, to_core(near_part))
    return finish(
        text_count, text_splits, video, local_part, from_chip, mod_gate, slot_rows
    )


def body(*arrays):
    video, text_cache, w_qkv = arrays[0], arrays[1], arrays[11]
    job_count = lax.axis_size("job")
    shard_count = lax.axis_size("seq")
    fits = (
        job_count == 4
        and shard_count == 2 * w_qkv.shape[1]
        and video.shape[1] == 128
        and text_cache.shape[1] == 32
    )
    return (two_wave_body if fits else general_body)(*arrays)


def solution(mesh):
    placed = (
        P("job", "seq", None),
        P("job", "seq", None),
        P(),
        P(),
        P(),
        P(),
        P(),
        P(),
        P(),
        P(None, "job"),
        P("job"),
        P(None, "job", None, None),
        P("job", None),
        P("job", None),
        P("job", None, None),
    )
    return jax.shard_map(
        body,
        mesh=mesh,
        in_specs=placed,
        out_specs=(P("job", "seq", None), P("job", "seq", None)),
        check_vma=False,
    )
```

```python
import functools

import jax
import jax.numpy as jnp
from jax import lax
from jax.experimental import pallas as pl
from jax.experimental.pallas import tpu as pltpu
from jax.sharding import PartitionSpec as P

HD = 128
TXT = 256


epsilon = 1e-06


def rms_scale(values, gains):
    mean_square = jnp.mean(values * values, axis=-1, keepdims=True)
    return values * lax.rsqrt(mean_square + epsilon) * gains


def modulate(tokens, shift_part, scale_part):
    widened = tokens.astype(jnp.float32)
    centre = jnp.mean(widened, axis=-1, keepdims=True)
    spread_sq = jnp.mean((widened - centre) ** 2, axis=-1, keepdims=True)
    normed = (widened - centre) * lax.rsqrt(spread_sq + epsilon)
    return (normed * (1.0 + scale_part) + shift_part).astype(jnp.bfloat16)


def refine_rows(raw_text, text_gain, refine_w, refine_bias):
    normed = rms_scale(raw_text.astype(jnp.float32), text_gain).astype(jnp.bfloat16)
    lifted = jnp.einsum("jrt,tc->jrc", normed, refine_w, preferred_element_type=jnp.float32)
    return (lifted + refine_bias).astype(jnp.bfloat16)


def project_heads(modded, w_qkv, q_gain, k_gain):
    projections = jnp.einsum("jrd,dhce->jrhce", modded, w_qkv, preferred_element_type=jnp.float32)
    queries = rms_scale(projections[:, :, :, 0], q_gain).astype(jnp.bfloat16)
    key_rows = rms_scale(projections[:, :, :, 1], k_gain).astype(jnp.bfloat16)
    values = projections[:, :, :, 2].astype(jnp.bfloat16)
    return jnp.stack([queries, key_rows, values], axis=3)


def query_block(query_count, unit_rows):
    unit_total = query_count // unit_rows
    for factor in range(1, unit_total + 1):
        if unit_total % factor == 0 and factor * unit_rows >= 512:
            return factor * unit_rows
    return query_count


def attend(queries, key_rows, values, key_ok, block_rows):
    query_count = queries.shape[0]
    stacked_blocks = queries.reshape(query_count // block_rows, block_rows, queries.shape[1])
    scale_factor = HD ** (-0.5)

    def one_block(query_part):
        scores = (
            jnp.einsum("qe,ke->qk", query_part, key_rows, preferred_element_type=jnp.float32)
            * scale_factor
        )
        scores = jnp.where(key_ok[None, :], scores, -1e30)
        highest = jnp.max(scores, axis=-1, keepdims=True)
        weights = jnp.exp(scores - highest)
        summed = jnp.sum(weights, axis=-1, keepdims=True)
        weights = (weights / summed).astype(jnp.bfloat16)
        return jnp.dot(weights, values, preferred_element_type=jnp.float32).astype(jnp.bfloat16)

    return lax.map(one_block, stacked_blocks).reshape(query_count, queries.shape[1])


def general_body(
    video,
    text_cache,
    text_count,
    holder,
    text_splits,
    mod_shift,
    mod_scale,
    mod_gate,
    text_gain,
    refine_w,
    refine_bias,
    w_qkv,
    q_gain,
    k_gain,
    w_out,
):
    job_count = lax.axis_size("job")
    shard_count = lax.axis_size("seq")
    my_job = lax.axis_index("job")
    my_shard = lax.axis_index("seq")
    video_rows = video.shape[1]
    block_rows = text_cache.shape[1]
    slot_count = 2 * block_rows
    row_count = video_rows + slot_count
    group_size = w_qkv.shape[1]
    pair_count = job_count * group_size
    slot_total = max(pair_count, shard_count)
    repeat_count = slot_total // pair_count
    per_device = slot_total // shard_count
    offsets = jnp.cumsum(text_splits, axis=1) - text_splits
    slot_ids = jnp.arange(slot_count, dtype=jnp.int32)
    my_offsets = lax.dynamic_index_in_dim(offsets, my_shard, 1, keepdims=False)
    my_splits = lax.dynamic_index_in_dim(text_splits, my_shard, 1, keepdims=False)
    slot_valid = (slot_ids[None, :] < my_splits[:, None]) & (
        my_offsets[:, None] + slot_ids[None, :] < text_count[:, None]
    )
    position = holder[:, None] * (TXT + slot_count) + my_offsets[:, None] + slot_ids[None, :]
    cache_rows = lax.all_gather(text_cache, "job", axis=0, tiled=True)
    refined = refine_rows(cache_rows, text_gain, refine_w, refine_bias)
    gathered_text = lax.all_gather(refined, "seq", axis=1, tiled=True)
    width = gathered_text.shape[2]
    padded = jnp.concatenate(
        [
            gathered_text,
            jnp.zeros((gathered_text.shape[0], slot_count, width), gathered_text.dtype),
        ],
        axis=1,
    )
    flat_rows = padded.reshape(-1, width)
    chosen = jnp.take(flat_rows, position.reshape(-1), axis=0).reshape(job_count, slot_count, width)
    text_cols = jnp.where(slot_valid[:, :, None], chosen, jnp.zeros_like(chosen))
    text_full = lax.all_gather(text_cols, "job", axis=2, tiled=True)
    modded = modulate(
        lax.all_gather(video, "job", axis=0, tiled=True),
        mod_shift[:, None, :],
        mod_scale[:, None, :],
    )
    video_heads = project_heads(modded, w_qkv, q_gain, k_gain)
    text_modded = modulate(text_full, mod_shift[:, None, :], mod_scale[:, None, :])
    text_heads = project_heads(text_modded, w_qkv, q_gain, k_gain)
    heads_all = jnp.concatenate([video_heads, text_heads], axis=1)
    by_row = jnp.transpose(heads_all, (1, 0, 2, 3, 4)).reshape(row_count, pair_count, 3, HD)
    query_rows = by_row[:, :, 0]
    key_rows = jnp.tile(by_row[:, :, 1], (1, repeat_count, 1))
    value_rows = jnp.tile(by_row[:, :, 2], (1, repeat_count, 1))
    query_send = jnp.tile(query_rows, (1, repeat_count, 1))
    query_recv, key_recv, value_recv = (
        lax.all_to_all(query_send, "seq", split_axis=1, concat_axis=0, tiled=True),
        lax.all_to_all(key_rows, "seq", split_axis=1, concat_axis=0, tiled=True),
        lax.all_to_all(value_rows, "seq", split_axis=1, concat_axis=0, tiled=True),
    )
    my_part = my_shard * per_device // pair_count
    outputs = []
    for slot_index in range(per_device):
        slot_global = my_shard * per_device + slot_index
        job_of_slot = slot_global % pair_count // group_size
        splits_row = lax.dynamic_index_in_dim(text_splits, job_of_slot, 0, keepdims=False)
        offsets_row = lax.dynamic_index_in_dim(offsets, job_of_slot, 0, keepdims=False)
        count_of_job = lax.dynamic_index_in_dim(text_count, job_of_slot, 0, keepdims=False)
        key_valid = (slot_ids[None, :] < splits_row[:, None]) & (
            offsets_row[:, None] + slot_ids[None, :] < count_of_job
        )
        key_ok = jnp.concatenate(
            [jnp.ones((shard_count, video_rows), jnp.bool_), key_valid], axis=1
        ).reshape(-1)
        grouped = query_recv[:, slot_index].reshape(
            shard_count // repeat_count, repeat_count, row_count, HD
        )
        queries = lax.dynamic_index_in_dim(grouped, my_part, 1, keepdims=False).reshape(-1, HD)
        block_size = query_block(queries.shape[0], row_count)
        outputs.append(
            attend(queries, key_recv[:, slot_index], value_recv[:, slot_index], key_ok, block_size)
        )
    attended = jnp.stack(outputs, axis=1)
    spread_out = attended.reshape(shard_count // repeat_count, 1, row_count, per_device, HD)
    selector = (
        (jnp.arange(repeat_count) == my_part).astype(jnp.bfloat16).reshape(1, repeat_count, 1, 1, 1)
    )
    send_back = (spread_out * selector).reshape(shard_count * row_count, per_device, HD)
    returned = lax.all_to_all(send_back, "seq", split_axis=0, concat_axis=1, tiled=True)
    own_heads = lax.dynamic_index_in_dim(
        returned.reshape(row_count, repeat_count, pair_count, HD),
        my_shard % repeat_count,
        1,
        keepdims=False,
    )
    per_job = jnp.transpose(
        own_heads.reshape(row_count, job_count, group_size * HD), (1, 0, 2)
    ).reshape(job_count * row_count, group_size * HD)
    out_weight = w_out.reshape(group_size * HD, w_out.shape[2])
    projected = lax.psum_scatter(
        jnp.dot(per_job, out_weight, preferred_element_type=jnp.float32).astype(jnp.bfloat16),
        "job",
        scatter_dimension=0,
        tiled=True,
    ).astype(jnp.float32)
    own_rows = jnp.concatenate(
        [video[0], lax.dynamic_index_in_dim(text_full, my_job, 0, keepdims=False)], axis=0
    )
    gate_row = lax.dynamic_index_in_dim(mod_gate, my_job, 0, keepdims=False)
    result = (own_rows.astype(jnp.float32) + gate_row * projected).astype(jnp.bfloat16)
    own_valid = lax.dynamic_index_in_dim(slot_valid, my_job, 0, keepdims=False)
    text_result = jnp.where(
        own_valid[:, None], result[video_rows:], jnp.zeros_like(result[video_rows:])
    )
    return (result[:video_rows][None], text_result[None])


def vmem_spec():
    return pl.BlockSpec(memory_space=pltpu.VMEM)


def smem_spec():
    return pl.BlockSpec(memory_space=pltpu.SMEM)


def hbm_spec():
    return pl.BlockSpec(memory_space=pltpu.HBM)


def params(mib):
    return pltpu.CompilerParams(vmem_limit_bytes=mib << 20)


def cost(flops, moved, exps=0):
    return pl.CostEstimate(flops=int(flops), bytes_accessed=int(moved), transcendentals=int(exps))


def norm_kernel(rows_ref, gain_ref, out_ref):
    out_ref[...] = rms_scale(rows_ref[0].astype(jnp.float32), gain_ref[...]).astype(jnp.bfloat16)


def norm_text(rows, gain):
    return pl.pallas_call(
        norm_kernel,
        out_shape=jax.ShapeDtypeStruct(rows.shape[1:], jnp.bfloat16),
        in_specs=[vmem_spec(), vmem_spec()],
        out_specs=vmem_spec(),
        compiler_params=params(8),
        cost_estimate=cost(4 * rows.size, 4 * rows.size),
    )(rows, gain[None])


def table_row(ref, index):
    return ref[pl.ds(index, 1)]


def project_heads_into(out_ref, x_ref, w_ref, qg_ref, kg_ref, place):
    heads = w_ref.shape[1]
    for first in range(0, heads, 2):
        pair = range(first, first + 2)
        weights = jnp.concatenate([w_ref[c, h] for h in pair for c in range(3)], axis=1)
        raw = jnp.dot(x_ref[...], weights, preferred_element_type=jnp.float32)
        for i, h in enumerate(pair):
            lo = 3 * HD * i
            queries = rms_scale(raw[:, lo : lo + HD], qg_ref[h : h + 1]).astype(jnp.bfloat16)
            keys = rms_scale(raw[:, lo + HD : lo + 2 * HD], kg_ref[h : h + 1]).astype(jnp.bfloat16)
            values = raw[:, lo + 2 * HD : lo + 3 * HD].astype(jnp.bfloat16)
            for lo_row, count, r, to in place:
                for c, part in enumerate((queries, keys, values)):
                    out_ref[r, h, to : to + count, c * HD : (c + 1) * HD] = part[
                        lo_row : lo_row + count
                    ]


def local_kernel(a_ref, b_ref, shift_ref, scale_ref, w_ref, qg_ref, kg_ref, out_ref, x_ref):
    rows = a_ref.shape[0]
    mine = lax.axis_index("job")
    for r, ref in enumerate((a_ref, b_ref)):
        x_ref[r * rows : (r + 1) * rows] = modulate(
            ref[...], table_row(shift_ref, mine ^ r), table_row(scale_ref, mine ^ r)
        )
    place = [(r * rows, rows, r, 0) for r in range(2)]
    project_heads_into(out_ref, x_ref, w_ref, qg_ref, kg_ref, place)


def remote_kernel(
    holder_ref, a_ref, b_ref, t0_ref, t1_ref, t2_ref, t3_ref, shift_ref, scale_ref, w_ref,
    qg_ref, kg_ref, out_ref, x_ref, text_ref,
):
    rows = a_ref.shape[0]
    jobs, trows, width = t0_ref.shape
    mine = lax.axis_index("job")
    for b in range(jobs):
        for q, part in enumerate((t0_ref, t1_ref, t2_ref, t3_ref)):

            @pl.when(mine ^ b == q)
            def _():
                for r in range(jobs):
                    text_ref[r * trows : (r + 1) * trows, b * width : (b + 1) * width] = part[
                        holder_ref[mine ^ r] ^ b
                    ]

    for r, ref in enumerate((a_ref, b_ref)):
        x_ref[r * rows : (r + 1) * rows] = modulate(
            ref[...], table_row(shift_ref, mine ^ (2 + r)), table_row(scale_ref, mine ^ (2 + r))
        )
    for r in range(jobs):
        lo = 2 * rows + r * trows
        x_ref[lo : lo + trows] = modulate(
            text_ref[r * trows : (r + 1) * trows],
            table_row(shift_ref, mine ^ r),
            table_row(scale_ref, mine ^ r),
        )
    place = [(r * rows, rows, r, 0) for r in range(2)]
    place += [
        (2 * rows + r * trows, trows, r % 2, rows + (r // 2) * trows) for r in range(jobs)
    ]
    project_heads_into(out_ref, x_ref, w_ref, qg_ref, kg_ref, place)
    for r in range(2):
        for h in range(w_ref.shape[1]):
            lo = (r * w_ref.shape[1] + h) * 3 * HD
            out_ref[r, h, rows + 2 * trows :] = text_ref[0:trows, lo : lo + 3 * HD]


def qkv_call(kernel, inputs, specs, rows_in, rows_out, extra, weights, q_gain, k_gain):
    group, width = weights.shape[1:3]
    return pl.pallas_call(
        kernel,
        out_shape=pltpu.HBM((2, group, rows_out, 3 * HD), jnp.bfloat16),
        in_specs=specs + [vmem_spec()] * 3,
        out_specs=vmem_spec(),
        scratch_shapes=[pltpu.VMEM((rows_in, width), jnp.bfloat16), *extra],
        compiler_params=params(16),
        cost_estimate=cost(2 * rows_in * weights.size, 2 * weights.size + 4 * rows_in * width),
    )(*inputs, weights, q_gain, k_gain)


def qkv_local(own, core, shift, scale, weights, q_gain, k_gain):
    rows = own.shape[0]
    return qkv_call(
        local_kernel, (own, core, shift, scale), [vmem_spec()] * 4, 2 * rows, rows, [],
        weights, q_gain, k_gain,
    )


def qkv_remote(holder, pair, parts, shift, scale, weights, q_gain, k_gain):
    rows, width = pair[0].shape
    jobs, trows, _ = parts[0].shape
    return qkv_call(
        remote_kernel, (holder, *pair, *parts, shift, scale), [smem_spec()] + [vmem_spec()] * 8,
        2 * rows + jobs * trows, rows + 3 * trows,
        [pltpu.VMEM((jobs * trows, width), jnp.bfloat16)], weights, q_gain, k_gain,
    )


def choose_slots(count_ref, splits_ref, job, table, put):
    shards = splits_ref.shape[1]
    slots = 2 * table.shape[0] // shards
    slot = lax.broadcasted_iota(jnp.int32, (slots, table.shape[0]), 0)
    row = lax.broadcasted_iota(jnp.int32, (slots, table.shape[0]), 1)
    offset = jnp.int32(0)
    for s in range(shards):
        chosen = (row == slot + offset) & (slot < splits_ref[job, s]) & (row < count_ref[job])
        chosen = jnp.where(chosen, 1.0, 0.0).astype(jnp.bfloat16)
        put(s, jnp.dot(chosen, table, preferred_element_type=jnp.float32).astype(jnp.bfloat16))
        offset = offset + splits_ref[job, s]


def attention_kernel(
    far, text_base, count_ref, splits_ref, video_hbm, text_hbm, *refs
):
    out_hbm, v_refs, t_refs, mixed_ref, out_ref, sems = refs[0], refs[1:4], refs[4:7], *refs[7:10]
    col_ref = None if far else refs[10]
    shards, vrows, _ = v_refs[0].shape
    trows = t_refs[0].shape[1]
    copies = []
    for c in range(3):
        cols = pl.ds(c * HD, HD)
        copies.append(
            pltpu.make_async_copy(
                video_hbm.at[:, pl.ds(0, vrows), cols], v_refs[c], sems.at[c]
            )
        )
        copies.append(
            pltpu.make_async_copy(
                text_hbm.at[:, pl.ds(text_base, trows), cols], t_refs[c], sems.at[3 + c]
            )
        )
    if not far:
        copies.append(
            pltpu.make_async_copy(
                text_hbm.at[:, pl.ds(vrows + 2 * trows, trows)], col_ref, sems.at[6]
            )
        )
    for copy in copies:
        copy.start()
    for copy in copies:
        copy.wait()
    mine = lax.axis_index("job")
    half = lax.axis_index("seq") // (shards // 2)
    job = mine ^ half ^ (2 if far else 0)
    column = lax.broadcasted_iota(jnp.int32, (1, shards * trows), 1)
    key_ok = column < count_ref[job]
    scale = HD ** (-0.5)
    video_keys = v_refs[1][...].reshape(shards * vrows, HD)
    text_keys = t_refs[1][...].reshape(shards * trows, HD)
    video_values = v_refs[2][...].reshape(shards * vrows, HD)
    text_values = t_refs[2][...].reshape(shards * trows, HD)

    def product(a, b):
        return lax.dot_general(a, b, (((1,), (1,)), ((), ())), preferred_element_type=jnp.float32)

    def one_block(queries):
        video_scores = product(queries, video_keys)
        text_scores = jnp.where(key_ok, product(queries, text_keys), -1e30)
        highest = jnp.maximum(
            jnp.max(video_scores, axis=-1, keepdims=True),
            jnp.max(text_scores, axis=-1, keepdims=True),
        )
        video_w = jnp.exp((video_scores - highest) * scale)
        text_w = jnp.exp((text_scores - highest) * scale)
        summed = jnp.sum(video_w, axis=-1, keepdims=True) + jnp.sum(text_w, axis=-1, keepdims=True)
        mixed = jnp.dot(
            video_w.astype(jnp.bfloat16), video_values, preferred_element_type=jnp.float32
        ) + jnp.dot(text_w.astype(jnp.bfloat16), text_values, preferred_element_type=jnp.float32)
        return (mixed / summed).astype(jnp.bfloat16)

    mixed_ref[...] = one_block(t_refs[0][...].reshape(shards * trows, HD))
    rows = vrows + 2 * trows
    sends = [
        pltpu.make_async_copy(out_ref.at[s], out_hbm.at[s], sems.at[7 + s]) for s in range(shards)
    ]

    def put(s, chosen):
        out_ref[s, vrows:rows] = chosen

    choose_slots(count_ref, splits_ref, job, mixed_ref[...], put)
    if not far:

        def put_columns(s, chosen):
            for c in range(3):
                lo = rows + 2 * trows * c
                out_ref[s, lo : lo + 2 * trows] = chosen[:, c * HD : (c + 1) * HD]

        choose_slots(
            count_ref, splits_ref, mine, col_ref[...].reshape(shards * trows, 3 * HD), put_columns
        )
    for i in range(0, shards, 2):
        done = one_block(v_refs[0][i : i + 2].reshape(2 * vrows, HD))
        out_ref[i, 0:vrows] = done[:vrows]
        out_ref[i + 1, 0:vrows] = done[vrows:]
        sends[i].start()
        sends[i + 1].start()
    for send in sends:
        send.wait()


def attend_pair(far, count, splits, video_qkv, text_qkv, vrows, trows):
    shards = video_qkv.shape[0]
    slots = 2 * trows
    total = shards * (vrows + trows)
    rows_out = vrows + slots * (1 if far else 4)
    scratch = [pltpu.VMEM((shards, vrows, HD), jnp.bfloat16)] * 3
    scratch += [pltpu.VMEM((shards, trows, HD), jnp.bfloat16)] * 3
    scratch += [pltpu.VMEM((shards * trows, HD), jnp.bfloat16)]
    scratch += [pltpu.VMEM((shards, rows_out, HD), jnp.bfloat16)]
    scratch += [pltpu.SemaphoreType.DMA((7 + shards,))]
    if not far:
        scratch += [pltpu.VMEM((shards, trows, 3 * HD), jnp.bfloat16)]
    return pl.pallas_call(
        functools.partial(attention_kernel, far, vrows + (trows if far else 0)),
        out_shape=pltpu.HBM((shards, rows_out, HD), jnp.bfloat16),
        in_specs=[smem_spec(), smem_spec(), hbm_spec(), hbm_spec()],
        out_specs=hbm_spec(),
        scratch_shapes=scratch,
        compiler_params=params(12),
        cost_estimate=cost(4 * total * total * HD, 3 << 20, total * total),
    )(count, splits, video_qkv, text_qkv)


def project_rows(heads_ref, w_ref, which, count, put):
    group, width = w_ref.shape[0] // HD, w_ref.shape[1]
    rows = jnp.concatenate([heads_ref[which * group + h, 0:count] for h in range(group)], axis=1)
    for lo in range(0, width, width // 4):
        cols = slice(lo, lo + width // 4)
        put(cols, jnp.dot(rows, w_ref[:, cols], preferred_element_type=jnp.float32))


def give_kernel(heads_ref, w_ref, *out_refs):
    size = out_refs[0].shape[0]

    def put(cols, total):
        for i, ref in enumerate(out_refs):
            ref[:, cols] = total[i * size : (i + 1) * size].astype(jnp.bfloat16)

    project_rows(heads_ref, w_ref, 1, size * len(out_refs), put)


def keep_kernel(pieces, heads_ref, w_ref, *refs):
    out_ref = refs[pieces]
    size = refs[0].shape[0]

    def put(cols, total):
        for i in range(pieces):
            part = total[i * size : (i + 1) * size] + refs[i][:, cols].astype(jnp.float32)
            out_ref[i * size : (i + 1) * size, cols] = part.astype(jnp.bfloat16)

    count = size * pieces
    project_rows(heads_ref, w_ref, 0, count, put)
    if len(refs) > pieces + 1:
        slot_ref = refs[pieces + 1]
        slots, width = slot_ref.shape
        for block in range(width // HD):
            lo = count + (block % 3) * slots
            slot_ref[:, block * HD : (block + 1) * HD] = heads_ref[block // 3, lo : lo + slots]


def out_call(kernel, rows, weights, inputs, outs):
    depth, width = weights.shape
    return pl.pallas_call(
        kernel,
        out_shape=tuple(jax.ShapeDtypeStruct((n, width), jnp.bfloat16) for n in outs),
        in_specs=[vmem_spec()] * len(inputs),
        out_specs=(vmem_spec(),) * len(outs),
        compiler_params=params(8),
        cost_estimate=cost(2 * rows * depth * width, 2 * (depth + 2 * rows) * width),
    )(*inputs)


def project_out(heads, rows, pieces, slots, weights, to_core):
    given = out_call(give_kernel, rows, weights, (heads, weights), (rows // pieces,) * pieces)
    kernel = functools.partial(keep_kernel, pieces)
    outs = (rows, slots) if slots else (rows,)
    return out_call(kernel, rows, weights, (heads, weights, *map(to_core, given)), outs)


def final_kernel(
    count_ref, splits_ref, video_ref, part_ref, chip_hbm, gate_ref, slot_ref, vout_hbm, tout_hbm,
    chip_ref, out_ref, in_sems, out_sems,
):
    vrows, step = video_ref.shape[1], slot_ref.shape[0]
    total_rows = part_ref.shape[0]
    reads, writes = [], []
    for i, lo in enumerate(range(0, total_rows, step)):
        rows = pl.ds(lo, step)
        reads.append(pltpu.make_async_copy(chip_hbm.at[rows], chip_ref.at[rows], in_sems.at[i]))
        target = vout_hbm.at[0, rows] if lo < vrows else tout_hbm.at[0]
        writes.append(pltpu.make_async_copy(out_ref.at[rows], target, out_sems.at[i]))
    for read in reads:
        read.start()
    job, shard = lax.axis_index("job"), lax.axis_index("seq")
    gate = table_row(gate_ref, job)
    offset = jnp.int32(0)
    for s in range(splits_ref.shape[1]):
        offset = offset + jnp.where(s < shard, splits_ref[job, s], 0)
    slot = lax.broadcasted_iota(jnp.int32, (step, 1), 0)
    valid = (slot < splits_ref[job, shard]) & (slot + offset < count_ref[job])
    for i, lo in enumerate(range(0, total_rows, step)):
        reads[i].wait()
        rows = slice(lo, lo + step)
        total = part_ref[rows].astype(jnp.float32) + chip_ref[rows].astype(jnp.float32)
        base = video_ref[0, rows] if lo < vrows else slot_ref[...]
        result = base.astype(jnp.float32) + gate * total
        if lo >= vrows:
            result = jnp.where(valid, result, 0.0)
        out_ref[rows] = result.astype(jnp.bfloat16)
        writes[i].start()
    for write in writes:
        write.wait()


def finish(count, splits, video, part, from_chip, gate, slot_rows):
    rows, width = part.shape
    steps = rows // slot_rows.shape[0]
    vrows = video.shape[1]
    return pl.pallas_call(
        final_kernel,
        out_shape=(
            jax.ShapeDtypeStruct((1, vrows, width), jnp.bfloat16),
            jax.ShapeDtypeStruct((1, rows - vrows, width), jnp.bfloat16),
        ),
        in_specs=[
            smem_spec(), smem_spec(), vmem_spec(), vmem_spec(), hbm_spec(), vmem_spec(), vmem_spec(),
        ],
        out_specs=(hbm_spec(), hbm_spec()),
        scratch_shapes=[
            pltpu.VMEM((rows, width), jnp.bfloat16),
            pltpu.VMEM((rows, width), jnp.bfloat16),
            pltpu.SemaphoreType.DMA((steps,)),
            pltpu.SemaphoreType.DMA((steps,)),
        ],
        compiler_params=params(8),
        cost_estimate=cost(6 * rows * width, 10 * rows * width),
    )(count, splits, video, part, from_chip, gate, slot_rows)


def two_wave_body(
    video,
    text_cache,
    text_count,
    holder,
    text_splits,
    mod_shift,
    mod_scale,
    mod_gate,
    text_gain,
    refine_w,
    refine_bias,
    w_qkv,
    q_gain,
    k_gain,
    w_out,
):
    job_count = lax.axis_size("job")
    shard_count = lax.axis_size("seq")
    group_size = w_qkv.shape[1]
    trows = text_cache.shape[1]
    vrows = video.shape[1]

    def to_core(x):
        return lax.ppermute(x, "job", [(i, i ^ 1) for i in range(job_count)])

    def to_chip(x):
        return lax.ppermute(x, "job", [(i, i ^ 2) for i in range(job_count)])

    def over_seq(x):
        return lax.all_to_all(x, "seq", split_axis=0, concat_axis=0, tiled=False)

    def after(x, earlier):
        return lax.optimization_barrier((x, earlier))[0]

    qkv_w = jnp.transpose(w_qkv, (2, 1, 0, 3))
    own_video = video[0]
    core_video = to_core(own_video)

    normed = norm_text(text_cache, text_gain)
    normed_core = to_core(normed)
    normed_chip = to_chip(normed)
    chip_video = to_chip(after(own_video, normed))
    local_send = qkv_local(own_video, core_video, mod_shift, mod_scale, qkv_w, q_gain, k_gain)
    local_qkv = over_seq(local_send.reshape(shard_count, vrows, 3 * HD))
    normed_core, normed_chip = after((normed_core, normed_chip), local_send)
    normed_both = to_core(normed_chip)
    lifted = jnp.dot(
        jnp.concatenate([normed, normed_core, normed_chip, normed_both], axis=0),
        refine_w,
        preferred_element_type=jnp.float32,
    )
    refined = (lifted + refine_bias).astype(jnp.bfloat16).reshape(job_count, trows, -1)
    refined_core = to_core(refined)
    refined_chip = to_chip(refined)
    refined_both = to_core(refined_chip)

    chip_video = after(chip_video, refined)
    both_video = to_core(chip_video)
    send = qkv_remote(
        holder,
        (chip_video, both_video),
        (refined, refined_core, refined_chip, refined_both),
        mod_shift,
        mod_scale,
        qkv_w,
        q_gain,
        k_gain,
    )
    second = over_seq(after(send.reshape(shard_count, -1, 3 * HD), local_qkv))
    second = pltpu.with_memory_space_constraint(second, pltpu.HBM)

    remote_mixed = attend_pair(True, text_count, text_splits, second, second, vrows, trows)
    remote_back = over_seq(remote_mixed)
    local_mixed = attend_pair(
        False, text_count, text_splits, after(local_qkv, remote_mixed), second, vrows, trows
    )
    out_weight = w_out.reshape(group_size * HD, w_out.shape[2])
    rows = vrows + 2 * trows
    remote_back = after(remote_back, local_mixed)
    local_back = over_seq(after(local_mixed, remote_back))
    (crossing,) = project_out(remote_back, rows, 1, 0, out_weight, to_core)
    from_chip = to_chip(crossing)
    local_part, slot_rows = project_out(
        after(local_back, crossing), rows, 3, 2 * trows, out_weight, to_core
    )
    return finish(
        text_count, text_splits, video, local_part, from_chip, mod_gate, slot_rows
    )


def body(*arrays):
    video, text_cache, w_qkv = arrays[0], arrays[1], arrays[11]
    job_count = lax.axis_size("job")
    shard_count = lax.axis_size("seq")
    fits = (
        job_count == 4
        and shard_count == 2 * w_qkv.shape[1]
        and video.shape[1] == 128
        and text_cache.shape[1] == 32
    )
    return (two_wave_body if fits else general_body)(*arrays)


def solution(mesh):
    placed = (
        P("job", "seq", None),
        P("job", "seq", None),
        P(),
        P(),
        P(),
        P(),
        P(),
        P(),
        P(),
        P(None, "job"),
        P("job"),
        P(None, "job", None, None),
        P("job", None),
        P("job", None),
        P("job", None, None),
    )
    return jax.shard_map(
        body,
        mesh=mesh,
        in_specs=placed,
        out_specs=(P("job", "seq", None), P("job", "seq", None)),
        check_vma=False,
    )
```

```python
import functools
import math

import jax
import jax.numpy as jnp
from jax import lax
from jax.experimental import pallas as pl
from jax.experimental.pallas import tpu as pltpu
from jax.sharding import PartitionSpec as P

HD = 128
TXT = 256


epsilon = 1e-06


def rms_scale(values, gains):
    mean_square = jnp.mean(values * values, axis=-1, keepdims=True)
    return values * lax.rsqrt(mean_square + epsilon) * gains


def modulate(tokens, shift_part, scale_part):
    widened = tokens.astype(jnp.float32)
    centre = jnp.mean(widened, axis=-1, keepdims=True)
    spread_sq = jnp.mean((widened - centre) ** 2, axis=-1, keepdims=True)
    normed = (widened - centre) * lax.rsqrt(spread_sq + epsilon)
    return (normed * (1.0 + scale_part) + shift_part).astype(jnp.bfloat16)


def refine_rows(raw_text, text_gain, refine_w, refine_bias):
    normed = rms_scale(raw_text.astype(jnp.float32), text_gain).astype(jnp.bfloat16)
    lifted = jnp.einsum("jrt,tc->jrc", normed, refine_w, preferred_element_type=jnp.float32)
    return (lifted + refine_bias).astype(jnp.bfloat16)


def project_heads(modded, w_qkv, q_gain, k_gain):
    projections = jnp.einsum("jrd,dhce->jrhce", modded, w_qkv, preferred_element_type=jnp.float32)
    queries = rms_scale(projections[:, :, :, 0], q_gain).astype(jnp.bfloat16)
    key_rows = rms_scale(projections[:, :, :, 1], k_gain).astype(jnp.bfloat16)
    values = projections[:, :, :, 2].astype(jnp.bfloat16)
    return jnp.stack([queries, key_rows, values], axis=3)


def query_block(query_count, unit_rows):
    unit_total = query_count // unit_rows
    for factor in range(1, unit_total + 1):
        if unit_total % factor == 0 and factor * unit_rows >= 512:
            return factor * unit_rows
    return query_count


def attend(queries, key_rows, values, key_ok, block_rows):
    query_count = queries.shape[0]
    stacked_blocks = queries.reshape(query_count // block_rows, block_rows, queries.shape[1])
    scale_factor = HD ** (-0.5)

    def one_block(query_part):
        scores = (
            jnp.einsum("qe,ke->qk", query_part, key_rows, preferred_element_type=jnp.float32)
            * scale_factor
        )
        scores = jnp.where(key_ok[None, :], scores, -1e30)
        highest = jnp.max(scores, axis=-1, keepdims=True)
        weights = jnp.exp(scores - highest)
        summed = jnp.sum(weights, axis=-1, keepdims=True)
        weights = (weights / summed).astype(jnp.bfloat16)
        return jnp.dot(weights, values, preferred_element_type=jnp.float32).astype(jnp.bfloat16)

    return lax.map(one_block, stacked_blocks).reshape(query_count, queries.shape[1])


def general_body(
    video,
    text_cache,
    text_count,
    holder,
    text_splits,
    mod_shift,
    mod_scale,
    mod_gate,
    text_gain,
    refine_w,
    refine_bias,
    w_qkv,
    q_gain,
    k_gain,
    w_out,
):
    job_count = lax.axis_size("job")
    shard_count = lax.axis_size("seq")
    my_job = lax.axis_index("job")
    my_shard = lax.axis_index("seq")
    video_rows = video.shape[1]
    block_rows = text_cache.shape[1]
    slot_count = 2 * block_rows
    row_count = video_rows + slot_count
    group_size = w_qkv.shape[1]
    pair_count = job_count * group_size
    slot_total = max(pair_count, shard_count)
    repeat_count = slot_total // pair_count
    per_device = slot_total // shard_count
    offsets = jnp.cumsum(text_splits, axis=1) - text_splits
    slot_ids = jnp.arange(slot_count, dtype=jnp.int32)
    my_offsets = lax.dynamic_index_in_dim(offsets, my_shard, 1, keepdims=False)
    my_splits = lax.dynamic_index_in_dim(text_splits, my_shard, 1, keepdims=False)
    slot_valid = (slot_ids[None, :] < my_splits[:, None]) & (
        my_offsets[:, None] + slot_ids[None, :] < text_count[:, None]
    )
    position = holder[:, None] * (TXT + slot_count) + my_offsets[:, None] + slot_ids[None, :]
    cache_rows = lax.all_gather(text_cache, "job", axis=0, tiled=True)
    refined = refine_rows(cache_rows, text_gain, refine_w, refine_bias)
    gathered_text = lax.all_gather(refined, "seq", axis=1, tiled=True)
    width = gathered_text.shape[2]
    padded = jnp.concatenate(
        [
            gathered_text,
            jnp.zeros((gathered_text.shape[0], slot_count, width), gathered_text.dtype),
        ],
        axis=1,
    )
    flat_rows = padded.reshape(-1, width)
    chosen = jnp.take(flat_rows, position.reshape(-1), axis=0).reshape(job_count, slot_count, width)
    text_cols = jnp.where(slot_valid[:, :, None], chosen, jnp.zeros_like(chosen))
    text_full = lax.all_gather(text_cols, "job", axis=2, tiled=True)
    modded = modulate(
        lax.all_gather(video, "job", axis=0, tiled=True),
        mod_shift[:, None, :],
        mod_scale[:, None, :],
    )
    video_heads = project_heads(modded, w_qkv, q_gain, k_gain)
    text_modded = modulate(text_full, mod_shift[:, None, :], mod_scale[:, None, :])
    text_heads = project_heads(text_modded, w_qkv, q_gain, k_gain)
    heads_all = jnp.concatenate([video_heads, text_heads], axis=1)
    by_row = jnp.transpose(heads_all, (1, 0, 2, 3, 4)).reshape(row_count, pair_count, 3, HD)
    query_rows = by_row[:, :, 0]
    key_rows = jnp.tile(by_row[:, :, 1], (1, repeat_count, 1))
    value_rows = jnp.tile(by_row[:, :, 2], (1, repeat_count, 1))
    query_send = jnp.tile(query_rows, (1, repeat_count, 1))
    query_recv, key_recv, value_recv = (
        lax.all_to_all(query_send, "seq", split_axis=1, concat_axis=0, tiled=True),
        lax.all_to_all(key_rows, "seq", split_axis=1, concat_axis=0, tiled=True),
        lax.all_to_all(value_rows, "seq", split_axis=1, concat_axis=0, tiled=True),
    )
    my_part = my_shard * per_device // pair_count
    outputs = []
    for slot_index in range(per_device):
        slot_global = my_shard * per_device + slot_index
        job_of_slot = slot_global % pair_count // group_size
        splits_row = lax.dynamic_index_in_dim(text_splits, job_of_slot, 0, keepdims=False)
        offsets_row = lax.dynamic_index_in_dim(offsets, job_of_slot, 0, keepdims=False)
        count_of_job = lax.dynamic_index_in_dim(text_count, job_of_slot, 0, keepdims=False)
        key_valid = (slot_ids[None, :] < splits_row[:, None]) & (
            offsets_row[:, None] + slot_ids[None, :] < count_of_job
        )
        key_ok = jnp.concatenate(
            [jnp.ones((shard_count, video_rows), jnp.bool_), key_valid], axis=1
        ).reshape(-1)
        grouped = query_recv[:, slot_index].reshape(
            shard_count // repeat_count, repeat_count, row_count, HD
        )
        queries = lax.dynamic_index_in_dim(grouped, my_part, 1, keepdims=False).reshape(-1, HD)
        block_size = query_block(queries.shape[0], row_count)
        outputs.append(
            attend(queries, key_recv[:, slot_index], value_recv[:, slot_index], key_ok, block_size)
        )
    attended = jnp.stack(outputs, axis=1)
    spread_out = attended.reshape(shard_count // repeat_count, 1, row_count, per_device, HD)
    selector = (
        (jnp.arange(repeat_count) == my_part).astype(jnp.bfloat16).reshape(1, repeat_count, 1, 1, 1)
    )
    send_back = (spread_out * selector).reshape(shard_count * row_count, per_device, HD)
    returned = lax.all_to_all(send_back, "seq", split_axis=0, concat_axis=1, tiled=True)
    own_heads = lax.dynamic_index_in_dim(
        returned.reshape(row_count, repeat_count, pair_count, HD),
        my_shard % repeat_count,
        1,
        keepdims=False,
    )
    per_job = jnp.transpose(
        own_heads.reshape(row_count, job_count, group_size * HD), (1, 0, 2)
    ).reshape(job_count * row_count, group_size * HD)
    out_weight = w_out.reshape(group_size * HD, w_out.shape[2])
    projected = lax.psum_scatter(
        jnp.dot(per_job, out_weight, preferred_element_type=jnp.float32).astype(jnp.bfloat16),
        "job",
        scatter_dimension=0,
        tiled=True,
    ).astype(jnp.float32)
    own_rows = jnp.concatenate(
        [video[0], lax.dynamic_index_in_dim(text_full, my_job, 0, keepdims=False)], axis=0
    )
    gate_row = lax.dynamic_index_in_dim(mod_gate, my_job, 0, keepdims=False)
    result = (own_rows.astype(jnp.float32) + gate_row * projected).astype(jnp.bfloat16)
    own_valid = lax.dynamic_index_in_dim(slot_valid, my_job, 0, keepdims=False)
    text_result = jnp.where(
        own_valid[:, None], result[video_rows:], jnp.zeros_like(result[video_rows:])
    )
    return (result[:video_rows][None], text_result[None])


def vmem_spec():
    return pl.BlockSpec(memory_space=pltpu.VMEM)


def smem_spec():
    return pl.BlockSpec(memory_space=pltpu.SMEM)


def hbm_spec():
    return pl.BlockSpec(memory_space=pltpu.HBM)


def params(mib):
    return pltpu.CompilerParams(vmem_limit_bytes=mib << 20)


def cost(flops, moved, exps=0):
    return pl.CostEstimate(flops=int(flops), bytes_accessed=int(moved), transcendentals=int(exps))


def fetch(sources, targets, sems):
    copies = [
        pltpu.make_async_copy(source, target, sems.at[i])
        for i, (source, target) in enumerate(zip(sources, targets))
    ]
    for copy in copies:
        copy.start()
    return copies


def in_hbm(x):
    return pltpu.with_memory_space_constraint(x, pltpu.HBM)


def norm_kernel(rows_hbm, gain_hbm, out_ref, rows_ref, gain_ref, sems):
    for copy in fetch((rows_hbm.at[0], gain_hbm), (rows_ref, gain_ref), sems):
        copy.wait()
    out_ref[...] = rms_scale(rows_ref[...].astype(jnp.float32), gain_ref[...]).astype(jnp.bfloat16)


def norm_text(rows, gain):
    _, count, depth = rows.shape
    return pl.pallas_call(
        norm_kernel,
        out_shape=jax.ShapeDtypeStruct((count, depth), jnp.bfloat16),
        in_specs=[hbm_spec(), hbm_spec()],
        out_specs=vmem_spec(),
        scratch_shapes=[
            pltpu.VMEM((count, depth), jnp.bfloat16),
            pltpu.VMEM((1, depth), jnp.float32),
            pltpu.SemaphoreType.DMA((2,)),
        ],
        compiler_params=params(8),
        cost_estimate=cost(4 * rows.size, 4 * rows.size),
    )(in_hbm(rows), in_hbm(gain[None]))


def table_row(ref, index):
    return ref[pl.ds(index, 1)]


def weight_copies(w_hbm, w_ref, sems, first):
    return [
        pltpu.make_async_copy(w_hbm.at[:, h], w_ref.at[:, h], sems.at[h])
        for h in (first, first + 1)
    ]


def project_heads_into(out_hbm, out_ref, x_ref, w_hbm, w_ref, sems, qg_ref, kg_ref):
    heads, rows = w_ref.shape[1], x_ref.shape[0]
    sends = []
    for first in range(0, heads, 2):
        for copy in weight_copies(w_hbm, w_ref, sems, first):
            copy.wait()
        if first + 2 < heads:
            for copy in weight_copies(w_hbm, w_ref, sems, first + 2):
                copy.start()
        pair = (first, first + 1)
        weights = jnp.concatenate([w_ref[c, h] for h in pair for c in range(3)], axis=1)
        raw = jnp.dot(x_ref[...], weights, preferred_element_type=jnp.float32)
        for i, h in enumerate(pair):
            lo = 3 * HD * i
            queries = rms_scale(raw[:, lo : lo + HD], qg_ref[h : h + 1]).astype(jnp.bfloat16)
            keys = rms_scale(raw[:, lo + HD : lo + 2 * HD], kg_ref[h : h + 1]).astype(jnp.bfloat16)
            values = raw[:, lo + 2 * HD : lo + 3 * HD].astype(jnp.bfloat16)
            for c, part in enumerate((queries, keys, values)):
                out_ref[h, 0:rows, c * HD : (c + 1) * HD] = part
            sends.append(pltpu.make_async_copy(out_ref.at[h], out_hbm.at[h], sems.at[heads + h]))
            sends[-1].start()
    for send in sends:
        send.wait()


def my_place(group):
    mine = lax.axis_index("job")
    core, half = mine & 1, lax.axis_index("seq") // group
    return mine, core, half, (mine - core) | half


def take_rows(x_ref, lo, here_ref, core_refs, stays):
    rows = here_ref.shape[0]

    @pl.when(stays)
    def _():
        x_ref[lo : lo + rows] = here_ref[...]

    @pl.when(jnp.logical_not(stays))
    def _():
        size = rows // len(core_refs)
        for i, ref in enumerate(core_refs):
            x_ref[lo + i * size : lo + (i + 1) * size] = ref[...]


def modulate_rows(x_ref, lo, hi, shift_ref, scale_ref, job):
    x_ref[lo:hi] = modulate(x_ref[lo:hi], table_row(shift_ref, job), table_row(scale_ref, job))


def qkv_kernel(pieces, has_text, *refs):
    (a_ref, b_ref), refs = refs[:2], refs[2:]
    a_core, refs = refs[: pieces[0]], refs[pieces[0] :]
    b_core, refs = refs[: pieces[1]], refs[pieces[1] :]
    if has_text:
        (text_here_ref, text_core_ref), refs = refs[:2], refs[2:]
    table_hbm, w_hbm, out_hbm, refs = refs[:4], refs[4], refs[5], refs[6:]
    x_ref, w_ref, out_ref, table_refs, sems, refs = refs[0], refs[1], refs[2], refs[3:7], refs[7], refs[8:]
    shift_ref, scale_ref, qg_ref, kg_ref = table_refs
    rows, group = a_ref.shape[0], w_ref.shape[1]
    tables = fetch(table_hbm, table_refs, sems.at[pl.ds(2 * group, 4)])
    for copy in weight_copies(w_hbm, w_ref, sems, 0):
        copy.start()
    mine, core, half, job = my_place(group)
    take_rows(x_ref, 0, a_ref, a_core, core == half)
    take_rows(x_ref, rows, b_ref, b_core, core == half)
    for copy in tables:
        copy.wait()
    modulate_rows(x_ref, 0, rows, shift_ref, scale_ref, job)
    modulate_rows(x_ref, rows, 2 * rows, shift_ref, scale_ref, job ^ 2)
    lo = 2 * rows
    if has_text:
        text_ref = refs[0]
        blocks, trows, width = text_here_ref.shape
        blocks = blocks // 2
        for b in range(4):
            for q in range(4):
                part = text_core_ref if q & 1 else text_here_ref

                @pl.when(mine ^ b == q)
                def _():
                    for t in range(blocks):
                        job_of, shard_of, chip_of = t // 2, t % 2, q // 2
                        text_ref[t * trows : (t + 1) * trows, b * width : (b + 1) * width] = part[
                            4 * chip_of + 2 * shard_of + (job_of ^ chip_of)
                        ]

        x_ref[lo:] = text_ref[...]
        modulate_rows(x_ref, lo, lo + 2 * trows, shift_ref, scale_ref, job)
        modulate_rows(x_ref, lo + 2 * trows, lo + 4 * trows, shift_ref, scale_ref, job ^ 2)
        for h in range(group):
            cols = pl.ds(pl.multiple_of((2 * h + core) * 3 * HD, HD), 3 * HD)
            out_ref[h, lo + 4 * trows :] = text_ref[0 : 2 * trows, cols]
    project_heads_into(out_hbm, out_ref, x_ref, w_hbm, w_ref, sems, qg_ref, kg_ref)


def qkv_half(here, from_core, text, tables, weights, q_gain, k_gain):
    group, width = weights.shape[1:3]
    pieces = tuple(map(len, from_core))
    rows_in = rows_out = 2 * here[0].shape[0]
    extra = []
    if text:
        blocks, trows, _ = text[0].shape
        rows_in += blocks // 2 * trows
        rows_out = rows_in + 2 * trows
        extra = [pltpu.VMEM((blocks // 2 * trows, width), jnp.bfloat16)]
    inputs = (*here, *from_core[0], *from_core[1], *text)
    tables = (*tables, q_gain, k_gain)
    return pl.pallas_call(
        functools.partial(qkv_kernel, pieces, bool(text)),
        out_shape=pltpu.HBM((group, rows_out, 3 * HD), jnp.bfloat16),
        in_specs=[vmem_spec()] * len(inputs) + [hbm_spec()] * 5,
        out_specs=hbm_spec(),
        scratch_shapes=[
            pltpu.VMEM((rows_in, width), jnp.bfloat16),
            pltpu.VMEM(weights.shape, jnp.bfloat16),
            pltpu.VMEM((group, rows_out, 3 * HD), jnp.bfloat16),
            *[pltpu.VMEM(table.shape, jnp.float32) for table in tables],
            pltpu.SemaphoreType.DMA((2 * group + 4,)),
            *extra,
        ],
        compiler_params=params(24),
        cost_estimate=cost(2 * rows_in * weights.size, 2 * weights.size + 4 * rows_in * width),
    )(*inputs, *map(in_hbm, tables), in_hbm(weights))


def refine_kernel(
    group, holder_ref, n0_ref, n1_ref, n2_ref, n3_ref, w_hbm, bias_hbm, keep_ref, send_ref, x_ref,
    w_ref, bias_ref, sems,
):
    mine, _, _, job = my_place(group)
    chunks, depth, _ = w_ref.shape
    copies = fetch(
        [w_hbm.at[pl.ds(i * depth, depth)] for i in range(chunks)] + [bias_hbm],
        [w_ref.at[i] for i in range(chunks)] + [bias_ref],
        sems,
    )
    rows = n0_ref.shape[0]
    for k, flip in enumerate((0, 2, 1, 3)):
        for r, part in enumerate((n0_ref, n1_ref, n2_ref, n3_ref)):

            @pl.when(holder_ref[job ^ flip] ^ mine == r)
            def _():
                x_ref[k * rows : (k + 1) * rows] = part[...]

    copies[-1].wait()
    lifted = bias_ref[...]
    for i in range(chunks):
        copies[i].wait()
        part = x_ref[:, i * depth : (i + 1) * depth]
        lifted = lifted + jnp.dot(part, w_ref[i], preferred_element_type=jnp.float32)
    refined = lifted.astype(jnp.bfloat16)
    for k in range(2):
        keep_ref[k] = refined[k * rows : (k + 1) * rows]
        send_ref[k] = refined[(2 + k) * rows : (3 + k) * rows]


def refine_text(group, holder, normed, weights, bias):
    rows, depth = normed[0].shape
    width = weights.shape[1]
    chunks = 4
    out = jax.ShapeDtypeStruct((2, rows, width), jnp.bfloat16)
    return pl.pallas_call(
        functools.partial(refine_kernel, group),
        out_shape=(out, out),
        in_specs=[smem_spec()] + [vmem_spec()] * 4 + [hbm_spec()] * 2,
        out_specs=(vmem_spec(), vmem_spec()),
        scratch_shapes=[
            pltpu.VMEM((4 * rows, depth), jnp.bfloat16),
            pltpu.VMEM((chunks, depth // chunks, width), jnp.bfloat16),
            pltpu.VMEM((1, width), jnp.float32),
            pltpu.SemaphoreType.DMA((chunks + 1,)),
        ],
        compiler_params=params(14),
        cost_estimate=cost(8 * rows * depth * width, 2 * depth * width),
    )(holder, *normed, in_hbm(weights), in_hbm(bias[None]))


def pack_kernel(*refs):
    out_ref = refs[-1]
    for i, ref in enumerate(refs[:-1]):
        out_ref[i * ref.shape[0] : (i + 1) * ref.shape[0]] = ref[...]


def pack(parts):
    jobs, rows, width = parts[0].shape
    return pl.pallas_call(
        pack_kernel,
        out_shape=jax.ShapeDtypeStruct((len(parts) * jobs, rows, width), jnp.bfloat16),
        in_specs=[vmem_spec()] * len(parts),
        out_specs=vmem_spec(),
        compiler_params=params(4),
        cost_estimate=cost(0, 4 * len(parts) * parts[0].size),
    )(*parts)


def choose_slots(count_ref, splits_ref, job, row, table, put):
    shards = splits_ref.shape[1]
    slot = lax.broadcasted_iota(jnp.int32, (2 * row.shape[1] // shards, row.shape[1]), 0)
    offset = jnp.int32(0)
    for s in range(shards):
        chosen = (row == slot + offset) & (slot < splits_ref[job, s]) & (row < count_ref[job])
        chosen = jnp.where(chosen, 1.0, 0.0).astype(jnp.bfloat16)
        put(s, jnp.dot(chosen, table, preferred_element_type=jnp.float32).astype(jnp.bfloat16))
        offset = offset + splits_ref[job, s]


def attention_kernel(far, count_ref, splits_ref, first_hbm, second_hbm, *refs):
    out_hbm, v_refs, t_refs, mixed_ref, out_ref, sems = refs[0], refs[1:4], refs[4:7], *refs[7:10]
    col_ref = None if far else refs[10]
    group, vrows, _ = v_refs[0].shape
    trows = t_refs[0].shape[1]
    one = vrows // 2
    copies = []

    def fetch(source, target):
        copies.append(pltpu.make_async_copy(source, target, sems.at[len(copies)]))

    for c in (1, 0, 2):
        cols = pl.ds(c * HD, HD)
        mine = pl.ds(one if far else 0, one)
        fetch(first_hbm.at[:, mine, cols], v_refs[c].at[:, pl.ds(0, one)])
        fetch(second_hbm.at[:, mine, cols], v_refs[c].at[:, pl.ds(one, one)])
        text_rows = pl.ds(vrows + (trows if far else 0), trows)
        fetch(second_hbm.at[:, text_rows, cols], t_refs[c])
    if not far:
        fetch(second_hbm.at[:, pl.ds(vrows + 2 * trows, trows)], col_ref)
    for copy in copies:
        copy.start()
    for copy in copies:
        copy.wait()
    _, _, half, job = my_place(group)
    job = job ^ 2 if far else job
    block = trows // 2
    place = lax.broadcasted_iota(jnp.int32, (1, group * trows), 1)
    row = (place // trows) * block + place % block
    row = row + (((place // block) & 1) ^ half) * (group * block)
    key_ok = row < count_ref[job]
    scale = HD ** (-0.5) * math.log2(math.e)
    ones = jnp.ones((group * vrows, HD), jnp.bfloat16)
    video_keys = v_refs[1][...].reshape(group * vrows, HD)
    text_keys = t_refs[1][...].reshape(group * trows, HD)
    video_values = jnp.concatenate([v_refs[2][...].reshape(group * vrows, HD), ones], axis=1)
    text_values = jnp.concatenate(
        [t_refs[2][...].reshape(group * trows, HD), ones[: group * trows]], axis=1
    )

    def product(a, b):
        return lax.dot_general(a, b, (((1,), (1,)), ((), ())), preferred_element_type=jnp.float32)

    def one_block(queries):
        video_scores = product(queries, video_keys)
        text_scores = jnp.where(key_ok, product(queries, text_keys), -1e30)
        highest = jnp.maximum(
            jnp.max(video_scores, axis=-1, keepdims=True),
            jnp.max(text_scores, axis=-1, keepdims=True),
        )
        video_w = jnp.exp2((video_scores - highest) * scale)
        text_w = jnp.exp2((text_scores - highest) * scale)
        mixed = jnp.dot(
            video_w.astype(jnp.bfloat16), video_values, preferred_element_type=jnp.float32
        ) + jnp.dot(text_w.astype(jnp.bfloat16), text_values, preferred_element_type=jnp.float32)
        return (mixed[:, :HD] / mixed[:, HD:]).astype(jnp.bfloat16)

    mixed_ref[...] = one_block(t_refs[0][...].reshape(group * trows, HD))
    rows = vrows // 2 + trows

    def put(s, chosen):
        out_ref[s, vrows // 2 : rows] = chosen

    choose_slots(count_ref, splits_ref, job, row, mixed_ref[...], put)
    if not far:

        def put_columns(s, chosen):
            for c in range(3):
                lo = rows + trows * c
                out_ref[s, lo : lo + trows] = chosen[:, c * HD : (c + 1) * HD]

        columns = col_ref[...].reshape(group * trows, 3 * HD)
        choose_slots(count_ref, splits_ref, job, row, columns, put_columns)
    sends = []
    for i in range(group):
        done = one_block(v_refs[0][i])
        for part in range(2):
            shard = (half ^ part) * group + i
            out_ref[shard, 0 : vrows // 2] = done[part * (vrows // 2) : (part + 1) * (vrows // 2)]
            sends.append(
                pltpu.make_async_copy(
                    out_ref.at[shard], out_hbm.at[shard], sems.at[10 + 2 * i + part]
                )
            )
            sends[-1].start()
    for send in sends:
        send.wait()


def attend_pair(far, count, splits, first, second, vrows, trows):
    group, shards = first.shape[0], splits.shape[1]
    total = group * (vrows + trows)
    rows_out = vrows // 2 + trows * (1 if far else 4)
    scratch = [pltpu.VMEM((group, vrows, HD), jnp.bfloat16)] * 3
    scratch += [pltpu.VMEM((group, trows, HD), jnp.bfloat16)] * 3
    scratch += [pltpu.VMEM((group * trows, HD), jnp.bfloat16)]
    scratch += [pltpu.VMEM((shards, rows_out, HD), jnp.bfloat16)]
    scratch += [pltpu.SemaphoreType.DMA((10 + shards,))]
    if not far:
        scratch += [pltpu.VMEM((group, trows, 3 * HD), jnp.bfloat16)]
    return pl.pallas_call(
        functools.partial(attention_kernel, far),
        out_shape=pltpu.HBM((shards, rows_out, HD), jnp.bfloat16),
        in_specs=[smem_spec(), smem_spec(), hbm_spec(), hbm_spec()],
        out_specs=hbm_spec(),
        scratch_shapes=scratch,
        compiler_params=params(12),
        cost_estimate=cost(4 * total * total * HD, 3 << 20, total * total),
    )(count, splits, first, second)


def project_rows(heads_ref, w_ref, job, count, put):
    group, width = w_ref.shape[0] // HD, w_ref.shape[1]
    rows = jnp.concatenate([heads_ref[job * group + h, 0:count] for h in range(group)], axis=1)
    for lo in range(0, width, width // 4):
        cols = slice(lo, lo + width // 4)
        put(cols, jnp.dot(rows, w_ref[:, cols], preferred_element_type=jnp.float32))


def give_kernel(pieces, heads_ref, w_ref, *refs):
    core = lax.axis_index("job") & 1
    size = refs[0].shape[0]

    def put(cols, total):
        for i, ref in enumerate(refs[:pieces]):
            ref[:, cols] = total[i * size : (i + 1) * size].astype(jnp.bfloat16)

    project_rows(heads_ref, w_ref, 1 - core, size * pieces, put)
    if len(refs) > pieces:
        slot_ref = refs[pieces]
        slots = slot_ref.shape[0]
        for h in range(w_ref.shape[0] // HD):
            for c in range(3):
                lo = size * pieces + slots * c
                slot_ref[:, (3 * h + c) * HD : (3 * h + c + 1) * HD] = heads_ref[
                    (1 - core) * (w_ref.shape[0] // HD) + h, lo : lo + slots
                ]


def keep_kernel(pieces, given, heads_ref, w_ref, *refs):
    core = lax.axis_index("job") & 1
    out_ref = refs[given]
    size = refs[0].shape[0]

    def put(cols, total):
        for i in range(pieces):
            part = total[i * size : (i + 1) * size] + refs[i][:, cols].astype(jnp.float32)
            out_ref[i * size : (i + 1) * size, cols] = part.astype(jnp.bfloat16)

    project_rows(heads_ref, w_ref, core, size * pieces, put)
    if given > pieces:
        slot_ref, other_ref = refs[given + 1], refs[pieces]
        slots, group = slot_ref.shape[0], w_ref.shape[0] // HD
        for h in range(group):
            for c in range(3):
                lo = size * pieces + slots * c
                cols = pl.ds(pl.multiple_of((3 * (2 * h + core) + c) * HD, HD), HD)
                slot_ref[:, cols] = heads_ref[core * group + h, lo : lo + slots]
                cols = pl.ds(pl.multiple_of((3 * (2 * h + 1 - core) + c) * HD, HD), HD)
                slot_ref[:, cols] = other_ref[:, (3 * h + c) * HD : (3 * h + c + 1) * HD]


def out_call(kernel, rows, weights, inputs, outs):
    depth, width = weights.shape
    return pl.pallas_call(
        kernel,
        out_shape=tuple(jax.ShapeDtypeStruct(shape, jnp.bfloat16) for shape in outs),
        in_specs=[vmem_spec()] * len(inputs),
        out_specs=(vmem_spec(),) * len(outs),
        compiler_params=params(8),
        cost_estimate=cost(2 * rows * depth * width, 2 * (depth + 2 * rows) * width),
    )(*inputs)


def project_out(heads, rows, pieces, slots, weights, to_core):
    width = weights.shape[1]
    outs = [(rows // pieces, width)] * pieces + ([(slots, width // 2)] if slots else [])
    kernel = functools.partial(give_kernel, pieces)
    given = [to_core(x) for x in out_call(kernel, rows, weights, (heads, weights), outs)]
    kernel = functools.partial(keep_kernel, pieces, len(given))
    outs = [(rows, width)] + ([(slots, width)] if slots else [])
    return out_call(kernel, rows, weights, (heads, weights, *given), outs)


def final_kernel(
    count_ref, splits_ref, video_hbm, part_ref, chip_hbm, gate_hbm, slot_ref, vout_hbm, tout_hbm,
    chip_ref, out_ref, video_ref, gate_ref, in_sems, out_sems,
):
    vrows, step = video_ref.shape[0], slot_ref.shape[0]
    total_rows = part_ref.shape[0]
    reads, writes = [], []
    for i, lo in enumerate(range(0, total_rows, step)):
        rows = pl.ds(lo, step)
        reads.append(pltpu.make_async_copy(chip_hbm.at[rows], chip_ref.at[rows], in_sems.at[i]))
        target = vout_hbm.at[0, rows] if lo < vrows else tout_hbm.at[0]
        writes.append(pltpu.make_async_copy(out_ref.at[rows], target, out_sems.at[i]))
    for read in reads:
        read.start()
    steps = len(reads)
    for copy in fetch((video_hbm.at[0], gate_hbm), (video_ref, gate_ref), in_sems.at[pl.ds(steps, 2)]):
        copy.wait()
    job, shard = lax.axis_index("job"), lax.axis_index("seq")
    gate = table_row(gate_ref, job)
    offset = jnp.int32(0)
    for s in range(splits_ref.shape[1]):
        offset = offset + jnp.where(s < shard, splits_ref[job, s], 0)
    slot = lax.broadcasted_iota(jnp.int32, (step, 1), 0)
    valid = (slot < splits_ref[job, shard]) & (slot + offset < count_ref[job])
    for i, lo in enumerate(range(0, total_rows, step)):
        reads[i].wait()
        rows = slice(lo, lo + step)
        total = part_ref[rows].astype(jnp.float32) + chip_ref[rows].astype(jnp.float32)
        base = video_ref[rows] if lo < vrows else slot_ref[...]
        result = base.astype(jnp.float32) + gate * total
        if lo >= vrows:
            result = jnp.where(valid, result, 0.0)
        out_ref[rows] = result.astype(jnp.bfloat16)
        writes[i].start()
    for write in writes:
        write.wait()


def finish(count, splits, video, part, from_chip, gate, slot_rows):
    rows, width = part.shape
    steps = rows // slot_rows.shape[0]
    vrows = video.shape[1]
    return pl.pallas_call(
        final_kernel,
        out_shape=(
            jax.ShapeDtypeStruct((1, vrows, width), jnp.bfloat16),
            jax.ShapeDtypeStruct((1, rows - vrows, width), jnp.bfloat16),
        ),
        in_specs=[
            smem_spec(), smem_spec(), hbm_spec(), vmem_spec(), hbm_spec(), hbm_spec(), vmem_spec(),
        ],
        out_specs=(hbm_spec(), hbm_spec()),
        scratch_shapes=[
            pltpu.VMEM((rows, width), jnp.bfloat16),
            pltpu.VMEM((rows, width), jnp.bfloat16),
            pltpu.VMEM((vrows, width), jnp.bfloat16),
            pltpu.VMEM(gate.shape, jnp.float32),
            pltpu.SemaphoreType.DMA((steps + 2,)),
            pltpu.SemaphoreType.DMA((steps,)),
        ],
        compiler_params=params(8),
        cost_estimate=cost(6 * rows * width, 10 * rows * width),
    )(count, splits, in_hbm(video), part, from_chip, in_hbm(gate), slot_rows)


def two_wave_body(
    video,
    text_cache,
    text_count,
    holder,
    text_splits,
    mod_shift,
    mod_scale,
    mod_gate,
    text_gain,
    refine_w,
    refine_bias,
    w_qkv,
    q_gain,
    k_gain,
    w_out,
):
    job_count = lax.axis_size("job")
    shard_count = lax.axis_size("seq")
    group_size = w_qkv.shape[1]
    trows = text_cache.shape[1]
    vrows = video.shape[1]

    def to_core(x):
        return lax.ppermute(x, "job", [(i, i ^ 1) for i in range(job_count)])

    def to_chip(x):
        return lax.ppermute(x, "job", [(i, i ^ 2) for i in range(job_count)])

    def over_seq(x):
        return lax.all_to_all(x, "seq", split_axis=0, concat_axis=0, tiled=False)

    def after(x, earlier):
        return lax.optimization_barrier((x, earlier))[0]

    def to_device(x, chip, other_half, staying=None):
        perm = []
        for job in range(job_count):
            for shard in range(shard_count):
                if staying is None or (job % 2 == shard // group_size) == staying:
                    to = (job ^ chip, shard ^ (group_size if other_half else 0))
                    perm.append((job * shard_count + shard, to[0] * shard_count + to[1]))
        return lax.ppermute(x, ("job", "seq"), perm)

    def over_half(x):
        halves = [list(range(i, i + group_size)) for i in range(0, shard_count, group_size)]
        return lax.all_to_all(
            x, "seq", split_axis=0, concat_axis=0, tiled=False, axis_index_groups=halves
        )

    def core_pieces(x, count):
        return [to_core(part) for part in jnp.split(x, count)]

    tables = (mod_shift, mod_scale)
    qkv_w = jnp.transpose(w_qkv, (2, 1, 0, 3))
    own = video[0]
    normed = norm_text(text_cache, text_gain)
    other = to_device(after(own, normed), 0, True, staying=False)
    normed_chip = after(to_chip(normed), qkv_w)
    own_chip = to_device(after(own, normed_chip), 2, False, staying=True)
    normed_core = to_core(after(normed, qkv_w))

    normed_both = to_core(normed_chip)
    keep, send = refine_text(
        group_size, holder, (normed, normed_core, normed_chip, normed_both), refine_w, refine_bias
    )
    text = (
        keep,
        to_device(send, 0, True),
        to_device(keep, 2, False),
        to_device(send, 2, True),
    )

    other = after(other, keep)
    other_chip = to_device(other, 2, False, staying=True)
    own_chip = after(own_chip, keep)
    first_send = qkv_half(
        (own, own_chip), (core_pieces(own, 1), core_pieces(own_chip, 4)), (), tables, qkv_w, q_gain, k_gain
    )
    text = pack(after(text, first_send))
    first = over_half(after(first_send, text))

    other_chip = after(other_chip, first_send)
    second_send = qkv_half(
        (other, other_chip),
        (core_pieces(other, 1), core_pieces(other_chip, 2)),
        (text, to_core(text)),
        tables,
        qkv_w,
        q_gain,
        k_gain,
    )
    second = over_half(after(second_send, first))
    second = in_hbm(second)

    shapes = (2 * vrows, 2 * trows)
    remote_mixed = attend_pair(True, text_count, text_splits, first, second, *shapes)
    remote_back = over_seq(remote_mixed)
    local_mixed = attend_pair(
        False, text_count, text_splits, after(first, remote_mixed), second, *shapes
    )
    out_weight = w_out.reshape(group_size * HD, w_out.shape[2])
    rows, slots = vrows + 2 * trows, 2 * trows
    remote_back = after(remote_back, local_mixed)
    local_back = over_seq(after(local_mixed, remote_back))
    (crossing,) = project_out(remote_back, rows, 1, 0, out_weight, to_core)
    from_chip = to_chip(crossing)
    local_part, slot_rows = project_out(
        after(local_back, crossing), rows, 3, slots, out_weight, to_core
    )
    return finish(
        text_count, text_splits, video, local_part, from_chip, mod_gate, slot_rows
    )


def body(*arrays):
    video, text_cache, w_qkv = arrays[0], arrays[1], arrays[11]
    job_count = lax.axis_size("job")
    shard_count = lax.axis_size("seq")
    fits = (
        job_count == 4
        and shard_count == 2 * w_qkv.shape[1]
        and video.shape[1] == 128
        and text_cache.shape[1] == 32
    )
    return (two_wave_body if fits else general_body)(*arrays)


def solution(mesh):
    placed = (
        P("job", "seq", None),
        P("job", "seq", None),
        P(),
        P(),
        P(),
        P(),
        P(),
        P(),
        P(),
        P(None, "job"),
        P("job"),
        P(None, "job", None, None),
        P("job", None),
        P("job", None),
        P("job", None, None),
    )
    return jax.shard_map(
        body,
        mesh=mesh,
        in_specs=placed,
        out_specs=(P("job", "seq", None), P("job", "seq", None)),
        check_vma=False,
    )
```

```python
import functools
import math

import jax
import jax.numpy as jnp
from jax import lax
from jax.experimental import pallas as pl
from jax.experimental.pallas import tpu as pltpu
from jax.sharding import PartitionSpec as P

HD = 128
TXT = 256


epsilon = 1e-06


def rms_scale(values, gains):
    mean_square = jnp.mean(values * values, axis=-1, keepdims=True)
    return values * lax.rsqrt(mean_square + epsilon) * gains


def modulate(tokens, shift_part, scale_part):
    widened = tokens.astype(jnp.float32)
    centre = jnp.mean(widened, axis=-1, keepdims=True)
    spread_sq = jnp.mean((widened - centre) ** 2, axis=-1, keepdims=True)
    normed = (widened - centre) * lax.rsqrt(spread_sq + epsilon)
    return (normed * (1.0 + scale_part) + shift_part).astype(jnp.bfloat16)


def refine_rows(raw_text, text_gain, refine_w, refine_bias):
    normed = rms_scale(raw_text.astype(jnp.float32), text_gain).astype(jnp.bfloat16)
    lifted = jnp.einsum("jrt,tc->jrc", normed, refine_w, preferred_element_type=jnp.float32)
    return (lifted + refine_bias).astype(jnp.bfloat16)


def project_heads(modded, w_qkv, q_gain, k_gain):
    projections = jnp.einsum("jrd,dhce->jrhce", modded, w_qkv, preferred_element_type=jnp.float32)
    queries = rms_scale(projections[:, :, :, 0], q_gain).astype(jnp.bfloat16)
    key_rows = rms_scale(projections[:, :, :, 1], k_gain).astype(jnp.bfloat16)
    values = projections[:, :, :, 2].astype(jnp.bfloat16)
    return jnp.stack([queries, key_rows, values], axis=3)


def query_block(query_count, unit_rows):
    unit_total = query_count // unit_rows
    for factor in range(1, unit_total + 1):
        if unit_total % factor == 0 and factor * unit_rows >= 512:
            return factor * unit_rows
    return query_count


def attend(queries, key_rows, values, key_ok, block_rows):
    query_count = queries.shape[0]
    stacked_blocks = queries.reshape(query_count // block_rows, block_rows, queries.shape[1])
    scale_factor = HD ** (-0.5)

    def one_block(query_part):
        scores = (
            jnp.einsum("qe,ke->qk", query_part, key_rows, preferred_element_type=jnp.float32)
            * scale_factor
        )
        scores = jnp.where(key_ok[None, :], scores, -1e30)
        highest = jnp.max(scores, axis=-1, keepdims=True)
        weights = jnp.exp(scores - highest)
        summed = jnp.sum(weights, axis=-1, keepdims=True)
        weights = (weights / summed).astype(jnp.bfloat16)
        return jnp.dot(weights, values, preferred_element_type=jnp.float32).astype(jnp.bfloat16)

    return lax.map(one_block, stacked_blocks).reshape(query_count, queries.shape[1])


def general_body(
    video,
    text_cache,
    text_count,
    holder,
    text_splits,
    mod_shift,
    mod_scale,
    mod_gate,
    text_gain,
    refine_w,
    refine_bias,
    w_qkv,
    q_gain,
    k_gain,
    w_out,
):
    job_count = lax.axis_size("job")
    shard_count = lax.axis_size("seq")
    my_job = lax.axis_index("job")
    my_shard = lax.axis_index("seq")
    video_rows = video.shape[1]
    block_rows = text_cache.shape[1]
    slot_count = 2 * block_rows
    row_count = video_rows + slot_count
    group_size = w_qkv.shape[1]
    pair_count = job_count * group_size
    slot_total = max(pair_count, shard_count)
    repeat_count = slot_total // pair_count
    per_device = slot_total // shard_count
    offsets = jnp.cumsum(text_splits, axis=1) - text_splits
    slot_ids = jnp.arange(slot_count, dtype=jnp.int32)
    my_offsets = lax.dynamic_index_in_dim(offsets, my_shard, 1, keepdims=False)
    my_splits = lax.dynamic_index_in_dim(text_splits, my_shard, 1, keepdims=False)
    slot_valid = (slot_ids[None, :] < my_splits[:, None]) & (
        my_offsets[:, None] + slot_ids[None, :] < text_count[:, None]
    )
    position = holder[:, None] * (TXT + slot_count) + my_offsets[:, None] + slot_ids[None, :]
    cache_rows = lax.all_gather(text_cache, "job", axis=0, tiled=True)
    refined = refine_rows(cache_rows, text_gain, refine_w, refine_bias)
    gathered_text = lax.all_gather(refined, "seq", axis=1, tiled=True)
    width = gathered_text.shape[2]
    padded = jnp.concatenate(
        [
            gathered_text,
            jnp.zeros((gathered_text.shape[0], slot_count, width), gathered_text.dtype),
        ],
        axis=1,
    )
    flat_rows = padded.reshape(-1, width)
    chosen = jnp.take(flat_rows, position.reshape(-1), axis=0).reshape(job_count, slot_count, width)
    text_cols = jnp.where(slot_valid[:, :, None], chosen, jnp.zeros_like(chosen))
    text_full = lax.all_gather(text_cols, "job", axis=2, tiled=True)
    modded = modulate(
        lax.all_gather(video, "job", axis=0, tiled=True),
        mod_shift[:, None, :],
        mod_scale[:, None, :],
    )
    video_heads = project_heads(modded, w_qkv, q_gain, k_gain)
    text_modded = modulate(text_full, mod_shift[:, None, :], mod_scale[:, None, :])
    text_heads = project_heads(text_modded, w_qkv, q_gain, k_gain)
    heads_all = jnp.concatenate([video_heads, text_heads], axis=1)
    by_row = jnp.transpose(heads_all, (1, 0, 2, 3, 4)).reshape(row_count, pair_count, 3, HD)
    query_rows = by_row[:, :, 0]
    key_rows = jnp.tile(by_row[:, :, 1], (1, repeat_count, 1))
    value_rows = jnp.tile(by_row[:, :, 2], (1, repeat_count, 1))
    query_send = jnp.tile(query_rows, (1, repeat_count, 1))
    query_recv, key_recv, value_recv = (
        lax.all_to_all(query_send, "seq", split_axis=1, concat_axis=0, tiled=True),
        lax.all_to_all(key_rows, "seq", split_axis=1, concat_axis=0, tiled=True),
        lax.all_to_all(value_rows, "seq", split_axis=1, concat_axis=0, tiled=True),
    )
    my_part = my_shard * per_device // pair_count
    outputs = []
    for slot_index in range(per_device):
        slot_global = my_shard * per_device + slot_index
        job_of_slot = slot_global % pair_count // group_size
        splits_row = lax.dynamic_index_in_dim(text_splits, job_of_slot, 0, keepdims=False)
        offsets_row = lax.dynamic_index_in_dim(offsets, job_of_slot, 0, keepdims=False)
        count_of_job = lax.dynamic_index_in_dim(text_count, job_of_slot, 0, keepdims=False)
        key_valid = (slot_ids[None, :] < splits_row[:, None]) & (
            offsets_row[:, None] + slot_ids[None, :] < count_of_job
        )
        key_ok = jnp.concatenate(
            [jnp.ones((shard_count, video_rows), jnp.bool_), key_valid], axis=1
        ).reshape(-1)
        grouped = query_recv[:, slot_index].reshape(
            shard_count // repeat_count, repeat_count, row_count, HD
        )
        queries = lax.dynamic_index_in_dim(grouped, my_part, 1, keepdims=False).reshape(-1, HD)
        block_size = query_block(queries.shape[0], row_count)
        outputs.append(
            attend(queries, key_recv[:, slot_index], value_recv[:, slot_index], key_ok, block_size)
        )
    attended = jnp.stack(outputs, axis=1)
    spread_out = attended.reshape(shard_count // repeat_count, 1, row_count, per_device, HD)
    selector = (
        (jnp.arange(repeat_count) == my_part).astype(jnp.bfloat16).reshape(1, repeat_count, 1, 1, 1)
    )
    send_back = (spread_out * selector).reshape(shard_count * row_count, per_device, HD)
    returned = lax.all_to_all(send_back, "seq", split_axis=0, concat_axis=1, tiled=True)
    own_heads = lax.dynamic_index_in_dim(
        returned.reshape(row_count, repeat_count, pair_count, HD),
        my_shard % repeat_count,
        1,
        keepdims=False,
    )
    per_job = jnp.transpose(
        own_heads.reshape(row_count, job_count, group_size * HD), (1, 0, 2)
    ).reshape(job_count * row_count, group_size * HD)
    out_weight = w_out.reshape(group_size * HD, w_out.shape[2])
    projected = lax.psum_scatter(
        jnp.dot(per_job, out_weight, preferred_element_type=jnp.float32).astype(jnp.bfloat16),
        "job",
        scatter_dimension=0,
        tiled=True,
    ).astype(jnp.float32)
    own_rows = jnp.concatenate(
        [video[0], lax.dynamic_index_in_dim(text_full, my_job, 0, keepdims=False)], axis=0
    )
    gate_row = lax.dynamic_index_in_dim(mod_gate, my_job, 0, keepdims=False)
    result = (own_rows.astype(jnp.float32) + gate_row * projected).astype(jnp.bfloat16)
    own_valid = lax.dynamic_index_in_dim(slot_valid, my_job, 0, keepdims=False)
    text_result = jnp.where(
        own_valid[:, None], result[video_rows:], jnp.zeros_like(result[video_rows:])
    )
    return (result[:video_rows][None], text_result[None])


def vmem_spec():
    return pl.BlockSpec(memory_space=pltpu.VMEM)


def smem_spec():
    return pl.BlockSpec(memory_space=pltpu.SMEM)


def hbm_spec():
    return pl.BlockSpec(memory_space=pltpu.HBM)


def params(mib):
    return pltpu.CompilerParams(vmem_limit_bytes=mib << 20)


def cost(flops, moved, exps=0):
    return pl.CostEstimate(flops=int(flops), bytes_accessed=int(moved), transcendentals=int(exps))


def fetch(sources, targets, sems):
    copies = [
        pltpu.make_async_copy(source, target, sems.at[i])
        for i, (source, target) in enumerate(zip(sources, targets))
    ]
    for copy in copies:
        copy.start()
    return copies


def in_hbm(x):
    return pltpu.with_memory_space_constraint(x, pltpu.HBM)


def norm_kernel(rows_hbm, gain_hbm, out_ref, rows_ref, gain_ref, sems):
    for copy in fetch((rows_hbm.at[0], gain_hbm), (rows_ref, gain_ref), sems):
        copy.wait()
    out_ref[...] = rms_scale(rows_ref[...].astype(jnp.float32), gain_ref[...]).astype(jnp.bfloat16)


def norm_text(rows, gain):
    _, count, depth = rows.shape
    return pl.pallas_call(
        norm_kernel,
        out_shape=jax.ShapeDtypeStruct((count, depth), jnp.bfloat16),
        in_specs=[hbm_spec(), hbm_spec()],
        out_specs=vmem_spec(),
        scratch_shapes=[
            pltpu.VMEM((count, depth), jnp.bfloat16),
            pltpu.VMEM((1, depth), jnp.float32),
            pltpu.SemaphoreType.DMA((2,)),
        ],
        compiler_params=params(8),
        cost_estimate=cost(4 * rows.size, 4 * rows.size),
    )(in_hbm(rows), in_hbm(gain[None]))


def table_row(ref, index):
    return ref[pl.ds(index, 1)]


def weight_copies(w_hbm, w_ref, sems, first):
    return [
        pltpu.make_async_copy(w_hbm.at[:, h], w_ref.at[:, h], sems.at[h])
        for h in (first, first + 1)
    ]


def project_heads_into(out_hbm, out_ref, x_ref, w_hbm, w_ref, sems, qg_ref, kg_ref):
    heads, rows = w_ref.shape[1], x_ref.shape[0]
    sends = []
    for first in range(0, heads, 2):
        for copy in weight_copies(w_hbm, w_ref, sems, first):
            copy.wait()
        if first + 2 < heads:
            for copy in weight_copies(w_hbm, w_ref, sems, first + 2):
                copy.start()
        pair = (first, first + 1)
        weights = jnp.concatenate([w_ref[c, h] for h in pair for c in range(3)], axis=1)
        raw = jnp.dot(x_ref[...], weights, preferred_element_type=jnp.float32)
        for i, h in enumerate(pair):
            lo = 3 * HD * i
            queries = rms_scale(raw[:, lo : lo + HD], qg_ref[h : h + 1]).astype(jnp.bfloat16)
            keys = rms_scale(raw[:, lo + HD : lo + 2 * HD], kg_ref[h : h + 1]).astype(jnp.bfloat16)
            values = raw[:, lo + 2 * HD : lo + 3 * HD].astype(jnp.bfloat16)
            for c, part in enumerate((queries, keys, values)):
                out_ref[h, 0:rows, c * HD : (c + 1) * HD] = part
            sends.append(pltpu.make_async_copy(out_ref.at[h], out_hbm.at[h], sems.at[heads + h]))
            sends[-1].start()
    for send in sends:
        send.wait()


def my_place(group):
    mine = lax.axis_index("job")
    core, half = mine & 1, lax.axis_index("seq") // group
    return mine, core, half, (mine - core) | half


def take_rows(x_ref, lo, here_ref, core_refs, stays):
    rows = here_ref.shape[0]

    @pl.when(stays)
    def _():
        x_ref[lo : lo + rows] = here_ref[...]

    @pl.when(jnp.logical_not(stays))
    def _():
        size = rows // len(core_refs)
        for i, ref in enumerate(core_refs):
            x_ref[lo + i * size : lo + (i + 1) * size] = ref[...]


def modulate_rows(x_ref, lo, hi, shift_ref, scale_ref, job):
    x_ref[lo:hi] = modulate(x_ref[lo:hi], table_row(shift_ref, job), table_row(scale_ref, job))


def qkv_kernel(pieces, has_text, *refs):
    (a_ref, b_ref), refs = refs[:2], refs[2:]
    a_core, refs = refs[: pieces[0]], refs[pieces[0] :]
    b_core, refs = refs[: pieces[1]], refs[pieces[1] :]
    if has_text:
        (text_here_ref, text_core_ref), refs = refs[:2], refs[2:]
    table_hbm, w_hbm, out_hbm, refs = refs[:4], refs[4], refs[5], refs[6:]
    x_ref, w_ref, out_ref, table_refs, sems, refs = refs[0], refs[1], refs[2], refs[3:7], refs[7], refs[8:]
    shift_ref, scale_ref, qg_ref, kg_ref = table_refs
    rows, group = a_ref.shape[0], w_ref.shape[1]
    tables = fetch(table_hbm, table_refs, sems.at[pl.ds(2 * group, 4)])
    for copy in weight_copies(w_hbm, w_ref, sems, 0):
        copy.start()
    mine, core, half, job = my_place(group)
    take_rows(x_ref, 0, a_ref, a_core, core == half)
    take_rows(x_ref, rows, b_ref, b_core, core == half)
    for copy in tables:
        copy.wait()
    modulate_rows(x_ref, 0, rows, shift_ref, scale_ref, job)
    modulate_rows(x_ref, rows, 2 * rows, shift_ref, scale_ref, job ^ 2)
    lo = 2 * rows
    if has_text:
        text_ref = refs[0]
        _, _, trows, width = text_here_ref.shape
        blocks, row = 4, mine // 2
        for b in range(4):
            for q in range(4):
                part = text_core_ref if q & 1 else text_here_ref

                @pl.when(mine ^ b == q)
                def _():
                    for t in range(blocks):
                        job_of, shard_of, chip_of = t // 2, t % 2, q // 2
                        text_ref[t * trows : (t + 1) * trows, b * width : (b + 1) * width] = part[
                            2 * (row ^ chip_of) + (half ^ shard_of), job_of ^ chip_of
                        ]

        x_ref[lo:] = text_ref[...]
        modulate_rows(x_ref, lo, lo + 2 * trows, shift_ref, scale_ref, job)
        modulate_rows(x_ref, lo + 2 * trows, lo + 4 * trows, shift_ref, scale_ref, job ^ 2)
        for h in range(group):
            cols = pl.ds(pl.multiple_of((2 * h + core) * 3 * HD, HD), 3 * HD)
            out_ref[h, lo + 4 * trows :] = text_ref[0 : 2 * trows, cols]
    project_heads_into(out_hbm, out_ref, x_ref, w_hbm, w_ref, sems, qg_ref, kg_ref)


def qkv_half(here, from_core, text, tables, weights, q_gain, k_gain):
    group, width = weights.shape[1:3]
    pieces = tuple(map(len, from_core))
    rows_in = rows_out = 2 * here[0].shape[0]
    extra = []
    if text:
        blocks, jobs, trows, _ = text[0].shape
        rows_in += blocks * trows
        rows_out = rows_in + 2 * trows
        extra = [pltpu.VMEM((blocks * trows, width), jnp.bfloat16)]
    inputs = (*here, *from_core[0], *from_core[1], *text)
    tables = (*tables, q_gain, k_gain)
    return pl.pallas_call(
        functools.partial(qkv_kernel, pieces, bool(text)),
        out_shape=pltpu.HBM((group, rows_out, 3 * HD), jnp.bfloat16),
        in_specs=[vmem_spec()] * len(inputs) + [hbm_spec()] * 5,
        out_specs=hbm_spec(),
        scratch_shapes=[
            pltpu.VMEM((rows_in, width), jnp.bfloat16),
            pltpu.VMEM(weights.shape, jnp.bfloat16),
            pltpu.VMEM((group, rows_out, 3 * HD), jnp.bfloat16),
            *[pltpu.VMEM(table.shape, jnp.float32) for table in tables],
            pltpu.SemaphoreType.DMA((2 * group + 4,)),
            *extra,
        ],
        compiler_params=params(24),
        cost_estimate=cost(2 * rows_in * weights.size, 2 * weights.size + 4 * rows_in * width),
    )(*inputs, *map(in_hbm, tables), in_hbm(weights))


def refine_kernel(
    group, holder_ref, n0_ref, n1_ref, n2_ref, n3_ref, w_hbm, bias_hbm, out_ref, x_ref, w_ref,
    bias_ref, sems,
):
    mine, _, half, job = my_place(group)
    chunks, depth, _ = w_ref.shape
    copies = [
        pltpu.make_async_copy(w_hbm.at[pl.ds(i * depth, depth)], w_ref.at[i], sems.at[i])
        for i in range(chunks)
    ]
    (bias_copy,) = fetch([bias_hbm], [bias_ref], sems.at[pl.ds(chunks, 1)])
    copies[0].start()
    copies[1].start()
    rows = n0_ref.shape[0]
    for k, flip in enumerate((0, 2, 1, 3)):
        for r, part in enumerate((n0_ref, n1_ref, n2_ref, n3_ref)):

            @pl.when(holder_ref[job ^ flip] ^ mine == r)
            def _():
                x_ref[k * rows : (k + 1) * rows] = part[...]

    bias_copy.wait()
    lifted = bias_ref[...]
    for i in range(chunks):
        copies[i].wait()
        if i + 2 < chunks:
            copies[i + 2].start()
        part = x_ref[:, i * depth : (i + 1) * depth]
        lifted = lifted + jnp.dot(part, w_ref[i], preferred_element_type=jnp.float32)
    refined = lifted.astype(jnp.bfloat16)
    for chip in range(2):
        for k in range(2):
            out_ref[2 * chip + half, k] = refined[k * rows : (k + 1) * rows]
            out_ref[2 * chip + 1 - half, k] = refined[(2 + k) * rows : (3 + k) * rows]


def refine_text(group, holder, normed, weights, bias):
    rows, depth = normed[0].shape
    width = weights.shape[1]
    chunks = 4
    return pl.pallas_call(
        functools.partial(refine_kernel, group),
        out_shape=pltpu.HBM((4, 2, rows, width), jnp.bfloat16),
        in_specs=[smem_spec()] + [vmem_spec()] * 4 + [hbm_spec()] * 2,
        out_specs=vmem_spec(),
        scratch_shapes=[
            pltpu.VMEM((4 * rows, depth), jnp.bfloat16),
            pltpu.VMEM((chunks, depth // chunks, width), jnp.bfloat16),
            pltpu.VMEM((1, width), jnp.float32),
            pltpu.SemaphoreType.DMA((chunks + 1,)),
        ],
        compiler_params=params(14),
        cost_estimate=cost(8 * rows * depth * width, 2 * depth * width),
    )(holder, *normed, in_hbm(weights), in_hbm(bias[None]))


def choose_slots(count_ref, splits_ref, job, row, table, put):
    shards = splits_ref.shape[1]
    slot = lax.broadcasted_iota(jnp.int32, (2 * row.shape[1] // shards, row.shape[1]), 0)
    offset = jnp.int32(0)
    for s in range(shards):
        chosen = (row == slot + offset) & (slot < splits_ref[job, s]) & (row < count_ref[job])
        chosen = jnp.where(chosen, 1.0, 0.0).astype(jnp.bfloat16)
        put(s, jnp.dot(chosen, table, preferred_element_type=jnp.float32).astype(jnp.bfloat16))
        offset = offset + splits_ref[job, s]


def attention_kernel(far, count_ref, splits_ref, first_hbm, second_hbm, *refs):
    out_hbm, v_refs, t_refs, mixed_ref, out_ref, sems = refs[0], refs[1:4], refs[4:7], *refs[7:10]
    col_ref = None if far else refs[10]
    group, vrows, _ = v_refs[0].shape
    trows = t_refs[0].shape[1]
    one = vrows // 2
    copies = []

    def fetch(source, target):
        copies.append(pltpu.make_async_copy(source, target, sems.at[len(copies)]))

    for c in (1, 0, 2):
        cols = pl.ds(c * HD, HD)
        mine = pl.ds(one if far else 0, one)
        fetch(first_hbm.at[:, mine, cols], v_refs[c].at[:, pl.ds(0, one)])
        fetch(second_hbm.at[:, mine, cols], v_refs[c].at[:, pl.ds(one, one)])
        text_rows = pl.ds(vrows + (trows if far else 0), trows)
        fetch(second_hbm.at[:, text_rows, cols], t_refs[c])
    if not far:
        fetch(second_hbm.at[:, pl.ds(vrows + 2 * trows, trows)], col_ref)
    for copy in copies:
        copy.start()
    for copy in copies:
        copy.wait()
    _, _, half, job = my_place(group)
    job = job ^ 2 if far else job
    block = trows // 2
    place = lax.broadcasted_iota(jnp.int32, (1, group * trows), 1)
    row = (place // trows) * block + place % block
    row = row + (((place // block) & 1) ^ half) * (group * block)
    key_ok = row < count_ref[job]
    scale = HD ** (-0.5) * math.log2(math.e)
    ones = jnp.ones((group * vrows, HD), jnp.bfloat16)
    video_keys = v_refs[1][...].reshape(group * vrows, HD)
    text_keys = t_refs[1][...].reshape(group * trows, HD)
    video_values = jnp.concatenate([v_refs[2][...].reshape(group * vrows, HD), ones], axis=1)
    text_values = jnp.concatenate(
        [t_refs[2][...].reshape(group * trows, HD), ones[: group * trows]], axis=1
    )

    def product(a, b):
        return lax.dot_general(a, b, (((1,), (1,)), ((), ())), preferred_element_type=jnp.float32)

    def one_block(queries):
        video_scores = product(queries, video_keys)
        text_scores = jnp.where(key_ok, product(queries, text_keys), -1e30)
        highest = jnp.maximum(
            jnp.max(video_scores, axis=-1, keepdims=True),
            jnp.max(text_scores, axis=-1, keepdims=True),
        )
        video_w = jnp.exp2((video_scores - highest) * scale)
        text_w = jnp.exp2((text_scores - highest) * scale)
        mixed = jnp.dot(
            video_w.astype(jnp.bfloat16), video_values, preferred_element_type=jnp.float32
        ) + jnp.dot(text_w.astype(jnp.bfloat16), text_values, preferred_element_type=jnp.float32)
        return (mixed[:, :HD] / mixed[:, HD:]).astype(jnp.bfloat16)

    mixed_ref[...] = one_block(t_refs[0][...].reshape(group * trows, HD))
    rows = vrows // 2 + trows

    def put(s, chosen):
        out_ref[s, vrows // 2 : rows] = chosen

    choose_slots(count_ref, splits_ref, job, row, mixed_ref[...], put)
    if not far:

        def put_columns(s, chosen):
            for c in range(3):
                lo = rows + trows * c
                out_ref[s, lo : lo + trows] = chosen[:, c * HD : (c + 1) * HD]

        columns = col_ref[...].reshape(group * trows, 3 * HD)
        choose_slots(count_ref, splits_ref, job, row, columns, put_columns)
    sends = []
    for i in range(group):
        done = one_block(v_refs[0][i])
        for part in range(2):
            shard = (half ^ part) * group + i
            out_ref[shard, 0 : vrows // 2] = done[part * (vrows // 2) : (part + 1) * (vrows // 2)]
            sends.append(
                pltpu.make_async_copy(
                    out_ref.at[shard], out_hbm.at[shard], sems.at[10 + 2 * i + part]
                )
            )
            sends[-1].start()
    for send in sends:
        send.wait()


def attend_pair(far, count, splits, first, second, vrows, trows):
    group, shards = first.shape[0], splits.shape[1]
    total = group * (vrows + trows)
    rows_out = vrows // 2 + trows * (1 if far else 4)
    scratch = [pltpu.VMEM((group, vrows, HD), jnp.bfloat16)] * 3
    scratch += [pltpu.VMEM((group, trows, HD), jnp.bfloat16)] * 3
    scratch += [pltpu.VMEM((group * trows, HD), jnp.bfloat16)]
    scratch += [pltpu.VMEM((shards, rows_out, HD), jnp.bfloat16)]
    scratch += [pltpu.SemaphoreType.DMA((10 + shards,))]
    if not far:
        scratch += [pltpu.VMEM((group, trows, 3 * HD), jnp.bfloat16)]
    return pl.pallas_call(
        functools.partial(attention_kernel, far),
        out_shape=pltpu.HBM((shards, rows_out, HD), jnp.bfloat16),
        in_specs=[smem_spec(), smem_spec(), hbm_spec(), hbm_spec()],
        out_specs=hbm_spec(),
        scratch_shapes=scratch,
        compiler_params=params(12),
        cost_estimate=cost(4 * total * total * HD, 3 << 20, total * total),
    )(count, splits, first, second)


def project_rows(heads_ref, w_ref, job, count, put):
    group, width = w_ref.shape[0] // HD, w_ref.shape[1]
    rows = jnp.concatenate([heads_ref[job * group + h, 0:count] for h in range(group)], axis=1)
    for lo in range(0, width, width // 4):
        cols = slice(lo, lo + width // 4)
        put(cols, jnp.dot(rows, w_ref[:, cols], preferred_element_type=jnp.float32))


def give_kernel(pieces, heads_ref, w_ref, *refs):
    core = lax.axis_index("job") & 1
    size = refs[0].shape[0]

    def put(cols, total):
        for i, ref in enumerate(refs[:pieces]):
            ref[:, cols] = total[i * size : (i + 1) * size].astype(jnp.bfloat16)

    project_rows(heads_ref, w_ref, 1 - core, size * pieces, put)
    if len(refs) > pieces:
        slot_ref = refs[pieces]
        slots = slot_ref.shape[0]
        for h in range(w_ref.shape[0] // HD):
            for c in range(3):
                lo = size * pieces + slots * c
                slot_ref[:, (3 * h + c) * HD : (3 * h + c + 1) * HD] = heads_ref[
                    (1 - core) * (w_ref.shape[0] // HD) + h, lo : lo + slots
                ]


def keep_kernel(pieces, given, heads_ref, w_ref, *refs):
    core = lax.axis_index("job") & 1
    out_ref = refs[given]
    size = refs[0].shape[0]

    def put(cols, total):
        for i in range(pieces):
            part = total[i * size : (i + 1) * size] + refs[i][:, cols].astype(jnp.float32)
            out_ref[i * size : (i + 1) * size, cols] = part.astype(jnp.bfloat16)

    project_rows(heads_ref, w_ref, core, size * pieces, put)
    if given > pieces:
        slot_ref, other_ref = refs[given + 1], refs[pieces]
        slots, group = slot_ref.shape[0], w_ref.shape[0] // HD
        for h in range(group):
            for c in range(3):
                lo = size * pieces + slots * c
                cols = pl.ds(pl.multiple_of((3 * (2 * h + core) + c) * HD, HD), HD)
                slot_ref[:, cols] = heads_ref[core * group + h, lo : lo + slots]
                cols = pl.ds(pl.multiple_of((3 * (2 * h + 1 - core) + c) * HD, HD), HD)
                slot_ref[:, cols] = other_ref[:, (3 * h + c) * HD : (3 * h + c + 1) * HD]


def out_call(kernel, rows, weights, inputs, outs):
    depth, width = weights.shape
    return pl.pallas_call(
        kernel,
        out_shape=tuple(jax.ShapeDtypeStruct(shape, jnp.bfloat16) for shape in outs),
        in_specs=[vmem_spec()] * len(inputs),
        out_specs=(vmem_spec(),) * len(outs),
        compiler_params=params(8),
        cost_estimate=cost(2 * rows * depth * width, 2 * (depth + 2 * rows) * width),
    )(*inputs)


def project_out(heads, rows, pieces, slots, weights, to_core):
    width = weights.shape[1]
    outs = [(rows // pieces, width)] * pieces + ([(slots, width // 2)] if slots else [])
    kernel = functools.partial(give_kernel, pieces)
    given = [to_core(x) for x in out_call(kernel, rows, weights, (heads, weights), outs)]
    kernel = functools.partial(keep_kernel, pieces, len(given))
    outs = [(rows, width)] + ([(slots, width)] if slots else [])
    return out_call(kernel, rows, weights, (heads, weights, *given), outs)


def final_kernel(
    count_ref, splits_ref, video_ref, part_ref, chip_hbm, gate_ref, slot_ref, vout_hbm, tout_hbm,
    chip_ref, out_ref, in_sems, out_sems,
):
    vrows, step = video_ref.shape[1], slot_ref.shape[0]
    total_rows = part_ref.shape[0]
    reads, writes = [], []
    for i, lo in enumerate(range(0, total_rows, step)):
        rows = pl.ds(lo, step)
        reads.append(pltpu.make_async_copy(chip_hbm.at[rows], chip_ref.at[rows], in_sems.at[i]))
        target = vout_hbm.at[0, rows] if lo < vrows else tout_hbm.at[0]
        writes.append(pltpu.make_async_copy(out_ref.at[rows], target, out_sems.at[i]))
    for read in reads:
        read.start()
    job, shard = lax.axis_index("job"), lax.axis_index("seq")
    gate = table_row(gate_ref, job)
    offset = jnp.int32(0)
    for s in range(splits_ref.shape[1]):
        offset = offset + jnp.where(s < shard, splits_ref[job, s], 0)
    slot = lax.broadcasted_iota(jnp.int32, (step, 1), 0)
    valid = (slot < splits_ref[job, shard]) & (slot + offset < count_ref[job])
    for i, lo in enumerate(range(0, total_rows, step)):
        reads[i].wait()
        rows = slice(lo, lo + step)
        total = part_ref[rows].astype(jnp.float32) + chip_ref[rows].astype(jnp.float32)
        base = video_ref[0, rows] if lo < vrows else slot_ref[...]
        result = base.astype(jnp.float32) + gate * total
        if lo >= vrows:
            result = jnp.where(valid, result, 0.0)
        out_ref[rows] = result.astype(jnp.bfloat16)
        writes[i].start()
    for write in writes:
        write.wait()


def finish(count, splits, video, part, from_chip, gate, slot_rows):
    rows, width = part.shape
    steps = rows // slot_rows.shape[0]
    vrows = video.shape[1]
    return pl.pallas_call(
        final_kernel,
        out_shape=(
            jax.ShapeDtypeStruct((1, vrows, width), jnp.bfloat16),
            jax.ShapeDtypeStruct((1, rows - vrows, width), jnp.bfloat16),
        ),
        in_specs=[
            smem_spec(), smem_spec(), vmem_spec(), vmem_spec(), hbm_spec(), vmem_spec(), vmem_spec(),
        ],
        out_specs=(hbm_spec(), hbm_spec()),
        scratch_shapes=[
            pltpu.VMEM((rows, width), jnp.bfloat16),
            pltpu.VMEM((rows, width), jnp.bfloat16),
            pltpu.SemaphoreType.DMA((steps,)),
            pltpu.SemaphoreType.DMA((steps,)),
        ],
        compiler_params=params(8),
        cost_estimate=cost(6 * rows * width, 10 * rows * width),
    )(count, splits, video, part, from_chip, gate, slot_rows)


def two_wave_body(
    video,
    text_cache,
    text_count,
    holder,
    text_splits,
    mod_shift,
    mod_scale,
    mod_gate,
    text_gain,
    refine_w,
    refine_bias,
    w_qkv,
    q_gain,
    k_gain,
    w_out,
):
    job_count = lax.axis_size("job")
    shard_count = lax.axis_size("seq")
    group_size = w_qkv.shape[1]
    trows = text_cache.shape[1]
    vrows = video.shape[1]

    def to_core(x):
        return lax.ppermute(x, "job", [(i, i ^ 1) for i in range(job_count)])

    def to_chip(x):
        return lax.ppermute(x, "job", [(i, i ^ 2) for i in range(job_count)])

    def over_seq(x):
        return lax.all_to_all(x, "seq", split_axis=0, concat_axis=0, tiled=False)

    def after(x, earlier):
        return lax.optimization_barrier((x, earlier))[0]

    def to_device(x, chip, other_half, staying=None):
        perm = []
        for job in range(job_count):
            for shard in range(shard_count):
                if staying is None or (job % 2 == shard // group_size) == staying:
                    to = (job ^ chip, shard ^ (group_size if other_half else 0))
                    perm.append((job * shard_count + shard, to[0] * shard_count + to[1]))
        return lax.ppermute(x, ("job", "seq"), perm)

    def over_half(x):
        halves = [list(range(i, i + group_size)) for i in range(0, shard_count, group_size)]
        return lax.all_to_all(
            x, "seq", split_axis=0, concat_axis=0, tiled=False, axis_index_groups=halves
        )

    def core_pieces(x, count):
        return [to_core(part) for part in jnp.split(x, count)]

    tables = (mod_shift, mod_scale)
    qkv_w = jnp.transpose(w_qkv, (2, 1, 0, 3))
    own = video[0]
    normed = norm_text(text_cache, text_gain)
    other = to_device(after(own, normed), 0, True, staying=False)
    normed_chip = after(to_chip(normed), qkv_w)
    own_chip = to_device(after(own, normed_chip), 2, False, staying=True)
    normed_core = to_core(after(normed, qkv_w))

    normed_both = to_core(normed_chip)
    refined = refine_text(
        group_size, holder, (normed, normed_core, normed_chip, normed_both), refine_w, refine_bias
    )
    fours = [
        [
            (job + chip) * shard_count + shard + half
            for chip in (0, 2)
            for half in (0, group_size)
        ]
        for job in range(2)
        for shard in range(group_size)
    ]
    text = lax.all_to_all(
        refined, ("job", "seq"), split_axis=0, concat_axis=0, tiled=False, axis_index_groups=fours
    )

    other = after(other, refined)
    other_chip = to_device(other, 2, False, staying=True)
    own_chip = after(own_chip, refined)
    first_send = qkv_half(
        (own, own_chip), (core_pieces(own, 1), core_pieces(own_chip, 4)), (), tables, qkv_w, q_gain, k_gain
    )
    text = after(text, first_send)
    first = over_half(after(first_send, text))

    other_chip = after(other_chip, first_send)
    second_send = qkv_half(
        (other, other_chip),
        (core_pieces(other, 1), core_pieces(other_chip, 2)),
        (text, to_core(text)),
        tables,
        qkv_w,
        q_gain,
        k_gain,
    )
    second = over_half(after(second_send, first))
    second = in_hbm(second)

    shapes = (2 * vrows, 2 * trows)
    remote_mixed = attend_pair(True, text_count, text_splits, first, second, *shapes)
    remote_back = over_seq(remote_mixed)
    local_mixed = attend_pair(
        False, text_count, text_splits, after(first, remote_mixed), second, *shapes
    )
    out_weight = w_out.reshape(group_size * HD, w_out.shape[2])
    rows, slots = vrows + 2 * trows, 2 * trows
    remote_back = after(remote_back, local_mixed)
    local_back = over_seq(after(local_mixed, remote_back))
    (crossing,) = project_out(remote_back, rows, 1, 0, out_weight, to_core)
    from_chip = to_chip(crossing)
    local_part, slot_rows = project_out(
        after(local_back, crossing), rows, 3, slots, out_weight, to_core
    )
    return finish(
        text_count, text_splits, video, local_part, from_chip, mod_gate, slot_rows
    )


def body(*arrays):
    video, text_cache, w_qkv = arrays[0], arrays[1], arrays[11]
    job_count = lax.axis_size("job")
    shard_count = lax.axis_size("seq")
    fits = (
        job_count == 4
        and shard_count == 2 * w_qkv.shape[1]
        and video.shape[1] == 128
        and text_cache.shape[1] == 32
    )
    return (two_wave_body if fits else general_body)(*arrays)


def solution(mesh):
    placed = (
        P("job", "seq", None),
        P("job", "seq", None),
        P(),
        P(),
        P(),
        P(),
        P(),
        P(),
        P(),
        P(None, "job"),
        P("job"),
        P(None, "job", None, None),
        P("job", None),
        P("job", None),
        P("job", None, None),
    )
    return jax.shard_map(
        body,
        mesh=mesh,
        in_specs=placed,
        out_specs=(P("job", "seq", None), P("job", "seq", None)),
        check_vma=False,
    )
```

```python
import functools
import math

import jax
import jax.numpy as jnp
from jax import lax
from jax.experimental import pallas as pl
from jax.experimental.pallas import tpu as pltpu
from jax.sharding import PartitionSpec as P

HD = 128
TXT = 256


epsilon = 1e-06


def rms_scale(values, gains):
    mean_square = jnp.mean(values * values, axis=-1, keepdims=True)
    return values * lax.rsqrt(mean_square + epsilon) * gains


def modulate(tokens, shift_part, scale_part):
    widened = tokens.astype(jnp.float32)
    centre = jnp.mean(widened, axis=-1, keepdims=True)
    spread_sq = jnp.mean((widened - centre) ** 2, axis=-1, keepdims=True)
    normed = (widened - centre) * lax.rsqrt(spread_sq + epsilon)
    return (normed * (1.0 + scale_part) + shift_part).astype(jnp.bfloat16)


def refine_rows(raw_text, text_gain, refine_w, refine_bias):
    normed = rms_scale(raw_text.astype(jnp.float32), text_gain).astype(jnp.bfloat16)
    lifted = jnp.einsum("jrt,tc->jrc", normed, refine_w, preferred_element_type=jnp.float32)
    return (lifted + refine_bias).astype(jnp.bfloat16)


def project_heads(modded, w_qkv, q_gain, k_gain):
    projections = jnp.einsum("jrd,dhce->jrhce", modded, w_qkv, preferred_element_type=jnp.float32)
    queries = rms_scale(projections[:, :, :, 0], q_gain).astype(jnp.bfloat16)
    key_rows = rms_scale(projections[:, :, :, 1], k_gain).astype(jnp.bfloat16)
    values = projections[:, :, :, 2].astype(jnp.bfloat16)
    return jnp.stack([queries, key_rows, values], axis=3)


def query_block(query_count, unit_rows):
    unit_total = query_count // unit_rows
    for factor in range(1, unit_total + 1):
        if unit_total % factor == 0 and factor * unit_rows >= 512:
            return factor * unit_rows
    return query_count


def attend(queries, key_rows, values, key_ok, block_rows):
    query_count = queries.shape[0]
    stacked_blocks = queries.reshape(query_count // block_rows, block_rows, queries.shape[1])
    scale_factor = HD ** (-0.5)

    def one_block(query_part):
        scores = (
            jnp.einsum("qe,ke->qk", query_part, key_rows, preferred_element_type=jnp.float32)
            * scale_factor
        )
        scores = jnp.where(key_ok[None, :], scores, -1e30)
        highest = jnp.max(scores, axis=-1, keepdims=True)
        weights = jnp.exp(scores - highest)
        summed = jnp.sum(weights, axis=-1, keepdims=True)
        weights = (weights / summed).astype(jnp.bfloat16)
        return jnp.dot(weights, values, preferred_element_type=jnp.float32).astype(jnp.bfloat16)

    return lax.map(one_block, stacked_blocks).reshape(query_count, queries.shape[1])


def general_body(
    video,
    text_cache,
    text_count,
    holder,
    text_splits,
    mod_shift,
    mod_scale,
    mod_gate,
    text_gain,
    refine_w,
    refine_bias,
    w_qkv,
    q_gain,
    k_gain,
    w_out,
):
    job_count = lax.axis_size("job")
    shard_count = lax.axis_size("seq")
    my_job = lax.axis_index("job")
    my_shard = lax.axis_index("seq")
    video_rows = video.shape[1]
    block_rows = text_cache.shape[1]
    slot_count = 2 * block_rows
    row_count = video_rows + slot_count
    group_size = w_qkv.shape[1]
    pair_count = job_count * group_size
    slot_total = max(pair_count, shard_count)
    repeat_count = slot_total // pair_count
    per_device = slot_total // shard_count
    offsets = jnp.cumsum(text_splits, axis=1) - text_splits
    slot_ids = jnp.arange(slot_count, dtype=jnp.int32)
    my_offsets = lax.dynamic_index_in_dim(offsets, my_shard, 1, keepdims=False)
    my_splits = lax.dynamic_index_in_dim(text_splits, my_shard, 1, keepdims=False)
    slot_valid = (slot_ids[None, :] < my_splits[:, None]) & (
        my_offsets[:, None] + slot_ids[None, :] < text_count[:, None]
    )
    position = holder[:, None] * (TXT + slot_count) + my_offsets[:, None] + slot_ids[None, :]
    cache_rows = lax.all_gather(text_cache, "job", axis=0, tiled=True)
    refined = refine_rows(cache_rows, text_gain, refine_w, refine_bias)
    gathered_text = lax.all_gather(refined, "seq", axis=1, tiled=True)
    width = gathered_text.shape[2]
    padded = jnp.concatenate(
        [
            gathered_text,
            jnp.zeros((gathered_text.shape[0], slot_count, width), gathered_text.dtype),
        ],
        axis=1,
    )
    flat_rows = padded.reshape(-1, width)
    chosen = jnp.take(flat_rows, position.reshape(-1), axis=0).reshape(job_count, slot_count, width)
    text_cols = jnp.where(slot_valid[:, :, None], chosen, jnp.zeros_like(chosen))
    text_full = lax.all_gather(text_cols, "job", axis=2, tiled=True)
    modded = modulate(
        lax.all_gather(video, "job", axis=0, tiled=True),
        mod_shift[:, None, :],
        mod_scale[:, None, :],
    )
    video_heads = project_heads(modded, w_qkv, q_gain, k_gain)
    text_modded = modulate(text_full, mod_shift[:, None, :], mod_scale[:, None, :])
    text_heads = project_heads(text_modded, w_qkv, q_gain, k_gain)
    heads_all = jnp.concatenate([video_heads, text_heads], axis=1)
    by_row = jnp.transpose(heads_all, (1, 0, 2, 3, 4)).reshape(row_count, pair_count, 3, HD)
    query_rows = by_row[:, :, 0]
    key_rows = jnp.tile(by_row[:, :, 1], (1, repeat_count, 1))
    value_rows = jnp.tile(by_row[:, :, 2], (1, repeat_count, 1))
    query_send = jnp.tile(query_rows, (1, repeat_count, 1))
    query_recv, key_recv, value_recv = (
        lax.all_to_all(query_send, "seq", split_axis=1, concat_axis=0, tiled=True),
        lax.all_to_all(key_rows, "seq", split_axis=1, concat_axis=0, tiled=True),
        lax.all_to_all(value_rows, "seq", split_axis=1, concat_axis=0, tiled=True),
    )
    my_part = my_shard * per_device // pair_count
    outputs = []
    for slot_index in range(per_device):
        slot_global = my_shard * per_device + slot_index
        job_of_slot = slot_global % pair_count // group_size
        splits_row = lax.dynamic_index_in_dim(text_splits, job_of_slot, 0, keepdims=False)
        offsets_row = lax.dynamic_index_in_dim(offsets, job_of_slot, 0, keepdims=False)
        count_of_job = lax.dynamic_index_in_dim(text_count, job_of_slot, 0, keepdims=False)
        key_valid = (slot_ids[None, :] < splits_row[:, None]) & (
            offsets_row[:, None] + slot_ids[None, :] < count_of_job
        )
        key_ok = jnp.concatenate(
            [jnp.ones((shard_count, video_rows), jnp.bool_), key_valid], axis=1
        ).reshape(-1)
        grouped = query_recv[:, slot_index].reshape(
            shard_count // repeat_count, repeat_count, row_count, HD
        )
        queries = lax.dynamic_index_in_dim(grouped, my_part, 1, keepdims=False).reshape(-1, HD)
        block_size = query_block(queries.shape[0], row_count)
        outputs.append(
            attend(queries, key_recv[:, slot_index], value_recv[:, slot_index], key_ok, block_size)
        )
    attended = jnp.stack(outputs, axis=1)
    spread_out = attended.reshape(shard_count // repeat_count, 1, row_count, per_device, HD)
    selector = (
        (jnp.arange(repeat_count) == my_part).astype(jnp.bfloat16).reshape(1, repeat_count, 1, 1, 1)
    )
    send_back = (spread_out * selector).reshape(shard_count * row_count, per_device, HD)
    returned = lax.all_to_all(send_back, "seq", split_axis=0, concat_axis=1, tiled=True)
    own_heads = lax.dynamic_index_in_dim(
        returned.reshape(row_count, repeat_count, pair_count, HD),
        my_shard % repeat_count,
        1,
        keepdims=False,
    )
    per_job = jnp.transpose(
        own_heads.reshape(row_count, job_count, group_size * HD), (1, 0, 2)
    ).reshape(job_count * row_count, group_size * HD)
    out_weight = w_out.reshape(group_size * HD, w_out.shape[2])
    projected = lax.psum_scatter(
        jnp.dot(per_job, out_weight, preferred_element_type=jnp.float32).astype(jnp.bfloat16),
        "job",
        scatter_dimension=0,
        tiled=True,
    ).astype(jnp.float32)
    own_rows = jnp.concatenate(
        [video[0], lax.dynamic_index_in_dim(text_full, my_job, 0, keepdims=False)], axis=0
    )
    gate_row = lax.dynamic_index_in_dim(mod_gate, my_job, 0, keepdims=False)
    result = (own_rows.astype(jnp.float32) + gate_row * projected).astype(jnp.bfloat16)
    own_valid = lax.dynamic_index_in_dim(slot_valid, my_job, 0, keepdims=False)
    text_result = jnp.where(
        own_valid[:, None], result[video_rows:], jnp.zeros_like(result[video_rows:])
    )
    return (result[:video_rows][None], text_result[None])


def vmem_spec():
    return pl.BlockSpec(memory_space=pltpu.VMEM)


def smem_spec():
    return pl.BlockSpec(memory_space=pltpu.SMEM)


def hbm_spec():
    return pl.BlockSpec(memory_space=pltpu.HBM)


def params(mib):
    return pltpu.CompilerParams(vmem_limit_bytes=mib << 20)


def cost(flops, moved, exps=0):
    return pl.CostEstimate(flops=int(flops), bytes_accessed=int(moved), transcendentals=int(exps))


def fetch(sources, targets, sems):
    copies = [
        pltpu.make_async_copy(source, target, sems.at[i])
        for i, (source, target) in enumerate(zip(sources, targets))
    ]
    for copy in copies:
        copy.start()
    return copies


def in_hbm(x):
    return pltpu.with_memory_space_constraint(x, pltpu.HBM)


def norm_kernel(rows_hbm, gain_hbm, out_ref, rows_ref, gain_ref, sems):
    for copy in fetch((rows_hbm.at[0], gain_hbm), (rows_ref, gain_ref), sems):
        copy.wait()
    out_ref[...] = rms_scale(rows_ref[...].astype(jnp.float32), gain_ref[...]).astype(jnp.bfloat16)


def norm_text(rows, gain):
    _, count, depth = rows.shape
    return pl.pallas_call(
        norm_kernel,
        out_shape=jax.ShapeDtypeStruct((count, depth), jnp.bfloat16),
        in_specs=[hbm_spec(), hbm_spec()],
        out_specs=vmem_spec(),
        scratch_shapes=[
            pltpu.VMEM((count, depth), jnp.bfloat16),
            pltpu.VMEM((1, depth), jnp.float32),
            pltpu.SemaphoreType.DMA((2,)),
        ],
        compiler_params=params(8),
        cost_estimate=cost(4 * rows.size, 4 * rows.size),
    )(in_hbm(rows), in_hbm(gain[None]))


def table_row(ref, index):
    return ref[pl.ds(index, 1)]


def weight_copies(w_hbm, w_ref, sems, first):
    return [
        pltpu.make_async_copy(w_hbm.at[:, h], w_ref.at[:, h], sems.at[h])
        for h in (first, first + 1)
    ]


def project_heads_into(out_hbm, out_ref, x_ref, w_hbm, w_ref, sems, qg_ref, kg_ref):
    heads, rows = w_ref.shape[1], x_ref.shape[0]
    sends = []
    for first in range(0, heads, 2):
        for copy in weight_copies(w_hbm, w_ref, sems, first):
            copy.wait()
        pair = (first, first + 1)
        weights = jnp.concatenate([w_ref[c, h] for h in pair for c in range(3)], axis=1)
        raw = jnp.dot(x_ref[...], weights, preferred_element_type=jnp.float32)
        for i, h in enumerate(pair):
            lo = 3 * HD * i
            queries = rms_scale(raw[:, lo : lo + HD], qg_ref[h : h + 1]).astype(jnp.bfloat16)
            keys = rms_scale(raw[:, lo + HD : lo + 2 * HD], kg_ref[h : h + 1]).astype(jnp.bfloat16)
            values = raw[:, lo + 2 * HD : lo + 3 * HD].astype(jnp.bfloat16)
            for c, part in enumerate((queries, keys, values)):
                out_ref[h, 0:rows, c * HD : (c + 1) * HD] = part
            sends.append(pltpu.make_async_copy(out_ref.at[h], out_hbm.at[h], sems.at[heads + h]))
            sends[-1].start()
    for send in sends:
        send.wait()


def my_place(group):
    mine = lax.axis_index("job")
    core, half = mine & 1, lax.axis_index("seq") // group
    return mine, core, half, (mine - core) | half


def take_rows(x_ref, lo, here_ref, core_refs, stays):
    rows = here_ref.shape[0]

    @pl.when(stays)
    def _():
        x_ref[lo : lo + rows] = here_ref[...]

    @pl.when(jnp.logical_not(stays))
    def _():
        size = rows // len(core_refs)
        for i, ref in enumerate(core_refs):
            x_ref[lo + i * size : lo + (i + 1) * size] = ref[...]


def modulate_rows(x_ref, lo, hi, shift_ref, scale_ref, job):
    x_ref[lo:hi] = modulate(x_ref[lo:hi], table_row(shift_ref, job), table_row(scale_ref, job))


def qkv_kernel(pieces, has_text, *refs):
    (a_ref, b_ref), refs = refs[:2], refs[2:]
    a_core, refs = refs[: pieces[0]], refs[pieces[0] :]
    b_core, refs = refs[: pieces[1]], refs[pieces[1] :]
    if has_text:
        (text_here_ref, text_core_ref), refs = refs[:2], refs[2:]
    table_hbm, w_hbm, out_hbm, refs = refs[:4], refs[4], refs[5], refs[6:]
    x_ref, w_ref, out_ref, table_refs, sems, refs = refs[0], refs[1], refs[2], refs[3:7], refs[7], refs[8:]
    shift_ref, scale_ref, qg_ref, kg_ref = table_refs
    rows, group = a_ref.shape[0], w_ref.shape[1]
    tables = fetch(table_hbm, table_refs, sems.at[pl.ds(2 * group, 4)])
    for first in range(0, group, 2):
        for copy in weight_copies(w_hbm, w_ref, sems, first):
            copy.start()
    mine, core, half, job = my_place(group)
    take_rows(x_ref, 0, a_ref, a_core, core == half)
    take_rows(x_ref, rows, b_ref, b_core, core == half)
    for copy in tables:
        copy.wait()
    modulate_rows(x_ref, 0, rows, shift_ref, scale_ref, job)
    modulate_rows(x_ref, rows, 2 * rows, shift_ref, scale_ref, job ^ 2)
    lo = 2 * rows
    if has_text:
        text_ref = refs[0]
        _, _, trows, width = text_here_ref.shape
        blocks, row = 4, mine // 2
        for b in range(4):
            for q in range(4):
                part = text_core_ref if q & 1 else text_here_ref

                @pl.when(mine ^ b == q)
                def _():
                    for t in range(blocks):
                        job_of, shard_of, chip_of = t // 2, t % 2, q // 2
                        text_ref[t * trows : (t + 1) * trows, b * width : (b + 1) * width] = part[
                            2 * (row ^ chip_of) + (half ^ shard_of), job_of ^ chip_of
                        ]

        x_ref[lo:] = text_ref[...]
        modulate_rows(x_ref, lo, lo + 2 * trows, shift_ref, scale_ref, job)
        modulate_rows(x_ref, lo + 2 * trows, lo + 4 * trows, shift_ref, scale_ref, job ^ 2)
        for h in range(group):
            cols = pl.ds(pl.multiple_of((2 * h + core) * 3 * HD, HD), 3 * HD)
            out_ref[h, lo + 4 * trows :] = text_ref[0 : 2 * trows, cols]
    project_heads_into(out_hbm, out_ref, x_ref, w_hbm, w_ref, sems, qg_ref, kg_ref)


def qkv_half(here, from_core, text, tables, weights, q_gain, k_gain):
    group, width = weights.shape[1:3]
    pieces = tuple(map(len, from_core))
    rows_in = rows_out = 2 * here[0].shape[0]
    extra = []
    if text:
        blocks, jobs, trows, _ = text[0].shape
        rows_in += blocks * trows
        rows_out = rows_in + 2 * trows
        extra = [pltpu.VMEM((blocks * trows, width), jnp.bfloat16)]
    inputs = (*here, *from_core[0], *from_core[1], *text)
    tables = (*tables, q_gain, k_gain)
    return pl.pallas_call(
        functools.partial(qkv_kernel, pieces, bool(text)),
        out_shape=pltpu.HBM((group, rows_out, 3 * HD), jnp.bfloat16),
        in_specs=[vmem_spec()] * len(inputs) + [hbm_spec()] * 5,
        out_specs=hbm_spec(),
        scratch_shapes=[
            pltpu.VMEM((rows_in, width), jnp.bfloat16),
            pltpu.VMEM(weights.shape, jnp.bfloat16),
            pltpu.VMEM((group, rows_out, 3 * HD), jnp.bfloat16),
            *[pltpu.VMEM(table.shape, jnp.float32) for table in tables],
            pltpu.SemaphoreType.DMA((2 * group + 4,)),
            *extra,
        ],
        compiler_params=params(24),
        cost_estimate=cost(2 * rows_in * weights.size, 2 * weights.size + 4 * rows_in * width),
    )(*inputs, *map(in_hbm, tables), in_hbm(weights))


def refine_kernel(
    group, holder_ref, n0_ref, n1_ref, n2_ref, n3_ref, w_hbm, bias_hbm, out_ref, x_ref, w_ref,
    bias_ref, sems,
):
    mine, _, half, job = my_place(group)
    chunks, depth, _ = w_ref.shape
    copies = [
        pltpu.make_async_copy(w_hbm.at[pl.ds(i * depth, depth)], w_ref.at[i], sems.at[i])
        for i in range(chunks)
    ]
    (bias_copy,) = fetch([bias_hbm], [bias_ref], sems.at[pl.ds(chunks, 1)])
    for copy in copies[:3]:
        copy.start()
    rows = n0_ref.shape[0]
    for k, flip in enumerate((0, 2, 1, 3)):
        for r, part in enumerate((n0_ref, n1_ref, n2_ref, n3_ref)):

            @pl.when(holder_ref[job ^ flip] ^ mine == r)
            def _():
                x_ref[k * rows : (k + 1) * rows] = part[...]

    bias_copy.wait()
    lifted = bias_ref[...].reshape(1, -1)
    for i in range(chunks):
        copies[i].wait()
        if i + 3 < chunks:
            copies[i + 3].start()
        part = x_ref[:, i * depth : (i + 1) * depth]
        lifted = lifted + jnp.dot(part, w_ref[i], preferred_element_type=jnp.float32)
    refined = lifted.astype(jnp.bfloat16)
    for chip in range(2):
        for k in range(2):
            out_ref[2 * chip + half, k] = refined[k * rows : (k + 1) * rows]
            out_ref[2 * chip + 1 - half, k] = refined[(2 + k) * rows : (3 + k) * rows]


def refine_text(group, holder, normed, weights, bias):
    rows, depth = normed[0].shape
    width = weights.shape[1]
    chunks = 4
    return pl.pallas_call(
        functools.partial(refine_kernel, group),
        out_shape=jax.ShapeDtypeStruct((4, 2, rows, width), jnp.bfloat16),
        in_specs=[smem_spec()] + [vmem_spec()] * 4 + [hbm_spec()] * 2,
        out_specs=vmem_spec(),
        scratch_shapes=[
            pltpu.VMEM((4 * rows, depth), jnp.bfloat16),
            pltpu.VMEM((chunks, depth // chunks, width), jnp.bfloat16),
            pltpu.VMEM((width,), jnp.float32),
            pltpu.SemaphoreType.DMA((chunks + 1,)),
        ],
        compiler_params=params(14),
        cost_estimate=cost(8 * rows * depth * width, 2 * depth * width),
    )(holder, *normed, in_hbm(weights), in_hbm(bias))


def choose_slots(count_ref, splits_ref, job, row, table, put):
    shards = splits_ref.shape[1]
    slot = lax.broadcasted_iota(jnp.int32, (2 * row.shape[1] // shards, row.shape[1]), 0)
    offset = jnp.int32(0)
    for s in range(shards):
        chosen = (row == slot + offset) & (slot < splits_ref[job, s]) & (row < count_ref[job])
        chosen = jnp.where(chosen, 1.0, 0.0).astype(jnp.bfloat16)
        put(s, jnp.dot(chosen, table, preferred_element_type=jnp.float32).astype(jnp.bfloat16))
        offset = offset + splits_ref[job, s]


def attention_kernel(far, count_ref, splits_ref, first_hbm, second_hbm, *refs):
    out_hbm, v_refs, t_refs, mixed_ref, out_ref, sems = refs[0], refs[1:4], refs[4:7], *refs[7:10]
    col_ref = None if far else refs[10]
    group, vrows, _ = v_refs[0].shape
    trows = t_refs[0].shape[1]
    one = vrows // 2
    copies = []

    def fetch(source, target):
        copies.append(pltpu.make_async_copy(source, target, sems.at[len(copies)]))

    for c in (1, 0, 2):
        cols = pl.ds(c * HD, HD)
        mine = pl.ds(one if far else 0, one)
        fetch(first_hbm.at[:, mine, cols], v_refs[c].at[:, pl.ds(0, one)])
        fetch(second_hbm.at[:, mine, cols], v_refs[c].at[:, pl.ds(one, one)])
        text_rows = pl.ds(vrows + (trows if far else 0), trows)
        fetch(second_hbm.at[:, text_rows, cols], t_refs[c])
    if not far:
        fetch(second_hbm.at[:, pl.ds(vrows + 2 * trows, trows)], col_ref)
    for copy in copies:
        copy.start()
    for copy in copies:
        copy.wait()
    _, _, half, job = my_place(group)
    job = job ^ 2 if far else job
    block = trows // 2
    place = lax.broadcasted_iota(jnp.int32, (1, group * trows), 1)
    row = (place // trows) * block + place % block
    row = row + (((place // block) & 1) ^ half) * (group * block)
    key_ok = row < count_ref[job]
    scale = HD ** (-0.5) * math.log2(math.e)
    ones = jnp.ones((group * vrows, HD), jnp.bfloat16)
    video_keys = v_refs[1][...].reshape(group * vrows, HD)
    text_keys = t_refs[1][...].reshape(group * trows, HD)
    video_values = jnp.concatenate([v_refs[2][...].reshape(group * vrows, HD), ones], axis=1)
    text_values = jnp.concatenate(
        [t_refs[2][...].reshape(group * trows, HD), ones[: group * trows]], axis=1
    )

    def product(a, b):
        return lax.dot_general(a, b, (((1,), (1,)), ((), ())), preferred_element_type=jnp.float32)

    def one_block(queries):
        video_scores = product(queries, video_keys)
        text_scores = jnp.where(key_ok, product(queries, text_keys), -1e30)
        highest = jnp.maximum(
            jnp.max(video_scores, axis=-1, keepdims=True),
            jnp.max(text_scores, axis=-1, keepdims=True),
        )
        video_w = jnp.exp2((video_scores - highest) * scale)
        text_w = jnp.exp2((text_scores - highest) * scale)
        mixed = jnp.dot(
            video_w.astype(jnp.bfloat16), video_values, preferred_element_type=jnp.float32
        ) + jnp.dot(text_w.astype(jnp.bfloat16), text_values, preferred_element_type=jnp.float32)
        return (mixed[:, :HD] / mixed[:, HD:]).astype(jnp.bfloat16)

    mixed_ref[...] = one_block(t_refs[0][...].reshape(group * trows, HD))
    rows = vrows // 2 + trows

    def put(s, chosen):
        out_ref[s, vrows // 2 : rows] = chosen

    choose_slots(count_ref, splits_ref, job, row, mixed_ref[...], put)
    if not far:

        def put_columns(s, chosen):
            for c in range(3):
                lo = rows + trows * c
                out_ref[s, lo : lo + trows] = chosen[:, c * HD : (c + 1) * HD]

        columns = col_ref[...].reshape(group * trows, 3 * HD)
        choose_slots(count_ref, splits_ref, job, row, columns, put_columns)
    sends = []
    for i in range(group):
        done = one_block(v_refs[0][i])
        for part in range(2):
            shard = (half ^ part) * group + i
            out_ref[shard, 0 : vrows // 2] = done[part * (vrows // 2) : (part + 1) * (vrows // 2)]
            sends.append(
                pltpu.make_async_copy(
                    out_ref.at[shard], out_hbm.at[shard], sems.at[10 + 2 * i + part]
                )
            )
            sends[-1].start()
    for send in sends:
        send.wait()


def attend_pair(far, count, splits, first, second, vrows, trows):
    group, shards = first.shape[0], splits.shape[1]
    total = group * (vrows + trows)
    rows_out = vrows // 2 + trows * (1 if far else 4)
    scratch = [pltpu.VMEM((group, vrows, HD), jnp.bfloat16)] * 3
    scratch += [pltpu.VMEM((group, trows, HD), jnp.bfloat16)] * 3
    scratch += [pltpu.VMEM((group * trows, HD), jnp.bfloat16)]
    scratch += [pltpu.VMEM((shards, rows_out, HD), jnp.bfloat16)]
    scratch += [pltpu.SemaphoreType.DMA((10 + shards,))]
    if not far:
        scratch += [pltpu.VMEM((group, trows, 3 * HD), jnp.bfloat16)]
    return pl.pallas_call(
        functools.partial(attention_kernel, far),
        out_shape=pltpu.HBM((shards, rows_out, HD), jnp.bfloat16),
        in_specs=[smem_spec(), smem_spec(), hbm_spec(), hbm_spec()],
        out_specs=hbm_spec(),
        scratch_shapes=scratch,
        compiler_params=params(12),
        cost_estimate=cost(4 * total * total * HD, 3 << 20, total * total),
    )(count, splits, first, second)


def project_rows(heads_ref, w_ref, job, count, put):
    group, width = w_ref.shape[0] // HD, w_ref.shape[1]
    rows = jnp.concatenate([heads_ref[job * group + h, 0:count] for h in range(group)], axis=1)
    for lo in range(0, width, width // 4):
        cols = slice(lo, lo + width // 4)
        put(cols, jnp.dot(rows, w_ref[:, cols], preferred_element_type=jnp.float32))


def give_kernel(pieces, heads_ref, w_ref, *refs):
    core = lax.axis_index("job") & 1
    size = refs[0].shape[0]

    def put(cols, total):
        for i, ref in enumerate(refs[:pieces]):
            ref[:, cols] = total[i * size : (i + 1) * size].astype(jnp.bfloat16)

    project_rows(heads_ref, w_ref, 1 - core, size * pieces, put)
    if len(refs) > pieces:
        slot_ref = refs[pieces]
        slots = slot_ref.shape[0]
        for h in range(w_ref.shape[0] // HD):
            for c in range(3):
                lo = size * pieces + slots * c
                slot_ref[:, (3 * h + c) * HD : (3 * h + c + 1) * HD] = heads_ref[
                    (1 - core) * (w_ref.shape[0] // HD) + h, lo : lo + slots
                ]


def keep_kernel(pieces, given, heads_ref, w_ref, *refs):
    core = lax.axis_index("job") & 1
    out_ref = refs[given]
    size = refs[0].shape[0]

    def put(cols, total):
        for i in range(pieces):
            part = total[i * size : (i + 1) * size] + refs[i][:, cols].astype(jnp.float32)
            out_ref[i * size : (i + 1) * size, cols] = part.astype(jnp.bfloat16)

    project_rows(heads_ref, w_ref, core, size * pieces, put)
    if given > pieces:
        slot_ref, other_ref = refs[given + 1], refs[pieces]
        slots, group = slot_ref.shape[0], w_ref.shape[0] // HD
        for h in range(group):
            for c in range(3):
                lo = size * pieces + slots * c
                cols = pl.ds(pl.multiple_of((3 * (2 * h + core) + c) * HD, HD), HD)
                slot_ref[:, cols] = heads_ref[core * group + h, lo : lo + slots]
                cols = pl.ds(pl.multiple_of((3 * (2 * h + 1 - core) + c) * HD, HD), HD)
                slot_ref[:, cols] = other_ref[:, (3 * h + c) * HD : (3 * h + c + 1) * HD]


def out_call(kernel, rows, weights, inputs, outs):
    depth, width = weights.shape
    return pl.pallas_call(
        kernel,
        out_shape=tuple(jax.ShapeDtypeStruct(shape, jnp.bfloat16) for shape in outs),
        in_specs=[vmem_spec()] * len(inputs),
        out_specs=(vmem_spec(),) * len(outs),
        compiler_params=params(8),
        cost_estimate=cost(2 * rows * depth * width, 2 * (depth + 2 * rows) * width),
    )(*inputs)


def project_out(heads, rows, pieces, slots, weights, to_core):
    width = weights.shape[1]
    outs = [(rows // pieces, width)] * pieces + ([(slots, width // 2)] if slots else [])
    kernel = functools.partial(give_kernel, pieces)
    given = [to_core(x) for x in out_call(kernel, rows, weights, (heads, weights), outs)]
    kernel = functools.partial(keep_kernel, pieces, len(given))
    outs = [(rows, width)] + ([(slots, width)] if slots else [])
    return out_call(kernel, rows, weights, (heads, weights, *given), outs)


def final_kernel(
    count_ref, splits_ref, video_ref, part_ref, chip_hbm, gate_ref, slot_ref, vout_hbm, tout_hbm,
    chip_ref, out_ref, in_sems, out_sems,
):
    vrows, step = video_ref.shape[1], slot_ref.shape[0]
    total_rows = part_ref.shape[0]
    reads, writes = [], []
    for i, lo in enumerate(range(0, total_rows, step)):
        rows = pl.ds(lo, step)
        reads.append(pltpu.make_async_copy(chip_hbm.at[rows], chip_ref.at[rows], in_sems.at[i]))
        target = vout_hbm.at[0, rows] if lo < vrows else tout_hbm.at[0]
        writes.append(pltpu.make_async_copy(out_ref.at[rows], target, out_sems.at[i]))
    for read in reads:
        read.start()
    job, shard = lax.axis_index("job"), lax.axis_index("seq")
    gate = table_row(gate_ref, job)
    offset = jnp.int32(0)
    for s in range(splits_ref.shape[1]):
        offset = offset + jnp.where(s < shard, splits_ref[job, s], 0)
    slot = lax.broadcasted_iota(jnp.int32, (step, 1), 0)
    valid = (slot < splits_ref[job, shard]) & (slot + offset < count_ref[job])
    for i, lo in enumerate(range(0, total_rows, step)):
        reads[i].wait()
        rows = slice(lo, lo + step)
        total = part_ref[rows].astype(jnp.float32) + chip_ref[rows].astype(jnp.float32)
        base = video_ref[0, rows] if lo < vrows else slot_ref[...]
        result = base.astype(jnp.float32) + gate * total
        if lo >= vrows:
            result = jnp.where(valid, result, 0.0)
        out_ref[rows] = result.astype(jnp.bfloat16)
        writes[i].start()
    for write in writes:
        write.wait()


def finish(count, splits, video, part, from_chip, gate, slot_rows):
    rows, width = part.shape
    steps = rows // slot_rows.shape[0]
    vrows = video.shape[1]
    return pl.pallas_call(
        final_kernel,
        out_shape=(
            jax.ShapeDtypeStruct((1, vrows, width), jnp.bfloat16),
            jax.ShapeDtypeStruct((1, rows - vrows, width), jnp.bfloat16),
        ),
        in_specs=[
            smem_spec(), smem_spec(), vmem_spec(), vmem_spec(), hbm_spec(), vmem_spec(), vmem_spec(),
        ],
        out_specs=(hbm_spec(), hbm_spec()),
        scratch_shapes=[
            pltpu.VMEM((rows, width), jnp.bfloat16),
            pltpu.VMEM((rows, width), jnp.bfloat16),
            pltpu.SemaphoreType.DMA((steps,)),
            pltpu.SemaphoreType.DMA((steps,)),
        ],
        compiler_params=params(8),
        cost_estimate=cost(6 * rows * width, 10 * rows * width),
    )(count, splits, video, part, from_chip, gate, slot_rows)


def two_wave_body(
    video,
    text_cache,
    text_count,
    holder,
    text_splits,
    mod_shift,
    mod_scale,
    mod_gate,
    text_gain,
    refine_w,
    refine_bias,
    w_qkv,
    q_gain,
    k_gain,
    w_out,
):
    job_count = lax.axis_size("job")
    shard_count = lax.axis_size("seq")
    group_size = w_qkv.shape[1]
    trows = text_cache.shape[1]
    vrows = video.shape[1]

    def to_core(x):
        return lax.ppermute(x, "job", [(i, i ^ 1) for i in range(job_count)])

    def to_chip(x):
        return lax.ppermute(x, "job", [(i, i ^ 2) for i in range(job_count)])

    def over_seq(x):
        return lax.all_to_all(x, "seq", split_axis=0, concat_axis=0, tiled=False)

    def after(x, earlier):
        return lax.optimization_barrier((x, earlier))[0]

    def to_device(x, chip, other_half, staying=None):
        perm = []
        for job in range(job_count):
            for shard in range(shard_count):
                if staying is None or (job % 2 == shard // group_size) == staying:
                    to = (job ^ chip, shard ^ (group_size if other_half else 0))
                    perm.append((job * shard_count + shard, to[0] * shard_count + to[1]))
        return lax.ppermute(x, ("job", "seq"), perm)

    def over_half(x):
        halves = [list(range(i, i + group_size)) for i in range(0, shard_count, group_size)]
        return lax.all_to_all(
            x, "seq", split_axis=0, concat_axis=0, tiled=False, axis_index_groups=halves
        )

    def core_pieces(x, count):
        return [to_core(part) for part in jnp.split(x, count)]

    tables = (mod_shift, mod_scale)
    qkv_w = jnp.transpose(w_qkv, (2, 1, 0, 3))
    own = video[0]
    normed = norm_text(text_cache, text_gain)
    other = to_device(after(own, normed), 0, True, staying=False)
    normed_chip = after(to_chip(normed), qkv_w)
    own_chip = to_device(after(own, normed_chip), 2, False, staying=True)
    normed_core = to_core(after(normed, qkv_w))

    normed_both = to_core(normed_chip)
    refined = refine_text(
        group_size, holder, (normed, normed_core, normed_chip, normed_both), refine_w, refine_bias
    )
    fours = [
        [
            (job + chip) * shard_count + shard + half
            for chip in (0, 2)
            for half in (0, group_size)
        ]
        for job in range(2)
        for shard in range(group_size)
    ]
    text = lax.all_to_all(
        refined, ("job", "seq"), split_axis=0, concat_axis=0, tiled=False, axis_index_groups=fours
    )

    other = after(other, refined)
    other_chip = to_device(other, 2, False, staying=True)
    own_chip = after(own_chip, refined)
    first_send = qkv_half(
        (own, own_chip), (core_pieces(own, 1), core_pieces(own_chip, 4)), (), tables, qkv_w, q_gain, k_gain
    )
    text = after(text, first_send)
    first = over_half(after(first_send, text))

    other_chip = after(other_chip, first_send)
    second_send = qkv_half(
        (other, other_chip),
        (core_pieces(other, 1), core_pieces(other_chip, 2)),
        (text, to_core(text)),
        tables,
        qkv_w,
        q_gain,
        k_gain,
    )
    second = over_half(after(second_send, first))
    second = in_hbm(second)

    shapes = (2 * vrows, 2 * trows)
    remote_mixed = attend_pair(True, text_count, text_splits, first, second, *shapes)
    remote_back = over_seq(remote_mixed)
    local_mixed = attend_pair(
        False, text_count, text_splits, after(first, remote_mixed), second, *shapes
    )
    out_weight = w_out.reshape(group_size * HD, w_out.shape[2])
    rows, slots = vrows + 2 * trows, 2 * trows
    remote_back = after(remote_back, local_mixed)
    local_back = over_seq(after(local_mixed, remote_back))
    (crossing,) = project_out(remote_back, rows, 1, 0, out_weight, to_core)
    from_chip = to_chip(crossing)
    local_part, slot_rows = project_out(
        after(local_back, crossing), rows, 3, slots, out_weight, to_core
    )
    return finish(
        text_count, text_splits, video, local_part, from_chip, mod_gate, slot_rows
    )


def body(*arrays):
    video, text_cache, w_qkv = arrays[0], arrays[1], arrays[11]
    job_count = lax.axis_size("job")
    shard_count = lax.axis_size("seq")
    fits = (
        job_count == 4
        and shard_count == 2 * w_qkv.shape[1]
        and video.shape[1] == 128
        and text_cache.shape[1] == 32
    )
    return (two_wave_body if fits else general_body)(*arrays)


def solution(mesh):
    placed = (
        P("job", "seq", None),
        P("job", "seq", None),
        P(),
        P(),
        P(),
        P(),
        P(),
        P(),
        P(),
        P(None, "job"),
        P("job"),
        P(None, "job", None, None),
        P("job", None),
        P("job", None),
        P("job", None, None),
    )
    return jax.shard_map(
        body,
        mesh=mesh,
        in_specs=placed,
        out_specs=(P("job", "seq", None), P("job", "seq", None)),
        check_vma=False,
    )
```

```python
import functools
import math

import jax
import jax.numpy as jnp
from jax import lax
from jax.experimental import pallas as pl
from jax.experimental.pallas import tpu as pltpu
from jax.sharding import PartitionSpec as P

HD = 128
TXT = 256


epsilon = 1e-06


def rms_scale(values, gains):
    mean_square = jnp.mean(values * values, axis=-1, keepdims=True)
    return values * lax.rsqrt(mean_square + epsilon) * gains


def modulate(tokens, shift_part, scale_part):
    widened = tokens.astype(jnp.float32)
    centre = jnp.mean(widened, axis=-1, keepdims=True)
    spread_sq = jnp.mean((widened - centre) ** 2, axis=-1, keepdims=True)
    normed = (widened - centre) * lax.rsqrt(spread_sq + epsilon)
    return (normed * (1.0 + scale_part) + shift_part).astype(jnp.bfloat16)


def refine_rows(raw_text, text_gain, refine_w, refine_bias):
    normed = rms_scale(raw_text.astype(jnp.float32), text_gain).astype(jnp.bfloat16)
    lifted = jnp.einsum("jrt,tc->jrc", normed, refine_w, preferred_element_type=jnp.float32)
    return (lifted + refine_bias).astype(jnp.bfloat16)


def project_heads(modded, w_qkv, q_gain, k_gain):
    projections = jnp.einsum("jrd,dhce->jrhce", modded, w_qkv, preferred_element_type=jnp.float32)
    queries = rms_scale(projections[:, :, :, 0], q_gain).astype(jnp.bfloat16)
    key_rows = rms_scale(projections[:, :, :, 1], k_gain).astype(jnp.bfloat16)
    values = projections[:, :, :, 2].astype(jnp.bfloat16)
    return jnp.stack([queries, key_rows, values], axis=3)


def query_block(query_count, unit_rows):
    unit_total = query_count // unit_rows
    for factor in range(1, unit_total + 1):
        if unit_total % factor == 0 and factor * unit_rows >= 512:
            return factor * unit_rows
    return query_count


def attend(queries, key_rows, values, key_ok, block_rows):
    query_count = queries.shape[0]
    stacked_blocks = queries.reshape(query_count // block_rows, block_rows, queries.shape[1])
    scale_factor = HD ** (-0.5)

    def one_block(query_part):
        scores = (
            jnp.einsum("qe,ke->qk", query_part, key_rows, preferred_element_type=jnp.float32)
            * scale_factor
        )
        scores = jnp.where(key_ok[None, :], scores, -1e30)
        highest = jnp.max(scores, axis=-1, keepdims=True)
        weights = jnp.exp(scores - highest)
        summed = jnp.sum(weights, axis=-1, keepdims=True)
        weights = (weights / summed).astype(jnp.bfloat16)
        return jnp.dot(weights, values, preferred_element_type=jnp.float32).astype(jnp.bfloat16)

    return lax.map(one_block, stacked_blocks).reshape(query_count, queries.shape[1])


def general_body(
    video,
    text_cache,
    text_count,
    holder,
    text_splits,
    mod_shift,
    mod_scale,
    mod_gate,
    text_gain,
    refine_w,
    refine_bias,
    w_qkv,
    q_gain,
    k_gain,
    w_out,
):
    job_count = lax.axis_size("job")
    shard_count = lax.axis_size("seq")
    my_job = lax.axis_index("job")
    my_shard = lax.axis_index("seq")
    video_rows = video.shape[1]
    block_rows = text_cache.shape[1]
    slot_count = 2 * block_rows
    row_count = video_rows + slot_count
    group_size = w_qkv.shape[1]
    pair_count = job_count * group_size
    slot_total = max(pair_count, shard_count)
    repeat_count = slot_total // pair_count
    per_device = slot_total // shard_count
    offsets = jnp.cumsum(text_splits, axis=1) - text_splits
    slot_ids = jnp.arange(slot_count, dtype=jnp.int32)
    my_offsets = lax.dynamic_index_in_dim(offsets, my_shard, 1, keepdims=False)
    my_splits = lax.dynamic_index_in_dim(text_splits, my_shard, 1, keepdims=False)
    slot_valid = (slot_ids[None, :] < my_splits[:, None]) & (
        my_offsets[:, None] + slot_ids[None, :] < text_count[:, None]
    )
    position = holder[:, None] * (TXT + slot_count) + my_offsets[:, None] + slot_ids[None, :]
    cache_rows = lax.all_gather(text_cache, "job", axis=0, tiled=True)
    refined = refine_rows(cache_rows, text_gain, refine_w, refine_bias)
    gathered_text = lax.all_gather(refined, "seq", axis=1, tiled=True)
    width = gathered_text.shape[2]
    padded = jnp.concatenate(
        [
            gathered_text,
            jnp.zeros((gathered_text.shape[0], slot_count, width), gathered_text.dtype),
        ],
        axis=1,
    )
    flat_rows = padded.reshape(-1, width)
    chosen = jnp.take(flat_rows, position.reshape(-1), axis=0).reshape(job_count, slot_count, width)
    text_cols = jnp.where(slot_valid[:, :, None], chosen, jnp.zeros_like(chosen))
    text_full = lax.all_gather(text_cols, "job", axis=2, tiled=True)
    modded = modulate(
        lax.all_gather(video, "job", axis=0, tiled=True),
        mod_shift[:, None, :],
        mod_scale[:, None, :],
    )
    video_heads = project_heads(modded, w_qkv, q_gain, k_gain)
    text_modded = modulate(text_full, mod_shift[:, None, :], mod_scale[:, None, :])
    text_heads = project_heads(text_modded, w_qkv, q_gain, k_gain)
    heads_all = jnp.concatenate([video_heads, text_heads], axis=1)
    by_row = jnp.transpose(heads_all, (1, 0, 2, 3, 4)).reshape(row_count, pair_count, 3, HD)
    query_rows = by_row[:, :, 0]
    key_rows = jnp.tile(by_row[:, :, 1], (1, repeat_count, 1))
    value_rows = jnp.tile(by_row[:, :, 2], (1, repeat_count, 1))
    query_send = jnp.tile(query_rows, (1, repeat_count, 1))
    query_recv, key_recv, value_recv = (
        lax.all_to_all(query_send, "seq", split_axis=1, concat_axis=0, tiled=True),
        lax.all_to_all(key_rows, "seq", split_axis=1, concat_axis=0, tiled=True),
        lax.all_to_all(value_rows, "seq", split_axis=1, concat_axis=0, tiled=True),
    )
    my_part = my_shard * per_device // pair_count
    outputs = []
    for slot_index in range(per_device):
        slot_global = my_shard * per_device + slot_index
        job_of_slot = slot_global % pair_count // group_size
        splits_row = lax.dynamic_index_in_dim(text_splits, job_of_slot, 0, keepdims=False)
        offsets_row = lax.dynamic_index_in_dim(offsets, job_of_slot, 0, keepdims=False)
        count_of_job = lax.dynamic_index_in_dim(text_count, job_of_slot, 0, keepdims=False)
        key_valid = (slot_ids[None, :] < splits_row[:, None]) & (
            offsets_row[:, None] + slot_ids[None, :] < count_of_job
        )
        key_ok = jnp.concatenate(
            [jnp.ones((shard_count, video_rows), jnp.bool_), key_valid], axis=1
        ).reshape(-1)
        grouped = query_recv[:, slot_index].reshape(
            shard_count // repeat_count, repeat_count, row_count, HD
        )
        queries = lax.dynamic_index_in_dim(grouped, my_part, 1, keepdims=False).reshape(-1, HD)
        block_size = query_block(queries.shape[0], row_count)
        outputs.append(
            attend(queries, key_recv[:, slot_index], value_recv[:, slot_index], key_ok, block_size)
        )
    attended = jnp.stack(outputs, axis=1)
    spread_out = attended.reshape(shard_count // repeat_count, 1, row_count, per_device, HD)
    selector = (
        (jnp.arange(repeat_count) == my_part).astype(jnp.bfloat16).reshape(1, repeat_count, 1, 1, 1)
    )
    send_back = (spread_out * selector).reshape(shard_count * row_count, per_device, HD)
    returned = lax.all_to_all(send_back, "seq", split_axis=0, concat_axis=1, tiled=True)
    own_heads = lax.dynamic_index_in_dim(
        returned.reshape(row_count, repeat_count, pair_count, HD),
        my_shard % repeat_count,
        1,
        keepdims=False,
    )
    per_job = jnp.transpose(
        own_heads.reshape(row_count, job_count, group_size * HD), (1, 0, 2)
    ).reshape(job_count * row_count, group_size * HD)
    out_weight = w_out.reshape(group_size * HD, w_out.shape[2])
    projected = lax.psum_scatter(
        jnp.dot(per_job, out_weight, preferred_element_type=jnp.float32).astype(jnp.bfloat16),
        "job",
        scatter_dimension=0,
        tiled=True,
    ).astype(jnp.float32)
    own_rows = jnp.concatenate(
        [video[0], lax.dynamic_index_in_dim(text_full, my_job, 0, keepdims=False)], axis=0
    )
    gate_row = lax.dynamic_index_in_dim(mod_gate, my_job, 0, keepdims=False)
    result = (own_rows.astype(jnp.float32) + gate_row * projected).astype(jnp.bfloat16)
    own_valid = lax.dynamic_index_in_dim(slot_valid, my_job, 0, keepdims=False)
    text_result = jnp.where(
        own_valid[:, None], result[video_rows:], jnp.zeros_like(result[video_rows:])
    )
    return (result[:video_rows][None], text_result[None])


def vmem_spec():
    return pl.BlockSpec(memory_space=pltpu.VMEM)


def smem_spec():
    return pl.BlockSpec(memory_space=pltpu.SMEM)


def hbm_spec():
    return pl.BlockSpec(memory_space=pltpu.HBM)


def params(mib):
    return pltpu.CompilerParams(vmem_limit_bytes=mib << 20)


def cost(flops, moved, exps=0):
    return pl.CostEstimate(flops=int(flops), bytes_accessed=int(moved), transcendentals=int(exps))


def fetch(sources, targets, sems):
    copies = [
        pltpu.make_async_copy(source, target, sems.at[i])
        for i, (source, target) in enumerate(zip(sources, targets))
    ]
    for copy in copies:
        copy.start()
    return copies


def in_hbm(x):
    return pltpu.with_memory_space_constraint(x, pltpu.HBM)


def norm_kernel(rows_hbm, gain_hbm, out_ref, rows_ref, gain_ref, sems):
    for copy in fetch((rows_hbm.at[0], gain_hbm), (rows_ref, gain_ref), sems):
        copy.wait()
    out_ref[...] = rms_scale(rows_ref[...].astype(jnp.float32), gain_ref[...]).astype(jnp.bfloat16)


def norm_text(rows, gain):
    _, count, depth = rows.shape
    return pl.pallas_call(
        norm_kernel,
        out_shape=jax.ShapeDtypeStruct((count, depth), jnp.bfloat16),
        in_specs=[hbm_spec(), hbm_spec()],
        out_specs=vmem_spec(),
        scratch_shapes=[
            pltpu.VMEM((count, depth), jnp.bfloat16),
            pltpu.VMEM((1, depth), jnp.float32),
            pltpu.SemaphoreType.DMA((2,)),
        ],
        compiler_params=params(8),
        cost_estimate=cost(4 * rows.size, 4 * rows.size),
    )(in_hbm(rows), in_hbm(gain[None]))


def table_row(ref, index):
    return ref[pl.ds(index, 1)]


def weight_copies(w_hbm, w_ref, sems, first):
    return [
        pltpu.make_async_copy(w_hbm.at[:, h], w_ref.at[:, h], sems.at[h])
        for h in (first, first + 1)
    ]


def project_heads_into(out_hbm, out_ref, x_ref, w_hbm, w_ref, sems, qg_ref, kg_ref):
    heads, rows = w_ref.shape[1], x_ref.shape[0]
    sends = []
    for first in range(0, heads, 2):
        for copy in weight_copies(w_hbm, w_ref, sems, first):
            copy.wait()
        pair = (first, first + 1)
        weights = jnp.concatenate([w_ref[c, h] for h in pair for c in range(3)], axis=1)
        raw = jnp.dot(x_ref[...], weights, preferred_element_type=jnp.float32)
        for i, h in enumerate(pair):
            lo = 3 * HD * i
            queries = rms_scale(raw[:, lo : lo + HD], qg_ref[h : h + 1]).astype(jnp.bfloat16)
            keys = rms_scale(raw[:, lo + HD : lo + 2 * HD], kg_ref[h : h + 1]).astype(jnp.bfloat16)
            values = raw[:, lo + 2 * HD : lo + 3 * HD].astype(jnp.bfloat16)
            for c, part in enumerate((queries, keys, values)):
                out_ref[h, 0:rows, c * HD : (c + 1) * HD] = part
            sends.append(pltpu.make_async_copy(out_ref.at[h], out_hbm.at[h], sems.at[heads + h]))
            sends[-1].start()
    for send in sends:
        send.wait()


def my_place(group):
    mine = lax.axis_index("job")
    core, half = mine & 1, lax.axis_index("seq") // group
    return mine, core, half, (mine - core) | half


def take_rows(x_ref, lo, here_ref, core_refs, stays):
    rows = here_ref.shape[0]

    @pl.when(stays)
    def _():
        x_ref[lo : lo + rows] = here_ref[...]

    @pl.when(jnp.logical_not(stays))
    def _():
        size = rows // len(core_refs)
        for i, ref in enumerate(core_refs):
            x_ref[lo + i * size : lo + (i + 1) * size] = ref[...]


def modulate_rows(x_ref, lo, hi, shift_ref, scale_ref, job):
    x_ref[lo:hi] = modulate(x_ref[lo:hi], table_row(shift_ref, job), table_row(scale_ref, job))


def qkv_kernel(pieces, has_text, *refs):
    (a_ref, b_ref), refs = refs[:2], refs[2:]
    a_core, refs = refs[: pieces[0]], refs[pieces[0] :]
    b_core, refs = refs[: pieces[1]], refs[pieces[1] :]
    if has_text:
        (text_here_ref, text_core_ref), refs = refs[:2], refs[2:]
    table_hbm, w_hbm, out_hbm, refs = refs[:4], refs[4], refs[5], refs[6:]
    x_ref, w_ref, out_ref, table_refs, sems, refs = refs[0], refs[1], refs[2], refs[3:7], refs[7], refs[8:]
    shift_ref, scale_ref, qg_ref, kg_ref = table_refs
    rows, group = a_ref.shape[0], w_ref.shape[1]
    tables = fetch(table_hbm, table_refs, sems.at[pl.ds(2 * group, 4)])
    for first in range(0, group, 2):
        for copy in weight_copies(w_hbm, w_ref, sems, first):
            copy.start()
    mine, core, half, job = my_place(group)
    take_rows(x_ref, 0, a_ref, a_core, core == half)
    take_rows(x_ref, rows, b_ref, b_core, core == half)
    for copy in tables:
        copy.wait()
    modulate_rows(x_ref, 0, rows, shift_ref, scale_ref, job)
    modulate_rows(x_ref, rows, 2 * rows, shift_ref, scale_ref, job ^ 2)
    lo = 2 * rows
    if has_text:
        text_ref = refs[0]
        _, _, trows, width = text_here_ref.shape
        blocks, row = 4, mine // 2
        for b in range(4):
            for q in range(4):
                part = text_core_ref if q & 1 else text_here_ref

                @pl.when(mine ^ b == q)
                def _():
                    for t in range(blocks):
                        job_of, shard_of, chip_of = t // 2, t % 2, q // 2
                        text_ref[t * trows : (t + 1) * trows, b * width : (b + 1) * width] = part[
                            2 * (row ^ chip_of) + (half ^ shard_of), job_of ^ chip_of
                        ]

        x_ref[lo:] = text_ref[...]
        modulate_rows(x_ref, lo, lo + 2 * trows, shift_ref, scale_ref, job)
        modulate_rows(x_ref, lo + 2 * trows, lo + 4 * trows, shift_ref, scale_ref, job ^ 2)
        for h in range(group):
            cols = pl.ds(pl.multiple_of((2 * h + core) * 3 * HD, HD), 3 * HD)
            out_ref[h, lo + 4 * trows :] = text_ref[0 : 2 * trows, cols]
    project_heads_into(out_hbm, out_ref, x_ref, w_hbm, w_ref, sems, qg_ref, kg_ref)


def qkv_half(here, from_core, text, tables, weights, q_gain, k_gain):
    group, width = weights.shape[1:3]
    pieces = tuple(map(len, from_core))
    rows_in = rows_out = 2 * here[0].shape[0]
    extra = []
    if text:
        blocks, jobs, trows, _ = text[0].shape
        rows_in += blocks * trows
        rows_out = rows_in + 2 * trows
        extra = [pltpu.VMEM((blocks * trows, width), jnp.bfloat16)]
    inputs = (*here, *from_core[0], *from_core[1], *text)
    tables = (*tables, q_gain, k_gain)
    return pl.pallas_call(
        functools.partial(qkv_kernel, pieces, bool(text)),
        out_shape=pltpu.HBM((group, rows_out, 3 * HD), jnp.bfloat16),
        in_specs=[vmem_spec()] * len(inputs) + [hbm_spec()] * 5,
        out_specs=hbm_spec(),
        scratch_shapes=[
            pltpu.VMEM((rows_in, width), jnp.bfloat16),
            pltpu.VMEM(weights.shape, jnp.bfloat16),
            pltpu.VMEM((group, rows_out, 3 * HD), jnp.bfloat16),
            *[pltpu.VMEM(table.shape, jnp.float32) for table in tables],
            pltpu.SemaphoreType.DMA((2 * group + 4,)),
            *extra,
        ],
        compiler_params=params(24),
        cost_estimate=cost(2 * rows_in * weights.size, 2 * weights.size + 4 * rows_in * width),
    )(*inputs, *map(in_hbm, tables), in_hbm(weights))


def refine_kernel(
    group, holder_ref, n0_ref, n1_ref, n2_ref, n3_ref, w_hbm, bias_hbm, out_ref, x_ref, w_ref,
    bias_ref, sems,
):
    mine, _, half, job = my_place(group)
    chunks, depth, _ = w_ref.shape
    copies = [
        pltpu.make_async_copy(w_hbm.at[pl.ds(i * depth, depth)], w_ref.at[i], sems.at[i])
        for i in range(chunks)
    ]
    (bias_copy,) = fetch([bias_hbm], [bias_ref], sems.at[pl.ds(chunks, 1)])
    for copy in copies[:3]:
        copy.start()
    rows = n0_ref.shape[0]
    for k, flip in enumerate((0, 2, 1, 3)):
        for r, part in enumerate((n0_ref, n1_ref, n2_ref, n3_ref)):

            @pl.when(holder_ref[job ^ flip] ^ mine == r)
            def _():
                x_ref[k * rows : (k + 1) * rows] = part[...]

    bias_copy.wait()
    lifted = bias_ref[...].reshape(1, -1)
    for i in range(chunks):
        copies[i].wait()
        if i + 3 < chunks:
            copies[i + 3].start()
        part = x_ref[:, i * depth : (i + 1) * depth]
        lifted = lifted + jnp.dot(part, w_ref[i], preferred_element_type=jnp.float32)
    refined = lifted.astype(jnp.bfloat16)
    for chip in range(2):
        for k in range(2):
            out_ref[2 * chip + half, k] = refined[k * rows : (k + 1) * rows]
            out_ref[2 * chip + 1 - half, k] = refined[(2 + k) * rows : (3 + k) * rows]


def refine_text(group, holder, normed, weights, bias):
    rows, depth = normed[0].shape
    width = weights.shape[1]
    chunks = 4
    return pl.pallas_call(
        functools.partial(refine_kernel, group),
        out_shape=jax.ShapeDtypeStruct((4, 2, rows, width), jnp.bfloat16),
        in_specs=[smem_spec()] + [vmem_spec()] * 4 + [hbm_spec()] * 2,
        out_specs=vmem_spec(),
        scratch_shapes=[
            pltpu.VMEM((4 * rows, depth), jnp.bfloat16),
            pltpu.VMEM((chunks, depth // chunks, width), jnp.bfloat16),
            pltpu.VMEM((width,), jnp.float32),
            pltpu.SemaphoreType.DMA((chunks + 1,)),
        ],
        compiler_params=params(14),
        cost_estimate=cost(8 * rows * depth * width, 2 * depth * width),
    )(holder, *normed, in_hbm(weights), in_hbm(bias))


def choose_slots(count_ref, splits_ref, job, row, table, put):
    shards = splits_ref.shape[1]
    slot = lax.broadcasted_iota(jnp.int32, (2 * row.shape[1] // shards, row.shape[1]), 0)
    offset = jnp.int32(0)
    picks = []
    for s in range(shards):
        chosen = (row == slot + offset) & (slot < splits_ref[job, s]) & (row < count_ref[job])
        picks.append(jnp.where(chosen, 1.0, 0.0).astype(jnp.bfloat16))
        offset = offset + splits_ref[job, s]
    picked = jnp.dot(jnp.concatenate(picks, axis=0), table, preferred_element_type=jnp.float32)
    picked = picked.astype(jnp.bfloat16)
    for s in range(shards):
        put(s, picked[s * slot.shape[0] : (s + 1) * slot.shape[0]])


def attention_kernel(far, count_ref, splits_ref, first_hbm, second_hbm, *refs):
    out_hbm, v_refs, t_refs, mixed_ref, out_ref, sems = refs[0], refs[1:4], refs[4:7], *refs[7:10]
    col_ref = None if far else refs[10]
    group, vrows, _ = v_refs[0].shape
    trows = t_refs[0].shape[1]
    one = vrows // 2
    copies = []

    def fetch(source, target):
        copies.append(pltpu.make_async_copy(source, target, sems.at[len(copies)]))

    for c in (1, 0, 2):
        cols = pl.ds(c * HD, HD)
        mine = pl.ds(one if far else 0, one)
        fetch(first_hbm.at[:, mine, cols], v_refs[c].at[:, pl.ds(0, one)])
        fetch(second_hbm.at[:, mine, cols], v_refs[c].at[:, pl.ds(one, one)])
        text_rows = pl.ds(vrows + (trows if far else 0), trows)
        fetch(second_hbm.at[:, text_rows, cols], t_refs[c])
    if not far:
        fetch(second_hbm.at[:, pl.ds(vrows + 2 * trows, trows)], col_ref)
    for copy in copies:
        copy.start()
    for copy in copies:
        copy.wait()
    _, _, half, job = my_place(group)
    job = job ^ 2 if far else job
    block = trows // 2
    place = lax.broadcasted_iota(jnp.int32, (1, group * trows), 1)
    row = (place // trows) * block + place % block
    row = row + (((place // block) & 1) ^ half) * (group * block)
    key_ok = row < count_ref[job]
    scale = HD ** (-0.5) * math.log2(math.e)
    ones = jnp.ones((group * vrows, HD), jnp.bfloat16)
    video_keys = v_refs[1][...].reshape(group * vrows, HD)
    text_keys = t_refs[1][...].reshape(group * trows, HD)
    video_values = jnp.concatenate([v_refs[2][...].reshape(group * vrows, HD), ones], axis=1)
    text_values = jnp.concatenate(
        [t_refs[2][...].reshape(group * trows, HD), ones[: group * trows]], axis=1
    )

    def product(a, b):
        return lax.dot_general(a, b, (((1,), (1,)), ((), ())), preferred_element_type=jnp.float32)

    def one_block(queries):
        video_scores = product(queries, video_keys)
        text_scores = jnp.where(key_ok, product(queries, text_keys), -1e30)
        highest = jnp.maximum(
            jnp.max(video_scores, axis=-1, keepdims=True),
            jnp.max(text_scores, axis=-1, keepdims=True),
        )
        video_w = jnp.exp2((video_scores - highest) * scale)
        text_w = jnp.exp2((text_scores - highest) * scale)
        mixed = jnp.dot(
            video_w.astype(jnp.bfloat16), video_values, preferred_element_type=jnp.float32
        ) + jnp.dot(text_w.astype(jnp.bfloat16), text_values, preferred_element_type=jnp.float32)
        return (mixed[:, :HD] / mixed[:, HD:]).astype(jnp.bfloat16)

    mixed_ref[...] = one_block(t_refs[0][...].reshape(group * trows, HD))
    rows = vrows // 2 + trows

    def put(s, chosen):
        out_ref[s, vrows // 2 : rows] = chosen

    choose_slots(count_ref, splits_ref, job, row, mixed_ref[...], put)
    if not far:

        def put_columns(s, chosen):
            for c in range(3):
                lo = rows + trows * c
                out_ref[s, lo : lo + trows] = chosen[:, c * HD : (c + 1) * HD]

        columns = col_ref[...].reshape(group * trows, 3 * HD)
        choose_slots(count_ref, splits_ref, job, row, columns, put_columns)
    sends = []
    for i in range(group):
        done = one_block(v_refs[0][i])
        for part in range(2):
            shard = (half ^ part) * group + i
            out_ref[shard, 0 : vrows // 2] = done[part * (vrows // 2) : (part + 1) * (vrows // 2)]
            sends.append(
                pltpu.make_async_copy(
                    out_ref.at[shard], out_hbm.at[shard], sems.at[10 + 2 * i + part]
                )
            )
            sends[-1].start()
    for send in sends:
        send.wait()


def attend_pair(far, count, splits, first, second, vrows, trows):
    group, shards = first.shape[0], splits.shape[1]
    total = group * (vrows + trows)
    rows_out = vrows // 2 + trows * (1 if far else 4)
    scratch = [pltpu.VMEM((group, vrows, HD), jnp.bfloat16)] * 3
    scratch += [pltpu.VMEM((group, trows, HD), jnp.bfloat16)] * 3
    scratch += [pltpu.VMEM((group * trows, HD), jnp.bfloat16)]
    scratch += [pltpu.VMEM((shards, rows_out, HD), jnp.bfloat16)]
    scratch += [pltpu.SemaphoreType.DMA((10 + shards,))]
    if not far:
        scratch += [pltpu.VMEM((group, trows, 3 * HD), jnp.bfloat16)]
    return pl.pallas_call(
        functools.partial(attention_kernel, far),
        out_shape=pltpu.HBM((shards, rows_out, HD), jnp.bfloat16),
        in_specs=[smem_spec(), smem_spec(), hbm_spec(), hbm_spec()],
        out_specs=hbm_spec(),
        scratch_shapes=scratch,
        compiler_params=params(12),
        cost_estimate=cost(4 * total * total * HD, 3 << 20, total * total),
    )(count, splits, first, second)


def project_rows(heads_ref, w_ref, job, count, put):
    group, width = w_ref.shape[0] // HD, w_ref.shape[1]
    rows = jnp.concatenate([heads_ref[job * group + h, 0:count] for h in range(group)], axis=1)
    for lo in range(0, width, width // 4):
        cols = slice(lo, lo + width // 4)
        put(cols, jnp.dot(rows, w_ref[:, cols], preferred_element_type=jnp.float32))


def give_kernel(pieces, heads_ref, w_ref, *refs):
    core = lax.axis_index("job") & 1
    size = refs[0].shape[0]

    def put(cols, total):
        for i, ref in enumerate(refs[:pieces]):
            ref[:, cols] = total[i * size : (i + 1) * size].astype(jnp.bfloat16)

    project_rows(heads_ref, w_ref, 1 - core, size * pieces, put)
    if len(refs) > pieces:
        slot_ref = refs[pieces]
        slots = slot_ref.shape[0]
        for h in range(w_ref.shape[0] // HD):
            for c in range(3):
                lo = size * pieces + slots * c
                slot_ref[:, (3 * h + c) * HD : (3 * h + c + 1) * HD] = heads_ref[
                    (1 - core) * (w_ref.shape[0] // HD) + h, lo : lo + slots
                ]


def keep_kernel(pieces, given, heads_ref, w_ref, *refs):
    core = lax.axis_index("job") & 1
    out_ref = refs[given]
    size = refs[0].shape[0]

    def put(cols, total):
        for i in range(pieces):
            part = total[i * size : (i + 1) * size] + refs[i][:, cols].astype(jnp.float32)
            out_ref[i * size : (i + 1) * size, cols] = part.astype(jnp.bfloat16)

    project_rows(heads_ref, w_ref, core, size * pieces, put)
    if given > pieces:
        slot_ref, other_ref = refs[given + 1], refs[pieces]
        slots, group = slot_ref.shape[0], w_ref.shape[0] // HD
        for h in range(group):
            for c in range(3):
                lo = size * pieces + slots * c
                cols = pl.ds(pl.multiple_of((3 * (2 * h + core) + c) * HD, HD), HD)
                slot_ref[:, cols] = heads_ref[core * group + h, lo : lo + slots]
                cols = pl.ds(pl.multiple_of((3 * (2 * h + 1 - core) + c) * HD, HD), HD)
                slot_ref[:, cols] = other_ref[:, (3 * h + c) * HD : (3 * h + c + 1) * HD]


def out_call(kernel, rows, weights, inputs, outs):
    depth, width = weights.shape
    return pl.pallas_call(
        kernel,
        out_shape=tuple(jax.ShapeDtypeStruct(shape, jnp.bfloat16) for shape in outs),
        in_specs=[vmem_spec()] * len(inputs),
        out_specs=(vmem_spec(),) * len(outs),
        compiler_params=params(8),
        cost_estimate=cost(2 * rows * depth * width, 2 * (depth + 2 * rows) * width),
    )(*inputs)


def project_out(heads, rows, pieces, slots, weights, to_core):
    width = weights.shape[1]
    outs = [(rows // pieces, width)] * pieces + ([(slots, width // 2)] if slots else [])
    kernel = functools.partial(give_kernel, pieces)
    given = [to_core(x) for x in out_call(kernel, rows, weights, (heads, weights), outs)]
    kernel = functools.partial(keep_kernel, pieces, len(given))
    outs = [(rows, width)] + ([(slots, width)] if slots else [])
    return out_call(kernel, rows, weights, (heads, weights, *given), outs)


def final_kernel(
    count_ref, splits_ref, video_ref, part_ref, chip_hbm, gate_ref, slot_ref, vout_hbm, tout_hbm,
    chip_ref, out_ref, in_sems, out_sems,
):
    vrows, step = video_ref.shape[1], slot_ref.shape[0]
    total_rows = part_ref.shape[0]
    reads, writes = [], []
    for i, lo in enumerate(range(0, total_rows, step)):
        rows = pl.ds(lo, step)
        reads.append(pltpu.make_async_copy(chip_hbm.at[rows], chip_ref.at[rows], in_sems.at[i]))
        target = vout_hbm.at[0, rows] if lo < vrows else tout_hbm.at[0]
        writes.append(pltpu.make_async_copy(out_ref.at[rows], target, out_sems.at[i]))
    for read in reads:
        read.start()
    job, shard = lax.axis_index("job"), lax.axis_index("seq")
    gate = table_row(gate_ref, job)
    offset = jnp.int32(0)
    for s in range(splits_ref.shape[1]):
        offset = offset + jnp.where(s < shard, splits_ref[job, s], 0)
    slot = lax.broadcasted_iota(jnp.int32, (step, 1), 0)
    valid = (slot < splits_ref[job, shard]) & (slot + offset < count_ref[job])
    for i, lo in enumerate(range(0, total_rows, step)):
        reads[i].wait()
        rows = slice(lo, lo + step)
        total = part_ref[rows].astype(jnp.float32) + chip_ref[rows].astype(jnp.float32)
        base = video_ref[0, rows] if lo < vrows else slot_ref[...]
        result = base.astype(jnp.float32) + gate * total
        if lo >= vrows:
            result = jnp.where(valid, result, 0.0)
        out_ref[rows] = result.astype(jnp.bfloat16)
        writes[i].start()
    for write in writes:
        write.wait()


def finish(count, splits, video, part, from_chip, gate, slot_rows):
    rows, width = part.shape
    steps = rows // slot_rows.shape[0]
    vrows = video.shape[1]
    return pl.pallas_call(
        final_kernel,
        out_shape=(
            jax.ShapeDtypeStruct((1, vrows, width), jnp.bfloat16),
            jax.ShapeDtypeStruct((1, rows - vrows, width), jnp.bfloat16),
        ),
        in_specs=[
            smem_spec(), smem_spec(), vmem_spec(), vmem_spec(), hbm_spec(), vmem_spec(), vmem_spec(),
        ],
        out_specs=(hbm_spec(), hbm_spec()),
        scratch_shapes=[
            pltpu.VMEM((rows, width), jnp.bfloat16),
            pltpu.VMEM((rows, width), jnp.bfloat16),
            pltpu.SemaphoreType.DMA((steps,)),
            pltpu.SemaphoreType.DMA((steps,)),
        ],
        compiler_params=params(8),
        cost_estimate=cost(6 * rows * width, 10 * rows * width),
    )(count, splits, video, part, from_chip, gate, slot_rows)


def two_wave_body(
    video,
    text_cache,
    text_count,
    holder,
    text_splits,
    mod_shift,
    mod_scale,
    mod_gate,
    text_gain,
    refine_w,
    refine_bias,
    w_qkv,
    q_gain,
    k_gain,
    w_out,
):
    job_count = lax.axis_size("job")
    shard_count = lax.axis_size("seq")
    group_size = w_qkv.shape[1]
    trows = text_cache.shape[1]
    vrows = video.shape[1]

    def to_core(x):
        return lax.ppermute(x, "job", [(i, i ^ 1) for i in range(job_count)])

    def to_chip(x):
        return lax.ppermute(x, "job", [(i, i ^ 2) for i in range(job_count)])

    def over_seq(x):
        return lax.all_to_all(x, "seq", split_axis=0, concat_axis=0, tiled=False)

    def after(x, earlier):
        return lax.optimization_barrier((x, earlier))[0]

    def to_device(x, chip, other_half, staying=None):
        perm = []
        for job in range(job_count):
            for shard in range(shard_count):
                if staying is None or (job % 2 == shard // group_size) == staying:
                    to = (job ^ chip, shard ^ (group_size if other_half else 0))
                    perm.append((job * shard_count + shard, to[0] * shard_count + to[1]))
        return lax.ppermute(x, ("job", "seq"), perm)

    def over_half(x):
        halves = [list(range(i, i + group_size)) for i in range(0, shard_count, group_size)]
        return lax.all_to_all(
            x, "seq", split_axis=0, concat_axis=0, tiled=False, axis_index_groups=halves
        )

    def core_pieces(x, count):
        return [to_core(part) for part in jnp.split(x, count)]

    tables = (mod_shift, mod_scale)
    qkv_w = jnp.transpose(w_qkv, (2, 1, 0, 3))
    own = video[0]
    normed = norm_text(text_cache, text_gain)
    other = to_device(after(own, normed), 0, True, staying=False)
    normed_chip = after(to_chip(normed), qkv_w)
    own_chip = to_device(after(own, normed_chip), 2, False, staying=True)
    normed_core = to_core(after(normed, qkv_w))

    normed_both = to_core(normed_chip)
    refined = refine_text(
        group_size, holder, (normed, normed_core, normed_chip, normed_both), refine_w, refine_bias
    )
    fours = [
        [
            (job + chip) * shard_count + shard + half
            for chip in (0, 2)
            for half in (0, group_size)
        ]
        for job in range(2)
        for shard in range(group_size)
    ]
    text = lax.all_to_all(
        refined, ("job", "seq"), split_axis=0, concat_axis=0, tiled=False, axis_index_groups=fours
    )

    other = after(other, refined)
    other_chip = to_device(other, 2, False, staying=True)
    own_chip = after(own_chip, refined)
    first_send = qkv_half(
        (own, own_chip), (core_pieces(own, 1), core_pieces(own_chip, 4)), (), tables, qkv_w, q_gain, k_gain
    )
    text = after(text, first_send)
    first = over_half(after(first_send, text))

    other_chip = after(other_chip, first_send)
    second_send = qkv_half(
        (other, other_chip),
        (core_pieces(other, 1), core_pieces(other_chip, 2)),
        (text, to_core(text)),
        tables,
        qkv_w,
        q_gain,
        k_gain,
    )
    second = over_half(after(second_send, first))
    second = in_hbm(second)

    shapes = (2 * vrows, 2 * trows)
    remote_mixed = attend_pair(True, text_count, text_splits, first, second, *shapes)
    remote_back = over_seq(remote_mixed)
    local_mixed = attend_pair(
        False, text_count, text_splits, after(first, remote_mixed), second, *shapes
    )
    out_weight = w_out.reshape(group_size * HD, w_out.shape[2])
    rows, slots = vrows + 2 * trows, 2 * trows
    remote_back = after(remote_back, local_mixed)
    local_back = over_seq(after(local_mixed, remote_back))
    (crossing,) = project_out(remote_back, rows, 1, 0, out_weight, to_core)
    from_chip = to_chip(crossing)
    local_part, slot_rows = project_out(
        after(local_back, crossing), rows, 3, slots, out_weight, to_core
    )
    return finish(
        text_count, text_splits, video, local_part, from_chip, mod_gate, slot_rows
    )


def body(*arrays):
    video, text_cache, w_qkv = arrays[0], arrays[1], arrays[11]
    job_count = lax.axis_size("job")
    shard_count = lax.axis_size("seq")
    fits = (
        job_count == 4
        and shard_count == 2 * w_qkv.shape[1]
        and video.shape[1] == 128
        and text_cache.shape[1] == 32
    )
    return (two_wave_body if fits else general_body)(*arrays)


def solution(mesh):
    placed = (
        P("job", "seq", None),
        P("job", "seq", None),
        P(),
        P(),
        P(),
        P(),
        P(),
        P(),
        P(),
        P(None, "job"),
        P("job"),
        P(None, "job", None, None),
        P("job", None),
        P("job", None),
        P("job", None, None),
    )
    return jax.shard_map(
        body,
        mesh=mesh,
        in_specs=placed,
        out_specs=(P("job", "seq", None), P("job", "seq", None)),
        check_vma=False,
    )
```
